32 devices in a mesh: batch: 4 (over z), seq: 8 (over y, x, core).
Axes of the slice: x: 2, y: 2, z: 4, core: 2. Of those that a mesh axis runs over, the one named last changes fastest.
Arguments:
- mel_inputs: bfloat16 [8, 1536, 200], P('batch', 'seq'), may hold values from -6 to 6
- text_ids: int32 [8, 1536], P('batch', 'seq'), may hold values from 0 to 2545
- segment_ids: int32 [8, 1536], P('batch'), may hold values from 0 to 3, as said below
- key_mask: int32 [8, 1536], P('batch'), may hold values from 0 to 1, as said below
- time_index: int32 [8, 4], P('batch'), may hold values from 0 to 31
- input_proj: bfloat16 [712, 1024], P(None, ('batch', 'seq')), may hold values from -0.21875 to 0.21875
- conv_first: bfloat16 [31, 1024, 64], P(None, ('batch', 'seq')), may hold values from -0.125 to 0.125
- conv_second: bfloat16 [31, 1024, 64], P(None, ('batch', 'seq')), may hold values from -0.125 to 0.125
- time_table: bfloat16 [32, 1024], P(None, ('batch', 'seq')), may hold values from -6 to 6
- adaln_proj: bfloat16 [1024, 6144], P(None, ('batch', 'seq')), may hold values from -0.1875 to 0.1875
- qkv_proj: bfloat16 [1024, 3072], P(None, ('batch', 'seq')), may hold values from -0.1875 to 0.1875
- out_proj: bfloat16 [1024, 1024], P(None, ('batch', 'seq')), may hold values from -2.5 to 2.5
- up_proj: bfloat16 [1024, 2048], P(None, ('batch', 'seq')), may hold values from -0.1875 to 0.1875
- down_proj: bfloat16 [2048, 1024], P(None, ('batch', 'seq')), may hold values from -0.125 to 0.125
- text_table: bfloat16 [2546, 512], P(None, ('batch', 'seq')), may hold values from -6 to 6
- grad_out: bfloat16 [8, 1536, 1024], P('batch', 'seq'), may hold values from -6 to 6
Outputs:
- block_out: bfloat16 [8, 1536, 1024], P('batch', 'seq')
- grad_mels: float32 [8, 1536, 200], P('batch', 'seq')
- grad_input_proj: float32 [712, 1024], P(None, ('batch', 'seq'))
- grad_conv_first: float32 [31, 1024, 64], P(None, ('batch', 'seq'))
- grad_conv_second: float32 [31, 1024, 64], P(None, ('batch', 'seq'))
- grad_time_table: float32 [32, 1024], P(None, ('batch', 'seq'))
- grad_adaln_proj: float32 [1024, 6144], P(None, ('batch', 'seq'))
- grad_qkv_proj: float32 [1024, 3072], P(None, ('batch', 'seq'))
- grad_out_proj: float32 [1024, 1024], P(None, ('batch', 'seq'))
- grad_up_proj: float32 [1024, 2048], P(None, ('batch', 'seq'))
- grad_down_proj: float32 [2048, 1024], P(None, ('batch', 'seq'))
- grad_text_table: float32 [2546, 512], P(None, ('batch', 'seq'))
The draws below stay inside these ranges and needn't reach their ends.
Inputs may be any that keep to these rules, and one draw needn't show every extreme that they name: `segment_ids`: in each row utterance numbers start at 0 and rise by one at each boundary; a row holds 1 to 4 utterances, each of 192 frames or more; of the 2 rows of each index of batch, one is a single utterance. `key_mask`: each row is 1 except for its last 48 to 191 frames.
All inputs are finite; a program needn't handle non-finite values.
Results may differ from the reference program's by a relative error of at most 0.023.
Values may be sent and summed in bfloat16 or wider, within the bound.
A program may use at most 448 MiB of HBM per device.

```python
import math
import jax
import jax.numpy as jnp
import numpy as np
from jax import lax

D = 1024
HEADS = 16
HEAD = 64
FF = 2048
MEL = 100
TEXT = 512
VOCAB = 2546
KERNEL = 31
GROUPS = 16
STEPS = 32
SEGS = 4
ROWS_DEV = 2
FRAMES_DEV = 192
ROWS = 8
ROW_LEN = 1536


def draw_segment_ids(key, part):
    key = jax.random.fold_in(key, 11)
    pick_key, count_key, jitter_key, most_key = jax.random.split(key, 4)
    group_total = ROWS // ROWS_DEV
    single_row = jax.random.randint(pick_key, (group_total,), 0, ROWS_DEV)
    fullest = jax.random.randint(most_key, (), 0, group_total)
    row_index = jnp.arange(ROWS, dtype=jnp.int32)
    group_of = row_index // ROWS_DEV
    is_single = row_index % ROWS_DEV == single_row[group_of]
    counts = jax.random.randint(count_key, (ROWS,), 2, SEGS + 1)
    counts = jnp.where(group_of == fullest, SEGS, counts)
    counts = jnp.where(is_single, 1, counts)
    spacing = ROW_LEN // counts
    cut_index = jnp.arange(1, SEGS, dtype=jnp.int32)
    jitter = jax.random.randint(jitter_key, (ROWS, SEGS - 1), 0, 1 << 20) % (spacing[:, None] // 2 + 1) - spacing[:, None] // 4
    cuts = cut_index[None, :] * spacing[:, None] + jitter
    cuts = jnp.where(cut_index[None, :] < counts[:, None], cuts, ROW_LEN)
    positions = jnp.arange(ROW_LEN, dtype=jnp.int32)
    return jnp.sum((positions[None, :, None] >= cuts[:, None, :]).astype(jnp.int32), axis=2)


def draw_key_mask(key, part):
    key = jax.random.fold_in(key, 23)
    tail_len = jax.random.randint(key, (ROWS,), FRAMES_DEV // 4, FRAMES_DEV)
    positions = jnp.arange(ROW_LEN, dtype=jnp.int32)
    return (positions[None, :] < ROW_LEN - tail_len[:, None]).astype(jnp.int32)


def place_ends(drawn, own_key, low, high):
    dims = drawn.shape
    place = [jax.random.randint(jax.random.fold_in(own_key, axis), (), 0, dims[axis]) for axis in range(len(dims))]
    drawn = drawn.at[tuple(place)].set(low)
    longest = dims.index(max(dims))
    place[longest] = (place[longest] + 1) % dims[longest]
    return drawn.at[tuple(place)].set(high)


def level_of(rng, extent, pieces, low, largest):
    factor_of = 1.0
    for position, shards_of in pieces:
        draws = jax.random.uniform(jax.random.fold_in(jax.random.fold_in(rng, 6), position), (shards_of,), jnp.float32, low / len(pieces), largest / len(pieces))
        factor_of = factor_of * jnp.repeat(jnp.exp(draws), extent[position] // shards_of).reshape((-1,) + (1,) * (len(extent) - 1 - position))
    return factor_of


def rank_bounds(number_of, skew):
    portions = [(1 << 20) // math.isqrt(grade ** skew) + 1 for grade in range(1, number_of + 1)]
    width = 1 + sum(portions) // (1 << 30)
    return np.cumsum(np.array([max(1, weight // width) for weight in portions]))


def ranked(rng, extent, amount, slope):
    table = rank_bounds(amount, slope)
    pick = jax.random.randint(jax.random.fold_in(rng, 1), extent, 0, int(table[amount - 1]))
    grade = jnp.searchsorted(jnp.asarray(table, jnp.int32), pick, side="right")
    return jax.random.permutation(jax.random.fold_in(rng, 2), amount)[grade].astype(jnp.int32)


def centred(rng, shape, width, limit, pieces=(), held_as=jnp.bfloat16):
    values = width * jax.random.normal(rng, shape, jnp.float32)
    if pieces:
        values = values * level_of(rng, shape, pieces, -0.22, 0.18)
    return jnp.clip(values, -limit, limit).astype(held_as)


def setup_inputs(seed: int = 0) -> dict:
    key_of = jax.random.split(jax.random.key(seed), 17)
    return {
        "mel_inputs": centred(key_of[0], (ROWS, ROW_LEN, 2 * MEL), 1.0, 6.0, ((0, 4), (1, 8))),
        "text_ids": place_ends(ranked(key_of[1], (ROWS, ROW_LEN), VOCAB, 2), jax.random.fold_in(key_of[1], 3), 0, VOCAB - 1).astype(jnp.int32),
        "segment_ids": draw_segment_ids(jax.random.fold_in(key_of[16], 71), 0),
        "key_mask": draw_key_mask(jax.random.fold_in(key_of[16], 71), 0),
        "time_index": place_ends(jax.random.randint(key_of[4], (ROWS, SEGS), 0, STEPS), jax.random.fold_in(key_of[4], 1), 0, STEPS - 1).astype(jnp.int32),
        "input_proj": centred(key_of[5], (2 * MEL + TEXT, D), (2 * MEL + TEXT) ** -0.5, 0.21875, ((1, 32),)),
        "conv_first": centred(key_of[6], (KERNEL, D, D // GROUPS), (KERNEL * (D // GROUPS)) ** -0.5, 0.125, ((1, 32),)),
        "conv_second": centred(key_of[7], (KERNEL, D, D // GROUPS), (KERNEL * (D // GROUPS)) ** -0.5, 0.125, ((1, 32),)),
        "time_table": centred(key_of[8], (STEPS, D), 1.0, 6.0, ((1, 32),)),
        "adaln_proj": centred(key_of[9], (D, 6 * D), D ** -0.5, 0.1875, ((1, 32),)),
        "qkv_proj": centred(key_of[10], (D, 3 * D), D ** -0.5, 0.1875, ((1, 32),)),
        "out_proj": centred(key_of[11], (D, D), (max(1, 8 * D // ROW_LEN)) ** -0.5, 2.5, ((1, 32),)),
        "up_proj": centred(key_of[12], (D, FF), D ** -0.5, 0.1875, ((1, 32),)),
        "down_proj": centred(key_of[13], (FF, D), FF ** -0.5, 0.125, ((1, 32),)),
        "text_table": centred(key_of[14], (VOCAB, TEXT), 1.0, 6.0, ((1, 32),)),
        "grad_out": centred(key_of[15], (ROWS, ROW_LEN, D), 1.0, 6.0, ((0, 4), (1, 8))),
    }


EPSILON = 1e-06
MASKED = -1e+30
EXACT = lax.Precision.HIGHEST

@jax.custom_vjp
def low(v):
    return lax.optimization_barrier(v.astype(jnp.bfloat16)).astype(jnp.float32)

@jax.custom_vjp
def low_back(v):
    return v

def low_keep(v):
    return (low(v), None)

def low_pass(kept, grad):
    return (grad,)

def back_keep(v):
    return (v, None)

def back_low(kept, grad):
    return (low(grad),)
low.defvjp(low_keep, low_pass)
low_back.defvjp(back_keep, back_low)

def matmul(left_side, right_side):
    return jnp.dot(left_side, right_side, precision=EXACT, preferred_element_type=jnp.float32)

def layer_norm(field):
    centre = field - lax.optimization_barrier(jnp.mean(field, axis=-1, keepdims=True))
    return centre * lax.rsqrt(lax.optimization_barrier(jnp.mean(centre * centre, axis=-1, keepdims=True)) + EPSILON)

def modulate(field, scaling, shifting):
    return layer_norm(field) * (1.0 + scaling) + shifting

def mish_curve(inputs):
    return inputs * jnp.tanh(jax.nn.softplus(inputs))

def gelu_curve(inputs):
    return jax.nn.gelu(inputs, approximate=True)

def rotary_tables(positions):
    inverse_freq = 10000.0 ** (-jnp.arange(0, HEAD, 2).astype(jnp.float32) / HEAD)
    angles = positions[..., None] * inverse_freq
    return (jnp.cos(angles), jnp.sin(angles))

def rotate(field, cos_tab, sin_tab):
    paired = field.reshape(field.shape[:-1] + (HEAD // 2, 2))
    even_part = paired[..., 0]
    odd_part = paired[..., 1]
    cos_heads = cos_tab[..., None, :]
    sin_heads = sin_tab[..., None, :]
    turned = jnp.stack([even_part * cos_heads - odd_part * sin_heads, even_part * sin_heads + odd_part * cos_heads], axis=-1)
    return turned.reshape(field.shape)

def neighbour_masks(seg_row):
    half_width = KERNEL // 2
    length = seg_row.shape[0]
    border = jnp.full((half_width,), -1, jnp.int32)
    padded = jnp.concatenate([border, seg_row, border])
    return jnp.stack([(padded[kernel_tap:kernel_tap + length] == seg_row).astype(jnp.float32) for kernel_tap in range(KERNEL)])

def group_conv(field, kernel, near_masks):
    length = field.shape[0]
    channel = kernel.shape[2]
    half_width = KERNEL // 2
    padded = jnp.pad(field, ((half_width, half_width), (0, 0)))
    grouped = kernel.reshape(KERNEL, GROUPS, channel, channel)
    summed = jnp.zeros((length, GROUPS, channel), jnp.float32)
    for kernel_tap in range(KERNEL):
        block_in = (padded[kernel_tap:kernel_tap + length] * near_masks[kernel_tap][:, None]).reshape(length, GROUPS, channel)
        summed = summed + jnp.einsum('lgi,gio->lgo', block_in, grouped[kernel_tap], precision=EXACT)
    return summed.reshape(length, GROUPS * channel)

def attention(queries, key_rows, value_rows, seg_row, keep_row):
    length = seg_row.shape[0]
    block_len = math.gcd(length, 512)

    def one_block(inputs):
        query_block, seg_block = inputs
        scores = low_back(jnp.einsum('qhd,khd->hqk', query_block, key_rows, precision=EXACT) * 0.125)
        allowed = (seg_block[:, None] == seg_row[None, :]) & (keep_row[None, :] > 0)
        scores = jnp.where(allowed[None], scores, MASKED)
        row_peak = lax.optimization_barrier(jnp.max(scores, axis=-1, keepdims=True))
        weights = jnp.exp(scores - row_peak)
        attn_probs = weights / lax.optimization_barrier(jnp.sum(weights, axis=-1, keepdims=True))
        return jnp.einsum('hqk,khd->qhd', low(attn_probs), value_rows, precision=EXACT)
    blocks = lax.map(jax.checkpoint(one_block), (queries.reshape(length // block_len, block_len, HEADS, HEAD), seg_row.reshape(length // block_len, block_len)))
    return blocks.reshape(length, HEADS * HEAD)

def row_forward(params, mel_row, ids_row, seg_row, keep_row, index_row):
    input_proj, conv_first, conv_second, time_table, adaln_proj, qkv_proj, out_proj, up_proj, down_proj, text_table = params
    length = seg_row.shape[0]
    text_embed = low_back(jnp.take(text_table, ids_row, axis=0))
    joined = jnp.concatenate([mel_row, text_embed], axis=1)
    hidden = low_back(matmul(joined, input_proj))
    near_masks = neighbour_masks(seg_row)
    conv_one = low_back(group_conv(low(hidden), conv_first, near_masks))
    act_one = low(mish_curve(conv_one))
    conv_two = low_back(group_conv(act_one, conv_second, near_masks))
    embedded = hidden + mish_curve(conv_two)
    seg_index = jnp.arange(SEGS, dtype=jnp.int32)
    select = (seg_row[:, None] == seg_index[None, :]).astype(jnp.float32)
    soft_cond = low(jax.nn.silu(jnp.take(time_table, index_row, axis=0)))
    modulation = low_back(matmul(soft_cond, adaln_proj))
    per_frame = matmul(select, modulation)
    shift_attn, scale_attn, gate_attn, shift_feed, scale_feed, gate_feed = jnp.split(per_frame, 6, axis=1)
    normed = low(modulate(embedded, scale_attn, shift_attn))
    projected = low_back(matmul(normed, qkv_proj))
    query_raw, key_raw, value_raw = jnp.split(projected, 3, axis=1)
    starts = lax.optimization_barrier(jnp.sum((seg_row[None, :] < seg_index[:, None]).astype(jnp.int32), axis=1))
    own_start = lax.optimization_barrier(jnp.sum(jnp.where(seg_row[:, None] == seg_index[None, :], starts[None, :], 0), axis=1))
    positions = (jnp.arange(length, dtype=jnp.int32) - own_start).astype(jnp.float32)
    cos_tab, sin_tab = rotary_tables(positions)
    head_shape = (length, HEADS, HEAD)
    turned_query = low(rotate(query_raw.reshape(head_shape), cos_tab, sin_tab))
    turned_key = low(rotate(key_raw.reshape(head_shape), cos_tab, sin_tab))
    value_heads = low(value_raw.reshape(head_shape))
    attended = low_back(attention(turned_query, turned_key, value_heads, seg_row, keep_row))
    branch = low_back(matmul(low(attended), out_proj))
    middle = embedded + gate_attn * branch
    normed_feed = low(modulate(middle, scale_feed, shift_feed))
    up_value = low_back(matmul(normed_feed, up_proj))
    feed_out = low_back(matmul(low(gelu_curve(up_value)), down_proj))
    return middle + gate_feed * feed_out

def reference(mel_inputs, text_ids, segment_ids, key_mask, time_index, input_proj, conv_first, conv_second, time_table, adaln_proj, qkv_proj, out_proj, up_proj, down_proj, text_table, grad_out):
    weights = tuple((weight_item.astype(jnp.float32) for weight_item in (input_proj, conv_first, conv_second, time_table, adaln_proj, qkv_proj, out_proj, up_proj, down_proj, text_table)))

    def one_row(totals, row_data):
        mel_row, ids_row, seg_row, keep_row, index_row, cotangent = row_data

        def forward_fn(params, mel_value):
            return row_forward(params, mel_value, ids_row, seg_row, keep_row, index_row)
        result, pullback = jax.vjp(forward_fn, weights, mel_row.astype(jnp.float32))
        grad_params, grad_mel = pullback(cotangent.astype(jnp.float32))
        totals = tuple((earlier + fresh for earlier, fresh in zip(totals, grad_params)))
        return (totals, (result.astype(jnp.bfloat16), grad_mel))
    zero_grads = tuple((jnp.zeros_like(weight_item) for weight_item in weights))
    totals, (block_out, grad_mels) = lax.scan(one_row, zero_grads, (mel_inputs, text_ids, segment_ids, key_mask, time_index, grad_out))
    return (block_out, grad_mels, totals[0], totals[1], totals[2], totals[3], totals[4], totals[5], totals[6], totals[7], totals[8], totals[9])
```

```python
import functools

import jax
import jax.numpy as jnp
import numpy as np
from jax import lax
from jax.experimental import pallas as pl
from jax.experimental.pallas import tpu as pltpu
from jax.sharding import PartitionSpec as P

D = 1024
HEADS = 16
HEAD = 64
MEL = 100
VOCAB = 2546
KERNEL = 31
HALF = KERNEL // 2
CHAN = 64
STEPS = 32
SEGS = 4
GAP = 16
FOLD = 4
TAPS = KERNEL + FOLD - 1

EPSILON = 1e-06
MASKED = -1e30
EXACT = lax.Precision.HIGHEST
MESH = pl.DeviceIdType.MESH
ANY = pl.BlockSpec(memory_space=pl.ANY)
VMEM_LIMIT = 56 * 1024 * 1024
F32 = jnp.float32
BF16 = jnp.bfloat16


def dims():
    return lax.axis_size("batch"), lax.axis_size("seq")


def params(cid=None):
    if cid is None:
        return pltpu.CompilerParams(vmem_limit_bytes=VMEM_LIMIT)
    return pltpu.CompilerParams(
        collective_id=cid, has_side_effects=True, vmem_limit_bytes=VMEM_LIMIT
    )


def greet_all(nb, n, b, s):
    sem = pltpu.get_barrier_semaphore()
    me = b * n + s
    for d in range(1, nb * n):
        other = lax.rem(me + d, nb * n)
        pl.semaphore_signal(
            sem,
            inc=1,
            device_id={"batch": other // n, "seq": lax.rem(other, n)},
            device_id_type=MESH,
        )
    pl.semaphore_wait(sem, nb * n - 1)


def greet_group(n, s):
    sem = pltpu.get_barrier_semaphore()
    for d in range(1, n):
        pl.semaphore_signal(
            sem, inc=1, device_id={"seq": lax.rem(s + d, n)}, device_id_type=MESH
        )
    pl.semaphore_wait(sem, n - 1)


def remote(src, dst, send, recv, **where):
    return pltpu.make_async_remote_copy(
        src_ref=src,
        dst_ref=dst,
        send_sem=send,
        recv_sem=recv,
        device_id=where,
        device_id_type=MESH,
    )


def swap_kernel(count, n, parts, *refs):
    ins, outs = refs[:count], refs[count : 2 * count]
    send, recv, local = refs[2 * count :]
    s = lax.axis_index("seq")
    greet_group(n, s)
    copies = []
    for a in range(count):
        src, dst = parts(ins[a], outs[a], s)
        own = pltpu.make_async_copy(src(s), dst, local.at[a])
        own.start()
        copies.append(own)
    for d in range(1, n):
        t = lax.rem(s + d, n)
        for a in range(count):
            src, dst = parts(ins[a], outs[a], s)
            copy = remote(src(t), dst, send.at[a, d], recv.at[a, d], seq=t)
            copy.start()
            copies.append(copy)
    for copy in copies:
        copy.wait()


def swap_call(arrays, shapes, parts, cid):
    n = dims()[1]
    count = len(arrays)
    return pl.pallas_call(
        functools.partial(swap_kernel, count, n, parts),
        out_shape=[jax.ShapeDtypeStruct(shape, a.dtype) for shape, a in zip(shapes, arrays)],
        in_specs=[ANY] * count,
        out_specs=[ANY] * count,
        scratch_shapes=[
            pltpu.SemaphoreType.DMA((count, n)),
            pltpu.SemaphoreType.DMA((count, n)),
            pltpu.SemaphoreType.DMA((count,)),
        ],
        compiler_params=params(cid),
    )(*arrays)


def blocks_part(x, o, s):
    return (lambda t: x.at[t]), o.at[s]


def to_channels(arrays, cid):
    n = dims()[1]
    rows, frames = arrays[0].shape[:2]
    width = arrays[0].shape[2] // n
    if width % 128 == 0:

        def parts(x, o, s):
            first = pl.multiple_of(s * frames, 16)
            return (
                lambda t: x.at[:, :, pl.ds(pl.multiple_of(t * width, 128), width)]
            ), o.at[:, pl.ds(first, frames), :]

        return swap_call(arrays, [(rows, n * frames, width)] * len(arrays), parts, cid)
    split = [a.reshape(rows, frames, n, width).transpose(2, 0, 1, 3) for a in arrays]
    got = swap_call(split, [a.shape for a in split], blocks_part, cid)
    return [g.transpose(1, 0, 2, 3).reshape(rows, n * frames, width) for g in got]


def to_frames(arrays, cid):
    n = dims()[1]
    rows, length, width = arrays[0].shape
    frames = length // n
    if width % 128 == 0:

        def parts(x, o, s):
            first = pl.multiple_of(s * width, 128)
            return (
                lambda t: x.at[:, pl.ds(pl.multiple_of(t * frames, 16), frames), :]
            ), o.at[:, :, pl.ds(first, width)]

        return swap_call(arrays, [(rows, frames, n * width)] * len(arrays), parts, cid)
    split = [a.reshape(rows, n, frames, width).transpose(1, 0, 2, 3) for a in arrays]
    got = swap_call(split, [a.shape for a in split], blocks_part, cid)
    return [g.transpose(1, 2, 0, 3).reshape(rows, frames, n * width) for g in got]


def group_gather_kernel(n, x, o, send, recv, local):
    s = lax.axis_index("seq")
    core = lax.rem(s, 2)
    sibling = s + 1 - 2 * core
    chips = n // 2
    greet_group(n, s)
    own = pltpu.make_async_copy(x, o.at[:, s], local)
    own.start()
    far, near = [], []
    for d in range(1, chips):
        copy = remote(x, o.at[:, s], send.at[d], recv.at[d], seq=lax.rem(s + 2 * d, n))
        copy.start()
        far.append(copy)
    copy = remote(x, o.at[:, s], send.at[0], recv.at[0], seq=sibling)
    copy.start()
    near.append(copy)
    for d in range(1, chips):
        far[d - 1].wait_recv()
        source = lax.rem(s - 2 * d + n, n)
        copy = remote(
            o.at[:, source],
            o.at[:, source],
            send.at[chips + d],
            recv.at[chips + d],
            seq=sibling,
        )
        copy.start()
        near.append(copy)
    own.wait()
    for copy in far:
        copy.wait_send()
    for copy in near:
        copy.wait()


def group_gather(x, cid):
    n = dims()[1]
    return pl.pallas_call(
        functools.partial(group_gather_kernel, n),
        out_shape=jax.ShapeDtypeStruct((x.shape[0], n) + x.shape[1:], x.dtype),
        in_specs=[ANY],
        out_specs=ANY,
        scratch_shapes=[
            pltpu.SemaphoreType.DMA((n,)),
            pltpu.SemaphoreType.DMA((n,)),
            pltpu.SemaphoreType.DMA,
        ],
        compiler_params=params(cid),
    )(x)


def group_sum_kernel(n, x, o, mine, first, passed, second, total, send, recv, local, out_sem):
    s = lax.axis_index("seq")
    core = lax.rem(s, 2)
    sibling = s + 1 - 2 * core
    chips = n // 2
    chip = s // 2
    greet_group(n, s)
    order = [lax.rem(chip + d, chips) for d in list(range(1, chips)) + [0]]
    pair, own = [], []
    for k, c in enumerate(order):
        copy = remote(
            x.at[:, 2 * c + 1 - core], first.at[k], send.at[k], recv.at[k], seq=sibling
        )
        copy.start()
        pair.append(copy)
        copy = pltpu.make_async_copy(x.at[:, 2 * c + core], mine.at[k], local.at[k])
        copy.start()
        own.append(copy)
    rows, frames = x.shape[0], x.shape[2]
    step = 16
    far = []
    for k in range(chips):
        pair[k].wait_recv()
        own[k].wait()
        if k < chips - 1:

            def add(i, carry, k=k):
                at = pl.ds(pl.multiple_of(i * step, step), step)
                for r in range(rows):
                    passed[k, r, at, :] = (
                        mine[k, r, at, :].astype(F32) + first[k, r, at, :].astype(F32)
                    ).astype(BF16)
                return carry

            lax.fori_loop(0, frames // step, add, 0)
            copy = remote(
                passed.at[k],
                second.at[k],
                send.at[chips + k],
                recv.at[chips + k],
                seq=2 * order[k] + core,
            )
            copy.start()
            far.append(copy)
    for copy in far:
        copy.wait_recv()

    def finish(i, carry):
        at = pl.ds(pl.multiple_of(i * step, step), step)
        for r in range(rows):
            value = mine[chips - 1, r, at, :].astype(F32) + first[chips - 1, r, at, :].astype(F32)
            for k in range(chips - 1):
                value = value + second[k, r, at, :].astype(F32)
            total[r, at, :] = value
        return carry

    lax.fori_loop(0, frames // step, finish, 0)
    out = pltpu.make_async_copy(total, o, out_sem)
    out.start()
    for copy in pair + far:
        copy.wait_send()
    out.wait()


def group_sum(x, cid):
    n = dims()[1]
    rows, _, frames, width = x.shape
    chips = n // 2
    slots = pltpu.VMEM((chips, rows, frames, width), BF16)
    fewer = pltpu.VMEM((chips - 1, rows, frames, width), BF16)
    return pl.pallas_call(
        functools.partial(group_sum_kernel, n),
        out_shape=jax.ShapeDtypeStruct((rows, frames, width), F32),
        in_specs=[ANY],
        out_specs=ANY,
        scratch_shapes=[
            slots,
            slots,
            fewer,
            fewer,
            pltpu.VMEM((rows, frames, width), F32),
            pltpu.SemaphoreType.DMA((n,)),
            pltpu.SemaphoreType.DMA((n,)),
            pltpu.SemaphoreType.DMA((chips,)),
            pltpu.SemaphoreType.DMA,
        ],
        compiler_params=params(cid),
    )(x)


def start_kernel(nb, n, wide, *refs):
    count = wide + 3
    ins, outs = refs[:count], refs[count : 2 * count]
    z_send, z_recv, p_send, p_recv, c_send, c_recv, local, g_send, g_recv = refs[2 * count :]
    b, s = lax.axis_index("batch"), lax.axis_index("seq")
    core = lax.rem(s, 2)
    sibling = s + 1 - 2 * core
    chips = n // 2
    ndev = nb * n
    me = b * n + s
    greet_all(nb, n, b, s)
    copies = []
    z_copies = {}
    for a in range(wide):
        copy = pltpu.make_async_copy(ins[a], outs[a].at[b, s], local.at[a])
        copy.start()
        copies.append(copy)
    for d in range(1, nb):
        for a in range(wide):
            copy = remote(
                ins[a],
                outs[a].at[b, s],
                z_send.at[a, d],
                z_recv.at[a, d],
                batch=lax.rem(b + d, nb),
                seq=s,
            )
            copy.start()
            z_copies[a, d] = copy
    far = []
    near = []

    def spread(a, d):
        plane = lax.rem(b - d + nb, nb)
        source = ins[a] if d == 0 else outs[a].at[plane, s]
        for c in range(1, chips):
            copy = remote(
                source,
                outs[a].at[plane, s],
                p_send.at[a, d, c],
                p_recv.at[a, d, c],
                seq=lax.rem(s + 2 * c, n),
            )
            copy.start()
            far.append((a, d, c, plane, copy))
        copy = remote(
            source,
            outs[a].at[plane, s],
            c_send.at[a, d, 0],
            c_recv.at[a, d, 0],
            seq=sibling,
        )
        copy.start()
        near.append(copy)

    for a in range(wide):
        spread(a, 0)

    pieces = []
    for a in range(2):
        pieces.append((ins[wide + a], outs[wide + a], me // nb, lax.rem(me, nb), a))
    for j in range(3):
        granule = 3 * me + j
        part = granule // ndev
        column = lax.rem(granule, ndev)
        pieces.append(
            (
                ins[wide + 2].at[j],
                outs[wide + 2].at[part],
                column // nb,
                lax.rem(column, nb),
                2 + j,
            )
        )
    slots = [g_recv.at[0], g_recv.at[1], g_recv.at[2], g_recv.at[3], g_recv.at[4]]
    sends = []
    for source, target, owner, slot, k in pieces:
        if k < 2:
            arrived = g_recv.at[k, slot]
        else:
            arrived = g_recv.at[2 + (3 * me + k - 2) // ndev, slot]
        for d in range(nb):
            plane = lax.rem(b + d, nb)
            if d == 0:

                @pl.when(owner == s)
                def _(source=source, target=target, slot=slot, arrived=arrived):
                    pltpu.make_async_copy(source, target.at[slot], arrived).start()

                @pl.when(owner != s)
                def _(source=source, target=target, slot=slot, arrived=arrived, k=k, owner=owner, plane=plane):
                    remote(
                        source,
                        target.at[slot],
                        g_send.at[k, 0],
                        arrived,
                        batch=plane,
                        seq=owner,
                    ).start()
            else:
                copy = remote(
                    source, target.at[slot], g_send.at[k, d], arrived, batch=plane, seq=owner
                )
                copy.start()
                sends.append(copy)

    for d in range(1, nb):
        for a in range(wide):
            z_copies[a, d].wait_recv()
            spread(a, d)
    for a, d, c, plane, copy in far:
        copy.wait_recv()
        source = lax.rem(s - 2 * c + n, n)
        onward = remote(
            outs[a].at[plane, source],
            outs[a].at[plane, source],
            c_send.at[a, d, c],
            c_recv.at[a, d, c],
            seq=sibling,
        )
        onward.start()
        near.append(onward)
    for copy in copies:
        copy.wait()
    for copy in z_copies.values():
        copy.wait_send()
    for entry in far:
        entry[4].wait_send()
    for copy in near:
        copy.wait()
    for copy in sends:
        copy.wait_send()
    for source, target, owner, slot, k in pieces:

        @pl.when(owner != s)
        def _(source=source, target=target, slot=slot, k=k, owner=owner):
            remote(
                source, target.at[slot], g_send.at[k, 0], g_recv.at[k, slot], batch=b, seq=owner
            ).wait_send()

    for a in range(2):
        for j in range(nb):
            pltpu.make_async_copy(ins[wide + a], outs[wide + a].at[j], g_recv.at[a, j]).wait()
    for p in range(3):
        for j in range(nb):
            pltpu.make_async_copy(
                ins[wide + 2].at[0], outs[wide + 2].at[p, j], g_recv.at[2 + p, j]
            ).wait()


def start_gather(wide_arrays, conv_first, conv_second, qkv_rows, cid):
    nb, n = dims()
    chips = n // 2
    wide = len(wide_arrays)
    arrays = list(wide_arrays) + [conv_first, conv_second, qkv_rows]
    shapes = [(nb, n) + a.shape for a in wide_arrays]
    shapes += [(nb,) + conv_first.shape, (nb,) + conv_second.shape]
    shapes += [(3, nb) + qkv_rows.shape[1:]]
    dma = pltpu.SemaphoreType.DMA
    return pl.pallas_call(
        functools.partial(start_kernel, nb, n, wide),
        out_shape=[jax.ShapeDtypeStruct(sh, a.dtype) for sh, a in zip(shapes, arrays)],
        in_specs=[ANY] * len(arrays),
        out_specs=[ANY] * len(arrays),
        scratch_shapes=[
            dma((wide, nb)),
            dma((wide, nb)),
            dma((wide, nb, chips)),
            dma((wide, nb, chips)),
            dma((wide, nb, chips)),
            dma((wide, nb, chips)),
            dma((wide,)),
            dma((5, nb)),
            dma((5, nb)),
        ],
        compiler_params=params(cid),
    )(*arrays)


def spray_kernel(nb, n, by_batch, x, o, send, recv, local):
    b, s = lax.axis_index("batch"), lax.axis_index("seq")
    me = b * n + s
    ndev = nb * n
    greet_all(nb, n, b, s)
    own = pltpu.make_async_copy(x.at[b if by_batch else me], o.at[me], local)
    own.start()
    copies = []
    for d in range(1, ndev):
        other = lax.rem(me + d, ndev)
        plane, place = other // n, lax.rem(other, n)
        copy = remote(
            x.at[plane if by_batch else other],
            o.at[me],
            send.at[d],
            recv.at[d],
            batch=plane,
            seq=place,
        )
        copy.start()
        copies.append(copy)
    own.wait()
    for copy in copies:
        copy.wait()


def spray(x, by_batch, cid):
    nb, n = dims()
    ndev = nb * n
    return pl.pallas_call(
        functools.partial(spray_kernel, nb, n, by_batch),
        out_shape=jax.ShapeDtypeStruct((ndev,) + x.shape[1:], x.dtype),
        in_specs=[ANY],
        out_specs=ANY,
        scratch_shapes=[
            pltpu.SemaphoreType.DMA((ndev,)),
            pltpu.SemaphoreType.DMA((ndev,)),
            pltpu.SemaphoreType.DMA,
        ],
        compiler_params=params(cid),
    )(x)


def columns_kernel(nb, n, count, kinds, *refs):
    ins, outs = refs[:count], refs[count : 2 * count]
    send, recv = refs[2 * count :]
    b, s = lax.axis_index("batch"), lax.axis_index("seq")
    ndev = nb * n
    me = b * n + s
    greet_all(nb, n, b, s)
    base = 0
    pieces = []
    for a in range(count):
        for p in range(kinds[a]):
            for j in range(nb):
                column = p * ndev + s * nb + j
                owner = column // kinds[a]
                part = lax.rem(column, kinds[a])
                pieces.append(
                    (
                        ins[a].at[p, j],
                        outs[a].at[b, part],
                        owner,
                        send.at[base + p, j],
                        recv.at[b, base + part],
                    )
                )
        base += kinds[a]
    for source, target, owner, sent, arrived in pieces:

        @pl.when(owner == me)
        def _(source=source, target=target, arrived=arrived):
            pltpu.make_async_copy(source, target, arrived).start()

        @pl.when(owner != me)
        def _(source=source, target=target, owner=owner, sent=sent, arrived=arrived):
            remote(
                source, target, sent, arrived, batch=owner // n, seq=lax.rem(owner, n)
            ).start()

    for source, target, owner, sent, arrived in pieces:

        @pl.when(owner != me)
        def _(source=source, target=target, owner=owner, sent=sent, arrived=arrived):
            remote(
                source, target, sent, arrived, batch=owner // n, seq=lax.rem(owner, n)
            ).wait_send()

    base = 0
    for a in range(count):
        for p in range(kinds[a]):
            for j in range(nb):
                pltpu.make_async_copy(
                    ins[a].at[0, 0], outs[a].at[j, p], recv.at[j, base + p]
                ).wait()
        base += kinds[a]


def column_grads(arrays, cid):
    nb, n = dims()
    kinds = tuple(a.shape[0] for a in arrays)
    total = sum(kinds)
    return pl.pallas_call(
        functools.partial(columns_kernel, nb, n, len(arrays), kinds),
        out_shape=[
            jax.ShapeDtypeStruct((nb, a.shape[0]) + a.shape[2:], a.dtype) for a in arrays
        ],
        in_specs=[ANY] * len(arrays),
        out_specs=[ANY] * len(arrays),
        scratch_shapes=[
            pltpu.SemaphoreType.DMA((total, nb)),
            pltpu.SemaphoreType.DMA((nb, total)),
        ],
        compiler_params=params(cid),
    )(*arrays)


def scatter_kernel(nb, n, count, *refs):
    ins, outs = refs[:count], refs[count : 2 * count]
    scratch = refs[2 * count : 2 * count + 5 * count]
    send, recv, local, z_send, z_recv, z_local = refs[7 * count :]
    b, s = lax.axis_index("batch"), lax.axis_index("seq")
    core = lax.rem(s, 2)
    sibling = s + 1 - 2 * core
    chips = n // 2
    chip = s // 2
    greet_all(nb, n, b, s)
    order = [lax.rem(chip + d, chips) for d in list(range(1, chips)) + [0]]
    pair, own, far, last = {}, {}, {}, []
    for k, c in enumerate(order):
        for a in range(count):
            mine, first = scratch[5 * a], scratch[5 * a + 1]
            copy = remote(
                ins[a].at[:, 2 * c + 1 - core],
                first.at[k],
                send.at[a, k],
                recv.at[a, k],
                seq=sibling,
            )
            copy.start()
            pair[a, k] = copy
            copy = pltpu.make_async_copy(ins[a].at[:, 2 * c + core], mine.at[k], local.at[a, k])
            copy.start()
            own[a, k] = copy
    for k in range(chips - 1):
        for a in range(count):
            mine, first, passed, second, total = scratch[5 * a : 5 * a + 5]
            pair[a, k].wait_recv()
            own[a, k].wait()

            def add(i, carry, k=k, mine=mine, first=first, passed=passed):
                passed[k, i] = (mine[k, i].astype(F32) + first[k, i].astype(F32)).astype(BF16)
                return carry

            lax.fori_loop(0, nb, add, 0)
            copy = remote(
                passed.at[k],
                second.at[k],
                send.at[a, chips + k],
                recv.at[a, chips + k],
                seq=2 * order[k] + core,
            )
            copy.start()
            far[a, k] = copy
    for a in range(count):
        mine, first, passed, second, total = scratch[5 * a : 5 * a + 5]
        pair[a, chips - 1].wait_recv()
        own[a, chips - 1].wait()
        for k in range(chips - 1):
            far[a, k].wait_recv()

        def finish(i, carry, mine=mine, first=first, second=second, total=total):
            value = mine[chips - 1, i].astype(F32) + first[chips - 1, i].astype(F32)
            for k in range(chips - 1):
                value = value + second[k, i].astype(F32)
            total[i] = value.astype(BF16)
            return carry

        lax.fori_loop(0, nb, finish, 0)
        for d in range(1, nb):
            plane = lax.rem(b + d, nb)
            copy = remote(
                total.at[plane],
                outs[a].at[b],
                z_send.at[a, d],
                z_recv.at[a, d],
                batch=plane,
                seq=s,
            )
            copy.start()
            last.append(copy)
        copy = pltpu.make_async_copy(total.at[b], outs[a].at[b], z_local.at[a])
        copy.start()
        last.append(copy)
    for copy in list(pair.values()) + list(far.values()):
        copy.wait_send()
    for copy in last:
        copy.wait()


def scatter_sum(arrays, cid):
    nb, n = dims()
    chips = n // 2
    count = len(arrays)
    scratch = []
    for a in arrays:
        block = (nb,) + a.shape[2:]
        scratch += [
            pltpu.VMEM((chips,) + block, BF16),
            pltpu.VMEM((chips,) + block, BF16),
            pltpu.VMEM((chips - 1,) + block, BF16),
            pltpu.VMEM((chips - 1,) + block, BF16),
            pltpu.VMEM(block, BF16),
        ]
    dma = pltpu.SemaphoreType.DMA
    return pl.pallas_call(
        functools.partial(scatter_kernel, nb, n, count),
        out_shape=[jax.ShapeDtypeStruct((nb,) + a.shape[2:], a.dtype) for a in arrays],
        in_specs=[ANY] * count,
        out_specs=[ANY] * count,
        scratch_shapes=scratch
        + [
            dma((count, n)),
            dma((count, n)),
            dma((count, chips)),
            dma((count, nb)),
            dma((count, nb)),
            dma((count,)),
        ],
        compiler_params=params(cid),
    )(*arrays)


def mish_parts(v):
    e = jnp.exp(jnp.minimum(v, 20.0))
    n = e * (e + 2.0)
    inverse = 1.0 / (n + 2.0)
    return e, n, inverse


def mish(v):
    e, n, inverse = mish_parts(v)
    return v * (n * inverse)


def mish_slope(v):
    e, n, inverse = mish_parts(v)
    return n * inverse + v * (4.0 * e * (1.0 + e)) * inverse * inverse


CHUNK = 128


def place(buf, source, seg, length):
    rows = buf.shape[0]

    def clear(i, carry):
        buf[pl.ds(pl.multiple_of(i * 8, 8), 8), :] = jnp.zeros((8, buf.shape[1]), F32)
        return carry

    lax.fori_loop(0, rows // 8, clear, 0)

    def move(i, carry):
        at = pl.multiple_of(i * CHUNK, CHUNK)
        value = source(at)
        ids = seg[0, pl.ds(at, CHUNK), :]
        for u in range(SEGS):
            to = pl.ds(at + GAP * (u + 1), CHUNK)
            buf[to, :] = buf[to, :] + jnp.where(ids == u, value, 0.0)
        return carry

    lax.fori_loop(0, length // CHUNK, move, 0)


def unplace(buf, sink, seg, length):
    def move(i, carry):
        at = pl.multiple_of(i * CHUNK, CHUNK)
        ids = seg[0, pl.ds(at, CHUNK), :]
        value = buf[pl.ds(at + GAP, CHUNK), :]
        for u in range(1, SEGS):
            value = jnp.where(ids == u, buf[pl.ds(at + GAP * (u + 1), CHUNK), :], value)
        sink[0, pl.ds(at, CHUNK), :] = value.astype(sink.dtype)
        return carry

    lax.fori_loop(0, length // CHUNK, move, 0)


def spread_taps(x, buf, count, width):
    for k in range(TAPS):
        x[:, k * width : (k + 1) * width] = buf[pl.ds(k + 1, count, stride=FOLD), :].astype(BF16)


def fill_band(band, kernel, width):
    band[...] = jnp.zeros_like(band)
    for m in range(FOLD):
        band[m * width : (m + KERNEL) * width, m * width : (m + 1) * width] = kernel[...]


def conv_forward_kernel(count, length, width, u, seg, k1, k2, c1, c2, out, buf, live, x, band1, band2):
    @pl.when(pl.program_id(0) == 0)
    def _():
        fill_band(band1, k1, width)
        fill_band(band2, k2, width)

    place(live, lambda at: jnp.ones((CHUNK, width), F32), seg, length)
    place(buf, lambda at: u[0, pl.ds(at, CHUNK), :].astype(F32), seg, length)
    spread_taps(x, buf, count, width)
    c1[0] = jnp.dot(x[...], band1[...], preferred_element_type=F32)
    for m in range(FOLD):
        at = pl.ds(GAP + m, count, stride=FOLD)
        buf[at, :] = mish(c1[0, :, m * width : (m + 1) * width]) * live[at, :]
    spread_taps(x, buf, count, width)
    c2[0] = jnp.dot(x[...], band2[...], preferred_element_type=F32)
    for m in range(FOLD):
        at = pl.ds(GAP + m, count, stride=FOLD)
        buf[at, :] = mish(c2[0, :, m * width : (m + 1) * width])
    unplace(buf, out, seg, length)


def conv_sizes(length):
    count = -(-(length + GAP * (SEGS - 1)) // FOLD)
    count = -(-count // 16) * 16
    return count, FOLD * count + 48


def whole(shape):
    zeros = (0,) * len(shape)
    return pl.BlockSpec(shape, lambda *i: zeros)


def by_row(shape):
    return pl.BlockSpec((1,) + tuple(shape[1:]), lambda r: (r,) + (0,) * (len(shape) - 1))


def conv_forward(u, seg, k1, k2):
    rows, length, width = u.shape
    count, buffer = conv_sizes(length)
    folded = (rows, count, FOLD * width)
    return pl.pallas_call(
        functools.partial(conv_forward_kernel, count, length, width),
        grid=(rows,),
        in_specs=[by_row(u.shape), by_row(seg.shape), whole(k1.shape), whole(k2.shape)],
        out_specs=[by_row(folded), by_row(folded), by_row(u.shape)],
        out_shape=[
            jax.ShapeDtypeStruct(folded, F32),
            jax.ShapeDtypeStruct(folded, F32),
            jax.ShapeDtypeStruct(u.shape, BF16),
        ],
        scratch_shapes=[
            pltpu.VMEM((buffer, width), F32),
            pltpu.VMEM((buffer, width), F32),
            pltpu.VMEM((count, TAPS * width), BF16),
            pltpu.VMEM((TAPS * width, FOLD * width), BF16),
            pltpu.VMEM((TAPS * width, FOLD * width), BF16),
        ],
        compiler_params=params(),
    )(u, seg, k1, k2)


def weight_sums(grad, turned, x, width):
    pair = 2 * width
    for t in range(TAPS // 2):
        product = jnp.dot(
            turned[...], x[:, t * pair : (t + 1) * pair], preferred_element_type=F32
        )
        for half in range(2):
            for m in range(FOLD):
                k = 2 * t + half - m
                if 0 <= k < KERNEL:
                    grad[k] = grad[k] + product[
                        m * width : (m + 1) * width, half * width : (half + 1) * width
                    ]


def conv_backward_kernel(
    count, length, width, d, u, seg, c1, c2, k1, k2, dh, g1, g2, buf, grads, live, x, turned, band1, band2
):
    @pl.when(pl.program_id(0) == 0)
    def _():
        fill_band(band1, k1, width)
        fill_band(band2, k2, width)
        g1[...] = jnp.zeros_like(g1)
        g2[...] = jnp.zeros_like(g2)

    place(live, lambda at: jnp.ones((CHUNK, width), F32), seg, length)
    place(grads, lambda at: d[0, pl.ds(at, CHUNK), :].astype(F32), seg, length)
    for m in range(FOLD):
        at = pl.ds(GAP + m, count, stride=FOLD)
        lanes = slice(m * width, (m + 1) * width)
        value = grads[at, :] * mish_slope(c2[0, :, lanes])
        grads[at, :] = value
        turned[lanes, :] = value.T.astype(BF16)
    place(buf, lambda at: jnp.zeros((CHUNK, width), F32), seg, length)
    for m in range(FOLD):
        at = pl.ds(GAP + m, count, stride=FOLD)
        buf[at, :] = mish(c1[0, :, m * width : (m + 1) * width]) * live[at, :]
    spread_taps(x, buf, count, width)
    weight_sums(g2, turned, x, width)
    spread_taps(x, grads, count, width)
    folded = jnp.dot(x[...], band2[...], preferred_element_type=F32)
    for m in range(FOLD):
        at = pl.ds(GAP + m, count, stride=FOLD)
        lanes = slice(m * width, (m + 1) * width)
        value = folded[:, lanes] * mish_slope(c1[0, :, lanes]) * live[at, :]
        grads[at, :] = value
        turned[lanes, :] = value.T.astype(BF16)
    place(buf, lambda at: u[0, pl.ds(at, CHUNK), :].astype(F32), seg, length)
    spread_taps(x, buf, count, width)
    weight_sums(g1, turned, x, width)
    spread_taps(x, grads, count, width)
    folded = jnp.dot(x[...], band1[...], preferred_element_type=F32)
    for m in range(FOLD):
        at = pl.ds(GAP + m, count, stride=FOLD)
        buf[at, :] = folded[:, m * width : (m + 1) * width]
    unplace(buf, dh, seg, length)


def conv_backward(d, u, seg, c1, c2, k1, k2):
    rows, length, width = u.shape
    count, buffer = conv_sizes(length)
    grad = (KERNEL, width, width)
    band = pltpu.VMEM((TAPS * width, FOLD * width), BF16)
    return pl.pallas_call(
        functools.partial(conv_backward_kernel, count, length, width),
        grid=(rows,),
        in_specs=[
            by_row(d.shape),
            by_row(u.shape),
            by_row(seg.shape),
            by_row(c1.shape),
            by_row(c2.shape),
            whole(k1.shape),
            whole(k2.shape),
        ],
        out_specs=[by_row(u.shape), whole(grad), whole(grad)],
        out_shape=[
            jax.ShapeDtypeStruct(u.shape, BF16),
            jax.ShapeDtypeStruct(grad, F32),
            jax.ShapeDtypeStruct(grad, F32),
        ],
        scratch_shapes=[
            pltpu.VMEM((buffer, width), F32),
            pltpu.VMEM((buffer, width), F32),
            pltpu.VMEM((buffer, width), F32),
            pltpu.VMEM((count, TAPS * width), BF16),
            pltpu.VMEM((FOLD * width, count), BF16),
            band,
            band,
        ],
        compiler_params=params(),
    )(d, u, seg, c1, c2, k1, k2)


def pair_swap(x):
    width = x.shape[1]
    if width % 128:
        x = jnp.concatenate([x, x], axis=1)
    lane = lax.broadcasted_iota(jnp.int32, x.shape, 1)
    after = pltpu.roll(x, x.shape[1] - 1, 1)
    before = pltpu.roll(x, 1, 1)
    return jnp.where(lax.rem(lane, 2) == 0, -after, before)[:, :width]


def qkv_kernel(width, x, w, cos, sin, q, k, v):
    got = lax.dot_general(
        x[0], w[...], (((1,), (1,)), ((), ())), preferred_element_type=F32
    )
    for p, out in enumerate((q, k)):
        part = got[:, p * width : (p + 1) * width]
        out[0] = (part * cos[0] + pair_swap(part) * sin[0]).astype(BF16)
    v[0] = got[:, 2 * width :].astype(BF16)


def qkv_forward(x, w, cos, sin):
    rows, length, depth = x.shape
    width = w.shape[0] // 3
    block = 512
    spec = pl.BlockSpec((1, block, width), lambda r, i: (r, i, 0))
    shape = jax.ShapeDtypeStruct((rows, length, width), BF16)
    return pl.pallas_call(
        functools.partial(qkv_kernel, width),
        grid=(rows, length // block),
        in_specs=[
            pl.BlockSpec((1, block, depth), lambda r, i: (r, i, 0)),
            whole(w.shape),
            spec,
            spec,
        ],
        out_specs=[spec] * 3,
        out_shape=[shape] * 3,
        compiler_params=params(),
    )(x, w, cos, sin)


def attention_forward_kernel(width, q, k, v, q_code, k_code, out, low, log_sum):
    heads = width // HEAD
    lane = lax.broadcasted_iota(jnp.int32, q.shape[1:], 1) // HEAD
    allowed = q_code[0] == k_code[0]
    queries = q[0] * 0.125
    result, logs = None, None
    for h in range(heads):
        chosen = jnp.where(lane == h, queries, jnp.zeros_like(queries))
        scores = lax.dot_general(
            chosen, k[0], (((1,), (1,)), ((), ())), preferred_element_type=F32
        )
        scores = jnp.where(allowed, scores, MASKED)
        peak = jnp.max(scores, axis=1, keepdims=True)
        weights = jnp.exp(scores - peak)
        total = jnp.sum(weights, axis=1, keepdims=True)
        value = jnp.dot(weights.astype(BF16), v[0], preferred_element_type=F32) / total
        log = jnp.broadcast_to(peak + jnp.log(total), value.shape)
        result = value if h == 0 else jnp.where(lane == h, value, result)
        logs = log if h == 0 else jnp.where(lane == h, log, logs)
    out[0] = result
    low[0] = result.astype(BF16)
    log_sum[0] = logs


def attention_forward(q, k, v, q_code, k_code):
    rows, length, width = q.shape
    block = 256
    spec = pl.BlockSpec((1, block, width), lambda r, i: (r, i, 0))
    row = pl.BlockSpec((1, length, width), lambda r, i: (r, 0, 0))
    return pl.pallas_call(
        functools.partial(attention_forward_kernel, width),
        grid=(rows, length // block),
        in_specs=[
            spec,
            row,
            row,
            pl.BlockSpec((1, block, 1), lambda r, i: (r, i, 0)),
            pl.BlockSpec((1, 1, length), lambda r, i: (r, 0, 0)),
        ],
        out_specs=[spec] * 3,
        out_shape=[
            jax.ShapeDtypeStruct(q.shape, F32),
            jax.ShapeDtypeStruct(q.shape, BF16),
            jax.ShapeDtypeStruct(q.shape, F32),
        ],
        compiler_params=params(),
    )(q, k, v, q_code, k_code)


BLOCK = 256


def attention_backward_kernel(
    length, width, low_edge, high_edge, q, k, v, g, log_sum, delta, k_code, q_code, cos, sin, out, dq, dk, dv
):
    heads = width // HEAD
    row = pl.program_id(0)
    lane = lax.broadcasted_iota(jnp.int32, (BLOCK, width), 1) // HEAD
    dk[...] = jnp.zeros_like(dk)
    dv[...] = jnp.zeros_like(dv)

    def outer(i, carry):
        at = pl.ds(pl.multiple_of(i * BLOCK, BLOCK), BLOCK)
        queries = q[0, at, :] * 0.125
        grads = g[0, at, :]
        zero = jnp.zeros_like(queries)
        queries_of = [jnp.where(lane == h, queries, zero) for h in range(heads)]
        grads_of = [jnp.where(lane == h, grads, zero) for h in range(heads)]
        dq[...] = jnp.zeros_like(dq)

        def inner(j, carry):
            to = pl.ds(pl.multiple_of(j * BLOCK, BLOCK), BLOCK)
            keys, values = k[0, to, :], v[0, to, :]
            allowed = k_code[0, to, :] == q_code[0, :, at]
            dk_part, dv_part, dq_part = None, None, None
            for h in range(heads):
                keys_of = jnp.where(lane == h, keys, zero)
                scores = lax.dot_general(
                    keys, queries_of[h], (((1,), (1,)), ((), ())), preferred_element_type=F32
                )
                probs = jnp.where(allowed, jnp.exp(scores - log_sum[0, h : h + 1, at]), 0.0)
                grad_probs = lax.dot_general(
                    values, grads_of[h], (((1,), (1,)), ((), ())), preferred_element_type=F32
                )
                grad_scores = (probs * (grad_probs - delta[0, h : h + 1, at])).astype(BF16)
                a = jnp.dot(probs.astype(BF16), grads_of[h], preferred_element_type=F32)
                c = jnp.dot(grad_scores, queries_of[h], preferred_element_type=F32)
                e = lax.dot_general(
                    grad_scores, keys_of, (((0,), (0,)), ((), ())), preferred_element_type=F32
                )
                dv_part = a if h == 0 else dv_part + a
                dk_part = c if h == 0 else dk_part + c
                dq_part = e if h == 0 else dq_part + e
            dv[to, :] = dv[to, :] + dv_part
            dk[to, :] = dk[to, :] + dk_part
            dq[...] = dq[...] + dq_part
            return carry

        lax.fori_loop(low_edge[row, i], high_edge[row, i], inner, 0)
        grad = dq[...] * 0.125
        turned = grad * cos[0, at, :] - pair_swap(grad) * sin[0, at, :]
        out[0, at, 0:width] = turned.astype(BF16)
        return carry

    lax.fori_loop(0, length // BLOCK, outer, 0)

    def finish(i, carry):
        at = pl.ds(pl.multiple_of(i * BLOCK, BLOCK), BLOCK)
        grad = dk[at, :]
        turned = grad * cos[0, at, :] - pair_swap(grad) * sin[0, at, :]
        out[0, at, width : 2 * width] = turned.astype(BF16)
        out[0, at, 2 * width : 3 * width] = dv[at, :].astype(BF16)
        return carry

    lax.fori_loop(0, length // BLOCK, finish, 0)


def attention_backward(q, k, v, g, log_sum, delta, k_code, q_code, cos, sin, low_edge, high_edge):
    rows, length, width = q.shape

    def spec(shape):
        return pl.BlockSpec((1,) + tuple(shape[1:]), lambda r, *_: (r,) + (0,) * (len(shape) - 1))

    arrays = (q, k, v, g, log_sum, delta, k_code, q_code, cos, sin)
    out = (rows, length, 3 * width)
    return pl.pallas_call(
        functools.partial(attention_backward_kernel, length, width),
        grid_spec=pltpu.PrefetchScalarGridSpec(
            num_scalar_prefetch=2,
            grid=(rows,),
            in_specs=[spec(a.shape) for a in arrays],
            out_specs=spec(out),
            scratch_shapes=[
                pltpu.VMEM((BLOCK, width), F32),
                pltpu.VMEM((length, width), F32),
                pltpu.VMEM((length, width), F32),
            ],
        ),
        out_shape=jax.ShapeDtypeStruct(out, BF16),
        compiler_params=params(),
    )(low_edge, high_edge, *arrays)


def times(left, right):
    return lax.dot_general(left, right, (((1,), (0,)), ((), ())), preferred_element_type=F32)


def times_t(left, right):
    return lax.dot_general(left, right, (((1,), (1,)), ((), ())), preferred_element_type=F32)


def rows_sum(left, right):
    return lax.dot_general(left, right, (((0,), (0,)), ((), ())), preferred_element_type=F32)


def layer_norm(field):
    centre = field - jnp.mean(field, axis=-1, keepdims=True)
    return centre * lax.rsqrt(jnp.mean(centre * centre, axis=-1, keepdims=True) + EPSILON)


def modulate(field, scaling, shifting):
    return layer_norm(field) * (1.0 + scaling) + shifting


def gelu_curve(inputs):
    return jax.nn.gelu(inputs, approximate=True)


def by_segment(ids, table):
    value = table[:, SEGS - 1][:, None, :]
    for u in range(SEGS - 2, -1, -1):
        value = jnp.where(ids[:, :, None] == u, table[:, u][:, None, :], value)
    return value


def rope_tables(segment_ids, starts, width):
    length = segment_ids.shape[1]
    pairs = (np.arange(width) % HEAD) // 2
    freq = 10000.0 ** (-2.0 * pairs / HEAD)
    angle = np.arange(length)[:, None] * freq[None, :]
    cos_t = jnp.asarray(np.cos(angle).astype(np.float32))[None]
    sin_t = jnp.asarray(np.sin(angle).astype(np.float32))[None]
    offset = starts.astype(F32)[:, :, None] * jnp.asarray(freq.astype(np.float32))
    cos_o = by_segment(segment_ids, jnp.cos(offset))
    sin_o = by_segment(segment_ids, jnp.sin(offset))
    return cos_t * cos_o + sin_t * sin_o, sin_t * cos_o - cos_t * sin_o


def conv_blocks(got, width):
    own = jnp.moveaxis(got, 0, 1).reshape(KERNEL, width, CHAN)
    groups = width // CHAN
    if groups == 1:
        return own
    index = np.arange(width) // CHAN
    same = jnp.asarray((index[:, None] == index[None, :]).astype(np.float32)).astype(BF16)
    return jnp.tile(own, (1, 1, groups)) * same


def on_device(
    mel_inputs,
    text_ids,
    segment_ids,
    key_mask,
    time_index,
    input_proj,
    conv_first,
    conv_second,
    time_table,
    adaln_proj,
    qkv_proj,
    out_proj,
    up_proj,
    down_proj,
    text_table,
    grad_out,
):
    nb, n = dims()
    ndev = nb * n
    rows, frames = mel_inputs.shape[:2]
    tokens = rows * frames
    length = frames * n
    width = D // n
    part = D // ndev
    mine = lax.axis_index("seq")
    first_frame = mine * frames

    out_t, up_t, down_t = out_proj.T, up_proj.T, down_proj.T
    wide_t = jnp.concatenate([out_t, up_t, down_t[:, :D], down_t[:, D:]], axis=0)
    per = wide_t.shape[0]
    late = lax.all_gather(wide_t, ("batch", "seq"), axis=0, tiled=True).reshape(ndev, per, D)

    full_in, full_text, full_time, all_index, got_first, got_second, got_qkv = start_gather(
        [input_proj.T, text_table.T, time_table.T, time_index],
        conv_first,
        conv_second,
        qkv_proj.T.reshape(3, part, D),
        0,
    )
    in_t = full_in.reshape(D, input_proj.shape[0])
    text_t = full_text.reshape(-1, VOCAB)
    time_t = full_time.reshape(D, STEPS)
    slot_steps = all_index[:, 0].reshape(nb * rows * SEGS)
    qkv_t = got_qkv.reshape(3 * width, D)
    block_first = conv_blocks(got_first, width)
    block_second = conv_blocks(got_second, width)

    own_ids = lax.dynamic_slice_in_dim(segment_ids, first_frame, frames, 1)
    seg_column = segment_ids[:, :, None]
    seg_index = jnp.arange(SEGS, dtype=jnp.int32)
    starts = jnp.sum((segment_ids[:, None, :] < seg_index[None, :, None]).astype(jnp.int32), axis=2)

    text_hot = (
        text_ids.reshape(-1)[:, None] == jnp.arange(VOCAB, dtype=jnp.int32)[None, :]
    ).astype(BF16)
    text_embed = times_t(text_hot, text_t).astype(BF16)
    joined = jnp.concatenate([mel_inputs.reshape(tokens, 2 * MEL), text_embed], axis=1)
    hidden = times_t(joined, in_t).reshape(rows, frames, D)

    step_hot = (
        slot_steps[:, None] == jnp.arange(STEPS, dtype=jnp.int32)[None, :]
    ).astype(BF16)
    cond_value = times_t(step_hot, time_t)
    soft_cond = jax.nn.silu(cond_value).astype(BF16)
    own_mod = times(soft_cond, adaln_proj)
    mod_got = spray(own_mod.reshape(nb, rows * SEGS, 6 * part), True, 1)
    modulation = mod_got.transpose(1, 0, 2).reshape(rows, SEGS, 6, D)
    shift_attn, scale_attn, gate_attn, shift_feed, scale_feed, gate_feed = (
        by_segment(own_ids, modulation[:, :, i]) for i in range(6)
    )

    (hidden_c,) = to_channels([hidden.astype(BF16)], 2)
    conv_one, conv_two, bump_c = conv_forward(
        hidden_c,
        seg_column,
        block_first.reshape(KERNEL * width, width),
        block_second.reshape(KERNEL * width, width),
    )
    (bump,) = to_frames([bump_c], 3)
    embedded = hidden + bump.astype(F32)

    normed = modulate(embedded, scale_attn, shift_attn).astype(BF16)
    normed_all = group_gather(normed, 4).reshape(rows, length, D)
    cos, sin = rope_tables(segment_ids, starts, width)
    query, key, value = qkv_forward(normed_all, qkv_t, cos, sin)
    seg_code = segment_ids.astype(F32)
    key_code = jnp.where(key_mask > 0, seg_code, -1.0)
    attended, attended_low, log_lanes = attention_forward(
        query, key, value, seg_code[:, :, None], key_code[:, None, :]
    )
    (attended_own,) = to_frames([attended_low], 5)
    attended_own = attended_own.reshape(tokens, D)

    full_out = late[:, :part].reshape(D, D)
    full_up = late[:, part : 3 * part].reshape(2 * D, D)
    full_down = jnp.concatenate([late[:, 3 * part : 4 * part], late[:, 4 * part :]], axis=2).reshape(
        D, 2 * D
    )

    branch = times_t(attended_own, full_out).reshape(rows, frames, D)
    middle = embedded + gate_attn * branch
    normed_feed = modulate(middle, scale_feed, shift_feed).astype(BF16).reshape(tokens, D)
    up_value = times_t(normed_feed, full_up)
    gelu_low = gelu_curve(up_value).astype(BF16)
    feed_out = times_t(gelu_low, full_down).reshape(rows, frames, D)
    block_out = (middle + gate_feed * feed_out).astype(BF16)

    cotangent = grad_out.astype(F32)
    grad_gate_feed = cotangent * feed_out
    grad_feed = (gate_feed * cotangent).astype(BF16).reshape(tokens, D)
    grad_down = rows_sum(grad_feed, gelu_low).astype(BF16)
    grad_gelu = times(grad_feed, full_down)
    grad_up_value = jax.vjp(gelu_curve, up_value)[1](grad_gelu)[0].astype(BF16)
    grad_up = rows_sum(grad_up_value, normed_feed).astype(BF16)
    grad_normed_feed = times(grad_up_value, full_up).reshape(rows, frames, D)
    grad_mid_part, grad_scale_feed, grad_shift_feed = jax.vjp(
        modulate, middle, scale_feed, shift_feed
    )[1](grad_normed_feed)
    grad_middle = cotangent + grad_mid_part
    grad_gate_attn = grad_middle * branch
    grad_branch = (gate_attn * grad_middle).astype(BF16).reshape(tokens, D)
    grad_out_weights = rows_sum(grad_branch, attended_own).astype(BF16)
    grad_att = times(grad_branch, full_out).astype(BF16).reshape(rows, frames, D)

    late_grads = jnp.concatenate(
        [
            grad_out_weights.reshape(ndev, part, D),
            grad_up.reshape(ndev, 2 * part, D),
            grad_down[:, :D].reshape(ndev, part, D),
            grad_down[:, D:].reshape(ndev, part, D),
        ],
        axis=1,
    )
    late_sum = lax.psum_scatter(
        late_grads, ("batch", "seq"), scatter_dimension=0, tiled=False
    ).astype(F32)

    (grad_att_c,) = to_channels([grad_att], 6)
    heads = width // HEAD
    delta = jnp.sum(
        (grad_att_c.astype(F32) * attended).reshape(rows, length, heads, HEAD), axis=3
    ).transpose(0, 2, 1)
    log_rows = log_lanes.reshape(rows, length, heads, HEAD)[:, :, :, 0].transpose(0, 2, 1)
    block_first_ids = segment_ids[:, ::BLOCK]
    block_last_ids = segment_ids[:, BLOCK - 1 :: BLOCK]
    ends = jnp.sum((segment_ids[:, None, :] <= seg_index[None, :, None]).astype(jnp.int32), axis=2)
    low_edge = (
        jnp.sum(jnp.where(block_first_ids[:, :, None] == seg_index, starts[:, None, :], 0), axis=2)
        // BLOCK
    )
    high_edge = (
        jnp.sum(jnp.where(block_last_ids[:, :, None] == seg_index, ends[:, None, :], 0), axis=2)
        + BLOCK
        - 1
    ) // BLOCK
    grad_projected = attention_backward(
        query,
        key,
        value,
        grad_att_c,
        log_rows,
        delta,
        key_code[:, :, None],
        seg_code[:, None, :],
        cos,
        sin,
        low_edge,
        high_edge,
    ).reshape(rows * length, 3 * width)
    grad_qkv = rows_sum(grad_projected, normed_all.reshape(rows * length, D)).astype(BF16)
    grad_normed = group_sum(
        times(grad_projected, qkv_t).astype(BF16).reshape(rows, n, frames, D), 7
    )

    grad_emb_part, grad_scale_attn, grad_shift_attn = jax.vjp(
        modulate, embedded, scale_attn, shift_attn
    )[1](grad_normed)
    grad_embedded = grad_middle + grad_emb_part

    select = (own_ids[:, :, None] == seg_index).astype(F32)
    grad_frame = jnp.concatenate(
        [
            grad_shift_attn,
            grad_scale_attn,
            grad_gate_attn,
            grad_shift_feed,
            grad_scale_feed,
            grad_gate_feed,
        ],
        axis=2,
    )
    local_sums = jnp.einsum("rfs,rfc->rsc", select, grad_frame, precision=EXACT)
    slots = rows * SEGS
    sums_out = local_sums.reshape(slots, ndev, 6 * part).transpose(1, 0, 2)
    sums_got = spray(sums_out, False, 8).reshape(nb, n, slots, 6 * part)
    grad_mod = jnp.sum(sums_got, axis=1).astype(BF16).reshape(nb * slots, 6 * part)
    grad_adaln = rows_sum(soft_cond, grad_mod)
    soft_part = times_t(grad_mod, adaln_proj)
    soft_got = spray(soft_part.reshape(nb * slots, ndev, part).transpose(1, 0, 2), False, 9)
    grad_soft = jnp.sum(soft_got, axis=0)
    own_cond = times(step_hot, time_table)
    grad_cond = jax.vjp(jax.nn.silu, own_cond)[1](grad_soft)[0]
    grad_time = jnp.dot(step_hot.astype(F32).T, grad_cond, precision=EXACT)

    (grad_emb_c,) = to_channels([grad_embedded.astype(BF16)], 10)
    flip_first = block_first[::-1].transpose(0, 2, 1).reshape(KERNEL * width, width)
    flip_second = block_second[::-1].transpose(0, 2, 1).reshape(KERNEL * width, width)
    grad_hidden_c, sums_first, sums_second = conv_backward(
        grad_emb_c, hidden_c, seg_column, conv_one, conv_two, flip_first, flip_second
    )
    (grad_hidden_conv,) = to_frames([grad_hidden_c], 11)

    def conv_pieces(sums):
        groups = width // CHAN
        own = jnp.stack(
            [
                sums[:, g * CHAN : (g + 1) * CHAN, g * CHAN : (g + 1) * CHAN]
                for g in range(groups)
            ],
            axis=1,
        )
        own = own.transpose(0, 1, 3, 2).reshape(KERNEL, nb, part, CHAN)
        return jnp.moveaxis(own, 1, 0)[None].astype(BF16)

    got = column_grads(
        [
            conv_pieces(sums_first),
            conv_pieces(sums_second),
            grad_qkv.reshape(3, nb, part, D),
        ],
        12,
    )
    grad_first = jnp.sum(got[0].astype(F32), axis=0)[0]
    grad_second = jnp.sum(got[1].astype(F32), axis=0)[0]
    grad_qkv_own = jnp.sum(got[2].astype(F32), axis=0).reshape(3 * part, D).T

    grad_hidden = (grad_embedded + grad_hidden_conv.astype(F32)).astype(BF16).reshape(tokens, D)
    grad_input = rows_sum(grad_hidden, joined).astype(BF16)
    grad_joined = times(grad_hidden, in_t)
    grad_mels = grad_joined[:, : 2 * MEL].reshape(rows, frames, 2 * MEL)
    grad_embed = grad_joined[:, 2 * MEL :].astype(BF16)
    grad_text = rows_sum(grad_embed, text_hot).astype(BF16)
    in_sum, text_sum = scatter_sum(
        [
            grad_input.reshape(nb, n, part, -1),
            grad_text.reshape(nb, n, -1, VOCAB),
        ],
        13,
    )
    grad_input_own = jnp.sum(in_sum.astype(F32), axis=0).T
    grad_text_own = jnp.sum(text_sum.astype(F32), axis=0).T
    grad_down_own = jnp.concatenate([late_sum[3 * part : 4 * part], late_sum[4 * part :]], axis=1)

    return (
        block_out,
        grad_mels,
        grad_input_own,
        grad_first,
        grad_second,
        grad_time,
        grad_adaln,
        grad_qkv_own,
        late_sum[:part].T,
        late_sum[part : 3 * part].T,
        grad_down_own.T,
        grad_text_own,
    )


def solution(mesh):
    frames = P("batch", "seq", None)
    columns = P(None, ("batch", "seq"))
    taps = P(None, ("batch", "seq"), None)
    in_specs = (
        frames,
        P("batch", "seq"),
        P("batch", None),
        P("batch", None),
        P("batch", None),
        columns,
        taps,
        taps,
        columns,
        columns,
        columns,
        columns,
        columns,
        columns,
        columns,
        frames,
    )
    out_specs = (
        frames,
        frames,
        columns,
        taps,
        taps,
        columns,
        columns,
        columns,
        columns,
        columns,
        columns,
        columns,
    )
    return jax.shard_map(
        on_device, mesh=mesh, in_specs=in_specs, out_specs=out_specs, check_vma=False
    )
```

```python
import functools

import jax
import jax.numpy as jnp
import numpy as np
from jax import lax
from jax.experimental import pallas as pl
from jax.experimental.pallas import tpu as pltpu
from jax.sharding import PartitionSpec as P

D = 1024
HEADS = 16
HEAD = 64
MEL = 100
VOCAB = 2546
KERNEL = 31
HALF = KERNEL // 2
CHAN = 64
STEPS = 32
SEGS = 4
GAP = 16
FOLD = 4
TAPS = KERNEL + FOLD - 1

EPSILON = 1e-06
MASKED = -1e30
EXACT = lax.Precision.HIGHEST
MESH = pl.DeviceIdType.MESH
ANY = pl.BlockSpec(memory_space=pl.ANY)
VMEM_LIMIT = 56 * 1024 * 1024
F32 = jnp.float32
BF16 = jnp.bfloat16


def dims():
    return lax.axis_size("batch"), lax.axis_size("seq")


def params(cid=None):
    if cid is None:
        return pltpu.CompilerParams(vmem_limit_bytes=VMEM_LIMIT)
    return pltpu.CompilerParams(
        collective_id=cid, has_side_effects=True, vmem_limit_bytes=VMEM_LIMIT
    )


def greet_all(nb, n, b, s):
    sem = pltpu.get_barrier_semaphore()
    me = b * n + s
    for d in range(1, nb * n):
        other = lax.rem(me + d, nb * n)
        pl.semaphore_signal(
            sem,
            inc=1,
            device_id={"batch": other // n, "seq": lax.rem(other, n)},
            device_id_type=MESH,
        )
    pl.semaphore_wait(sem, nb * n - 1)


def greet_group(n, s):
    sem = pltpu.get_barrier_semaphore()
    for d in range(1, n):
        pl.semaphore_signal(
            sem, inc=1, device_id={"seq": lax.rem(s + d, n)}, device_id_type=MESH
        )
    pl.semaphore_wait(sem, n - 1)


def block_of(b, s, n):
    chips, core = n // 2, lax.rem(s, 2)
    return 2 * lax.rem(s // 2 + b + (chips // 2) * core, chips) + core


def holder_of(b, m, n, nb):
    chips, core = n // 2, lax.rem(m, 2)
    turned = m // 2 + (nb + chips) * chips - b - (chips // 2) * core
    return 2 * lax.rem(turned, chips) + core


def remote(src, dst, send, recv, **where):
    return pltpu.make_async_remote_copy(
        src_ref=src,
        dst_ref=dst,
        send_sem=send,
        recv_sem=recv,
        device_id=where,
        device_id_type=MESH,
    )


class Task:
    def __init__(self, operands, outs, scratch, body, everyone=False):
        self.operands, self.outs, self.scratch = list(operands), list(outs), list(scratch)
        self.body, self.everyone = body, everyone


def transfer_kernel(bodies, sizes, everyone, nb, n, *refs):
    b, s = lax.axis_index("batch"), lax.axis_index("seq")
    counts = [sum(size[i] for size in sizes) for i in range(3)]
    pools = [
        list(refs[: counts[0]]),
        list(refs[counts[0] : counts[0] + counts[1]]),
        list(refs[counts[0] + counts[1] :]),
    ]
    running = []
    for body, size in zip(bodies, sizes):
        taken = []
        for i in range(3):
            taken.append(pools[i][: size[i]])
            pools[i] = pools[i][size[i] :]
        running.append(body(*taken, b, s, nb, n))
    if everyone:
        greet_all(nb, n, b, s)
    else:
        greet_group(n, s)
    while running:
        left = []
        for task in running:
            try:
                next(task)
                left.append(task)
            except StopIteration:
                pass
        running = left


def transfer(tasks, cid):
    nb, n = dims()
    operands = [x for task in tasks for x in task.operands]
    outs = [x for task in tasks for x in task.outs]
    sizes = [(len(t.operands), len(t.outs), len(t.scratch)) for t in tasks]
    got = pl.pallas_call(
        functools.partial(
            transfer_kernel,
            [t.body for t in tasks],
            sizes,
            any(t.everyone for t in tasks),
            nb,
            n,
        ),
        out_shape=outs,
        in_specs=[ANY] * len(operands),
        out_specs=[ANY] * len(outs),
        scratch_shapes=[x for task in tasks for x in task.scratch],
        compiler_params=params(cid),
    )(*operands)
    got = list(got)
    result = []
    for size in sizes:
        result.append(got[: size[1]])
        got = got[size[1] :]
    return result


DMA = pltpu.SemaphoreType.DMA


def like(x, shape, dtype=None):
    return jax.ShapeDtypeStruct(tuple(shape), dtype or x.dtype)


def swap_task(x, shape, parts):
    n = dims()[1]

    def body(ins, outs, scratch, b, s, nb, n):
        send, recv, local = scratch
        src, dst = parts(ins[0], outs[0], b, s)
        copies = []
        for d in range(1, n):
            t = lax.rem(s + d, n)
            copy = remote(src(t), dst, send.at[d], recv.at[d], seq=t)
            copy.start()
            copies.append(copy)
        own = pltpu.make_async_copy(src(s), dst, local)
        own.start()
        copies.append(own)
        yield
        yield
        for copy in copies:
            copy.wait()

    return Task([x], [like(x, shape)], [DMA((n,)), DMA((n,)), DMA], body)


def to_channels(x):
    n = dims()[1]
    rows, frames = x.shape[:2]
    width = x.shape[2] // n
    if width % 128 == 0:

        def parts(x, o, b, s):
            first = pl.multiple_of(s * frames, 16)
            return (
                lambda t: x.at[
                    :, :, pl.ds(pl.multiple_of(block_of(b, t, n) * width, 128), width)
                ]
            ), o.at[:, pl.ds(first, frames), :]

        return swap_task(x, (rows, n * frames, width), parts), lambda got: got[0]

    def split_parts(x, o, b, s):
        return (lambda t: x.at[block_of(b, t, n)]), o.at[s]

    split = x.reshape(rows, frames, n, width).transpose(2, 0, 1, 3)
    return (
        swap_task(split, split.shape, split_parts),
        lambda got: got[0].transpose(1, 0, 2, 3).reshape(rows, n * frames, width),
    )


def to_frames(x):
    n = dims()[1]
    rows, length, width = x.shape
    frames = length // n
    if width % 128 == 0:

        def parts(x, o, b, s):
            first = pl.multiple_of(block_of(b, s, n) * width, 128)
            return (
                lambda t: x.at[:, pl.ds(pl.multiple_of(t * frames, 16), frames), :]
            ), o.at[:, :, pl.ds(first, width)]

        return swap_task(x, (rows, frames, n * width), parts), lambda got: got[0]

    def split_parts(x, o, b, s):
        return (lambda t: x.at[t]), o.at[block_of(b, s, n)]

    split = x.reshape(rows, n, frames, width).transpose(1, 0, 2, 3)
    return (
        swap_task(split, split.shape, split_parts),
        lambda got: got[0].transpose(1, 2, 0, 3).reshape(rows, frames, n * width),
    )


def spray_task(x, by_batch):
    nb, n = dims()
    ndev = nb * n

    def body(ins, outs, scratch, b, s, nb, n):
        send, recv, local = scratch
        x, o = ins[0], outs[0]
        me = b * n + s
        own = pltpu.make_async_copy(x.at[b if by_batch else me], o.at[me], local)
        own.start()
        copies = [own]
        for d in range(1, ndev):
            other = lax.rem(me + d, ndev)
            plane, where = other // n, lax.rem(other, n)
            copy = remote(
                x.at[plane if by_batch else other],
                o.at[me],
                send.at[d],
                recv.at[d],
                batch=plane,
                seq=where,
            )
            copy.start()
            copies.append(copy)
        yield
        yield
        for copy in copies:
            copy.wait()

    return Task(
        [x], [like(x, (ndev,) + x.shape[1:])], [DMA((ndev,)), DMA((ndev,)), DMA], body, True
    )


def gather_task(x):
    n = dims()[1]

    def body(ins, outs, scratch, b, s, nb, n):
        send, recv, local = scratch
        x, o = ins[0], outs[0]
        core = lax.rem(s, 2)
        sibling = s + 1 - 2 * core
        chips = n // 2
        far, near = [], []
        for d in range(1, chips):
            copy = remote(x, o.at[:, s], send.at[d], recv.at[d], seq=lax.rem(s + 2 * d, n))
            copy.start()
            far.append(copy)
        copy = remote(x, o.at[:, s], send.at[0], recv.at[0], seq=sibling)
        copy.start()
        near.append(copy)
        own = pltpu.make_async_copy(x, o.at[:, s], local)
        own.start()
        yield
        for d in range(1, chips):
            far[d - 1].wait_recv()
            source = lax.rem(s - 2 * d + n, n)
            copy = remote(
                o.at[:, source],
                o.at[:, source],
                send.at[chips + d],
                recv.at[chips + d],
                seq=sibling,
            )
            copy.start()
            near.append(copy)
        yield
        own.wait()
        for copy in far:
            copy.wait_send()
        for copy in near:
            copy.wait()

    out = like(x, (x.shape[0], n) + x.shape[1:])
    return Task([x], [out], [DMA((n,)), DMA((n,)), DMA], body)


def quad_gather_task(x):
    n = dims()[1]
    frames = x.shape[1]
    half = frames // 2

    def body(ins, outs, scratch, b, s, nb, n):
        send, recv, local = scratch
        x, o = ins[0], outs[0]
        core, chip = lax.rem(s, 2), s // 2
        sibling = s + 1 - 2 * core
        flip_x = chip + 1 - 2 * lax.rem(chip, 2)
        flip_y = lax.rem(chip + 2, 4)
        diagonal = lax.rem(flip_x + 2, 4)
        seat = lambda c: 2 * c + core
        parts = (pl.ds(0, half), pl.ds(half, half))
        k = iter(range(16))

        def push(piece, source, target):
            i = next(k)
            where = o.at[:, source, parts[piece]]
            copy = remote(
                x.at[:, parts[piece]] if source is s else where,
                where,
                send.at[i],
                recv.at[i],
                seq=target,
            )
            copy.start()
            return copy

        to_x = [push(p, s, seat(flip_x)) for p in (0, 1)]
        to_y = [push(p, s, seat(flip_y)) for p in (1, 0)]
        near = [push(p, s, sibling) for p in (0, 1)]
        own = pltpu.make_async_copy(x, o.at[:, s], local)
        own.start()
        yield
        far = []
        to_x[0].wait_recv()
        far.append(push(0, seat(flip_x), seat(flip_y)))
        near.append(push(0, seat(flip_x), sibling))
        to_y[0].wait_recv()
        far.append(push(1, seat(flip_y), seat(flip_x)))
        near.append(push(1, seat(flip_y), sibling))
        to_x[1].wait_recv()
        near.append(push(1, seat(flip_x), sibling))
        to_y[1].wait_recv()
        near.append(push(0, seat(flip_y), sibling))
        far[0].wait_recv()
        near.append(push(0, seat(diagonal), sibling))
        far[1].wait_recv()
        near.append(push(1, seat(diagonal), sibling))
        yield
        own.wait()
        for copy in to_x + to_y + far:
            copy.wait_send()
        for copy in near:
            copy.wait()

    out = like(x, (x.shape[0], n) + x.shape[1:])
    return Task([x], [out], [DMA((16,)), DMA((16,)), DMA], body)


def sum_task(x):
    n = dims()[1]
    rows, _, frames, width = x.shape
    chips = n // 2
    step = 16

    def body(ins, outs, scratch, b, s, nb, n):
        mine, first, passed, second, total, send, recv, local, out_sem = scratch
        x, o = ins[0], outs[0]
        core = lax.rem(s, 2)
        sibling = s + 1 - 2 * core
        chip = s // 2
        order = [lax.rem(chip + d, chips) for d in list(range(1, chips)) + [0]]
        pair, own, far = [], [], []
        for k, c in enumerate(order):
            copy = remote(
                x.at[:, 2 * c + 1 - core], first.at[k], send.at[k], recv.at[k], seq=sibling
            )
            copy.start()
            pair.append(copy)
            copy = pltpu.make_async_copy(x.at[:, 2 * c + core], mine.at[k], local.at[k])
            copy.start()
            own.append(copy)
        yield
        for k in range(chips):
            pair[k].wait_recv()
            own[k].wait()
            if k < chips - 1:

                def add(i, carry, k=k):
                    at = pl.ds(pl.multiple_of(i * step, step), step)
                    for r in range(rows):
                        passed[k, r, at, :] = (
                            mine[k, r, at, :].astype(F32) + first[k, r, at, :].astype(F32)
                        ).astype(BF16)
                    return carry

                lax.fori_loop(0, frames // step, add, 0)
                copy = remote(
                    passed.at[k],
                    second.at[k],
                    send.at[chips + k],
                    recv.at[chips + k],
                    seq=2 * order[k] + core,
                )
                copy.start()
                far.append(copy)
        yield
        for copy in far:
            copy.wait_recv()

        def finish(i, carry):
            at = pl.ds(pl.multiple_of(i * step, step), step)
            for r in range(rows):
                value = mine[chips - 1, r, at, :].astype(F32) + first[chips - 1, r, at, :].astype(F32)
                for k in range(chips - 1):
                    value = value + second[k, r, at, :].astype(F32)
                total[r, at, :] = value
            return carry

        lax.fori_loop(0, frames // step, finish, 0)
        out = pltpu.make_async_copy(total, o, out_sem)
        out.start()
        for copy in pair + far:
            copy.wait_send()
        out.wait()

    slots = pltpu.VMEM((chips, rows, frames, width), BF16)
    fewer = pltpu.VMEM((chips - 1, rows, frames, width), BF16)
    return Task(
        [x],
        [like(x, (rows, frames, width), F32)],
        [
            slots,
            slots,
            fewer,
            fewer,
            pltpu.VMEM((rows, frames, width), F32),
            DMA((n,)),
            DMA((n,)),
            DMA((chips,)),
            DMA,
        ],
        body,
    )


def spread_task(x):
    nb, n = dims()
    chips = n // 2

    def body(ins, outs, scratch, b, s, nb, n):
        z_send, z_recv, p_send, p_recv, c_send, c_recv, local = scratch
        x, o = ins[0], outs[0]
        core = lax.rem(s, 2)
        sibling = s + 1 - 2 * core
        own = pltpu.make_async_copy(x, o.at[b, s], local)
        own.start()
        along = []
        for d in range(1, nb):
            copy = remote(
                x, o.at[b, s], z_send.at[d], z_recv.at[d], batch=lax.rem(b + d, nb), seq=s
            )
            copy.start()
            along.append(copy)
        far, near = [], []

        def onward(d):
            plane = lax.rem(b - d + nb, nb)
            source = x if d == 0 else o.at[plane, s]
            for c in range(1, chips):
                copy = remote(
                    source,
                    o.at[plane, s],
                    p_send.at[d, c],
                    p_recv.at[d, c],
                    seq=lax.rem(s + 2 * c, n),
                )
                copy.start()
                far.append((d, c, plane, copy))
            copy = remote(source, o.at[plane, s], c_send.at[d, 0], c_recv.at[d, 0], seq=sibling)
            copy.start()
            near.append(copy)

        onward(0)
        yield
        for d in range(1, nb):
            along[d - 1].wait_recv()
            onward(d)
        yield
        for d, c, plane, copy in far:
            copy.wait_recv()
            source = lax.rem(s - 2 * c + n, n)
            last = remote(
                o.at[plane, source],
                o.at[plane, source],
                c_send.at[d, c],
                c_recv.at[d, c],
                seq=sibling,
            )
            last.start()
            near.append(last)
        yield
        own.wait()
        for copy in along:
            copy.wait_send()
        for entry in far:
            entry[3].wait_send()
        for copy in near:
            copy.wait()

    square = DMA((nb, chips))
    return Task(
        [x],
        [like(x, (nb, n) + x.shape)],
        [DMA((nb,)), DMA((nb,)), square, square, square, square, DMA],
        body,
        True,
    )


def columns_out_task(x):
    nb, n = dims()
    ndev = nb * n
    kinds = x.shape[0]

    def body(ins, outs, scratch, b, s, nb, n):
        send, recv = scratch
        x, o = ins[0], outs[0]
        me = b * n + s
        pieces = []
        for j in range(kinds):
            piece = kinds * me + j
            column = lax.rem(piece, ndev)
            pieces.append((j, piece // ndev, column // nb, lax.rem(column, nb)))
        sent = []
        for j, part, block, slot in pieces:
            source, target, arrived = x.at[j], o.at[part, slot], recv.at[part, slot]
            for d in range(nb):
                plane = lax.rem(b + d, nb)
                owner = holder_of(plane, block, n, nb)
                if d == 0:

                    @pl.when(owner == s)
                    def _(source=source, target=target, arrived=arrived):
                        pltpu.make_async_copy(source, target, arrived).start()

                    @pl.when(owner != s)
                    def _(source=source, target=target, arrived=arrived, j=j, owner=owner):
                        remote(
                            source, target, send.at[j, 0], arrived, batch=b, seq=owner
                        ).start()
                else:
                    copy = remote(
                        source, target, send.at[j, d], arrived, batch=plane, seq=owner
                    )
                    copy.start()
                    sent.append(copy)
        yield
        yield
        yield
        for copy in sent:
            copy.wait_send()
        for j, part, block, slot in pieces:
            owner = holder_of(b, block, n, nb)

            @pl.when(owner != s)
            def _(j=j, part=part, slot=slot, owner=owner):
                remote(
                    x.at[j], o.at[part, slot], send.at[j, 0], recv.at[part, slot], batch=b, seq=owner
                ).wait_send()

        for p in range(kinds):
            for j in range(nb):
                pltpu.make_async_copy(x.at[0], o.at[p, j], recv.at[p, j]).wait()

    return Task(
        [x],
        [like(x, (kinds, nb) + x.shape[1:])],
        [DMA((kinds, nb)), DMA((kinds, nb))],
        body,
        True,
    )


def columns_back_task(x):
    nb, n = dims()
    ndev = nb * n
    kinds = x.shape[0]

    def body(ins, outs, scratch, b, s, nb, n):
        send, recv = scratch
        x, o = ins[0], outs[0]
        me = b * n + s
        pieces = []
        for p in range(kinds):
            for j in range(nb):
                column = p * ndev + block_of(b, s, n) * nb + j
                part = lax.rem(column, kinds)
                pieces.append(
                    (x.at[p, j], o.at[b, part], column // kinds, send.at[p, j], recv.at[b, part])
                )
        for source, target, owner, sent, arrived in pieces:

            @pl.when(owner == me)
            def _(source=source, target=target, arrived=arrived):
                pltpu.make_async_copy(source, target, arrived).start()

            @pl.when(owner != me)
            def _(source=source, target=target, owner=owner, sent=sent, arrived=arrived):
                remote(
                    source, target, sent, arrived, batch=owner // n, seq=lax.rem(owner, n)
                ).start()

        yield
        yield
        yield
        for source, target, owner, sent, arrived in pieces:

            @pl.when(owner != me)
            def _(source=source, target=target, owner=owner, sent=sent, arrived=arrived):
                remote(
                    source, target, sent, arrived, batch=owner // n, seq=lax.rem(owner, n)
                ).wait_send()

        for p in range(kinds):
            for j in range(nb):
                pltpu.make_async_copy(x.at[0, 0], o.at[j, p], recv.at[j, p]).wait()

    return Task(
        [x],
        [like(x, (nb, kinds) + x.shape[2:])],
        [DMA((kinds, nb)), DMA((nb, kinds))],
        body,
        True,
    )


def scatter_task(x):
    nb, n = dims()
    chips = n // 2

    def body(ins, outs, scratch, b, s, nb, n):
        mine, first, passed, second, total, send, recv, local, z_send, z_recv, z_local = scratch
        x, o = ins[0], outs[0]
        core = lax.rem(s, 2)
        sibling = s + 1 - 2 * core
        chip = s // 2
        order = [lax.rem(chip + d, chips) for d in list(range(1, chips)) + [0]]
        pair, own, far, last = [], [], [], []
        for k, c in enumerate(order):
            copy = remote(
                x.at[:, 2 * c + 1 - core], first.at[k], send.at[k], recv.at[k], seq=sibling
            )
            copy.start()
            pair.append(copy)
            copy = pltpu.make_async_copy(x.at[:, 2 * c + core], mine.at[k], local.at[k])
            copy.start()
            own.append(copy)
        yield
        for k in range(chips - 1):
            pair[k].wait_recv()
            own[k].wait()

            def add(i, carry, k=k):
                passed[k, i] = (mine[k, i].astype(F32) + first[k, i].astype(F32)).astype(BF16)
                return carry

            lax.fori_loop(0, nb, add, 0)
            copy = remote(
                passed.at[k],
                second.at[k],
                send.at[chips + k],
                recv.at[chips + k],
                seq=2 * order[k] + core,
            )
            copy.start()
            far.append(copy)
        yield
        pair[chips - 1].wait_recv()
        own[chips - 1].wait()
        for copy in far:
            copy.wait_recv()

        def finish(i, carry):
            value = mine[chips - 1, i].astype(F32) + first[chips - 1, i].astype(F32)
            for k in range(chips - 1):
                value = value + second[k, i].astype(F32)
            total[i] = value.astype(BF16)
            return carry

        lax.fori_loop(0, nb, finish, 0)
        for d in range(1, nb):
            plane = lax.rem(b + d, nb)
            copy = remote(
                total.at[plane], o.at[b], z_send.at[d], z_recv.at[d], batch=plane, seq=s
            )
            copy.start()
            last.append(copy)
        copy = pltpu.make_async_copy(total.at[b], o.at[b], z_local)
        copy.start()
        last.append(copy)
        yield
        for copy in pair + far:
            copy.wait_send()
        for copy in last:
            copy.wait()

    block = (nb,) + x.shape[2:]
    return Task(
        [x],
        [like(x, block)],
        [
            pltpu.VMEM((chips,) + block, BF16),
            pltpu.VMEM((chips,) + block, BF16),
            pltpu.VMEM((chips - 1,) + block, BF16),
            pltpu.VMEM((chips - 1,) + block, BF16),
            pltpu.VMEM(block, BF16),
            DMA((n,)),
            DMA((n,)),
            DMA((chips,)),
            DMA((nb,)),
            DMA((nb,)),
            DMA,
        ],
        body,
        True,
    )


def times(left, right):
    return lax.dot_general(left, right, (((1,), (0,)), ((), ())), preferred_element_type=F32)


def times_t(left, right):
    return lax.dot_general(left, right, (((1,), (1,)), ((), ())), preferred_element_type=F32)


def rows_sum(left, right):
    return lax.dot_general(left, right, (((0,), (0,)), ((), ())), preferred_element_type=F32)


def mish_parts(v):
    e = jnp.exp(jnp.minimum(v, 20.0))
    n = e * (e + 2.0)
    inverse = 1.0 / (n + 2.0)
    return e, n, inverse


def mish(v):
    e, n, inverse = mish_parts(v)
    return v * (n * inverse)


def mish_slope(v):
    e, n, inverse = mish_parts(v)
    return n * inverse + v * (4.0 * e * (1.0 + e)) * inverse * inverse


CHUNK = 128


def interleave(even, odd):
    low = lax.broadcasted_iota(jnp.int32, even.shape, 1) < CHAN
    return (
        jnp.where(low, even, pltpu.roll(odd, CHAN, 1)),
        jnp.where(low, pltpu.roll(even, CHAN, 1), odd),
    )


def to_groups(even, odd):
    if even.shape[1] == CHAN:
        return (jnp.concatenate([even, odd], axis=1),)
    return interleave(even, odd)


def to_pair(blocks):
    if len(blocks) == 1:
        return blocks[0][:, :CHAN], blocks[0][:, CHAN:]
    return interleave(*blocks)


def place(buf, source, seg, length):
    rows = buf.shape[0]

    def clear(i, carry):
        buf[pl.ds(pl.multiple_of(i * 16, 16), 16), :] = jnp.zeros((16, buf.shape[1]), F32)
        return carry

    lax.fori_loop(0, rows // 16, clear, 0)

    def move(i, carry):
        at = pl.multiple_of(i * CHUNK, CHUNK)
        value = source(at)
        ids = seg[0, pl.ds(at, CHUNK), :] & 7
        for u in range(SEGS):
            to = pl.ds(at + GAP * (u + 1), CHUNK)
            buf[to, :] = buf[to, :] + jnp.where(ids == u, value, 0.0)
        return carry

    lax.fori_loop(0, length // CHUNK, move, 0)


def unplace(buf, sink, seg, length):
    def move(i, carry):
        at = pl.multiple_of(i * CHUNK, CHUNK)
        ids = seg[0, pl.ds(at, CHUNK), :] & 7
        value = buf[pl.ds(at + GAP, CHUNK), :]
        for u in range(1, SEGS):
            value = jnp.where(ids == u, buf[pl.ds(at + GAP * (u + 1), CHUNK), :], value)
        sink[0, pl.ds(at, CHUNK), :] = value.astype(sink.dtype)
        return carry

    lax.fori_loop(0, length // CHUNK, move, 0)


def folded(buf, count, first):
    return buf[pl.ds(first, count, stride=FOLD), :]


def spread_taps(x, buf, count):
    for t in range(TAPS // 2):
        blocks = to_groups(folded(buf, count, 2 * t + 1), folded(buf, count, 2 * t + 2))
        for g, block in enumerate(blocks):
            x[g, :, 2 * CHAN * t : 2 * CHAN * (t + 1)] = block.astype(BF16)


def write_folded(buf, count, groups, value, live=None):
    for w in range(FOLD // 2):
        lanes = slice(2 * CHAN * w, 2 * CHAN * (w + 1))
        for half, part in enumerate(to_pair([value(g, lanes) for g in range(groups)])):
            at = pl.ds(GAP + 2 * w + half, count, stride=FOLD)
            buf[at, :] = part if live is None else part * live[at, :]


def fill_bands(bands, taps, groups, back):
    low = lax.broadcasted_iota(jnp.int32, (CHAN, 2 * CHAN), 1) < CHAN
    zero = jnp.zeros((CHAN, 2 * CHAN), F32)
    width = groups * CHAN

    def forms(k):
        if not 0 <= k < KERNEL:
            return None
        full = taps[:, KERNEL - 1 - k if back else k].astype(F32).reshape(width, 2 * CHAN)
        if back:
            full = full.T
            if groups == 1:
                full = jnp.concatenate([full, full], axis=1)
        turned = pltpu.roll(full, CHAN, 1)
        result = {}
        for c in range(2):
            for g in range(groups):
                if back:
                    rows, own = slice(c * CHAN, (c + 1) * CHAN), g
                else:
                    rows, own = slice(g * CHAN, (g + 1) * CHAN), c
                pair = (full[rows], turned[rows])
                result[c, g] = pair if own == 0 else pair[::-1]
        return result

    known = {}
    for tap in range(TAPS):
        known[tap] = forms(tap)
        known.pop(tap - FOLD, None)
        for w in range(FOLD // 2):
            left, right = known.get(tap - 2 * w), known.get(tap - 2 * w - 1)
            for c in range(2):
                for g in range(groups):
                    a = zero if left is None else left[c, g][0]
                    b = zero if right is None else right[c, g][1]
                    bands[
                        c, g, tap * CHAN : (tap + 1) * CHAN, 2 * CHAN * w : 2 * CHAN * (w + 1)
                    ] = jnp.where(low, a, b).astype(BF16)


FOLDED = FOLD * CHAN
DEPTH = TAPS * CHAN


def conv_forward_kernel(count, length, groups, u, seg, taps, c1, c2, out, buf, live, x, bands):
    @pl.when(pl.program_id(0) == 0)
    def _():
        fill_bands(bands, taps, groups, False)

    width = groups * CHAN
    place(live, lambda at: jnp.ones((CHUNK, width), F32), seg, length)
    place(buf, lambda at: u[0, pl.ds(at, CHUNK), :].astype(F32), seg, length)
    spread_taps(x, buf, count)
    for g in range(groups):
        c1[0, g] = times(x[g], bands[0, g])
    write_folded(buf, count, groups, lambda g, lanes: mish(c1[0, g, :, lanes]), live)
    spread_taps(x, buf, count)
    for g in range(groups):
        c2[0, g] = times(x[g], bands[1, g])
    write_folded(buf, count, groups, lambda g, lanes: mish(c2[0, g, :, lanes]))
    unplace(buf, out, seg, length)


def conv_sizes(length):
    count = -(-(length + GAP * (SEGS - 1)) // FOLD)
    count = -(-count // 16) * 16
    return count, FOLD * count + 48


def whole(shape):
    zeros = (0,) * len(shape)
    return pl.BlockSpec(shape, lambda *i: zeros)


def by_row(shape):
    return pl.BlockSpec((1,) + tuple(shape[1:]), lambda r: (r,) + (0,) * (len(shape) - 1))


def conv_forward(u, seg, taps):
    rows, length, width = u.shape
    groups = width // CHAN
    count, buffer = conv_sizes(length)
    kept = (rows, groups, count, FOLDED)
    return pl.pallas_call(
        functools.partial(conv_forward_kernel, count, length, groups),
        grid=(rows,),
        in_specs=[by_row(u.shape), by_row(seg.shape), whole(taps.shape)],
        out_specs=[by_row(kept), by_row(kept), by_row(u.shape)],
        out_shape=[
            jax.ShapeDtypeStruct(kept, F32),
            jax.ShapeDtypeStruct(kept, F32),
            jax.ShapeDtypeStruct(u.shape, BF16),
        ],
        scratch_shapes=[
            pltpu.VMEM((buffer, width), F32),
            pltpu.VMEM((buffer, width), F32),
            pltpu.VMEM((groups, count, DEPTH), BF16),
            pltpu.VMEM((2, groups, DEPTH, FOLDED), BF16),
        ],
        compiler_params=params(),
    )(u, seg, taps)


def weight_sums(even, odd, c, turned, x, groups):
    rows = slice(c * CHAN, (c + 1) * CHAN)
    blocks = TAPS // 2
    pair = 2 * CHAN
    for g in range(groups):
        for start in range(0, blocks, 2):
            stop = min(start + 2, blocks)
            product = times(turned[g], x[g, :, start * pair : stop * pair])
            for t in range(start, stop):
                part = product[:, (t - start) * pair : (t - start + 1) * pair]
                for m in range(FOLD):
                    to = t - m // 2
                    if 0 <= to < 16:
                        sums = odd if m % 2 else even
                        sums[g, to, rows] = sums[g, to, rows] + part[m * CHAN : (m + 1) * CHAN]


def conv_backward_kernel(
    count, length, groups, nb, d, u, seg, c1, c2, taps, dh, pieces, buf, grads, live, x, turned, bands, even, odd
):
    width = groups * CHAN
    row = pl.program_id(0)

    @pl.when(row == 0)
    def _():
        fill_bands(bands, taps, groups, True)
        even[...] = jnp.zeros_like(even)
        odd[...] = jnp.zeros_like(odd)

    place(live, lambda at: jnp.ones((CHUNK, width), F32), seg, length)
    place(grads, lambda at: d[0, pl.ds(at, CHUNK), :].astype(F32), seg, length)

    def slope(kept, scaled):
        values = {}
        for w in range(FOLD // 2):
            lanes = slice(2 * CHAN * w, 2 * CHAN * (w + 1))
            for g in range(groups):
                value = scaled(g, w, lanes) * mish_slope(kept[0, g, :, lanes])
                values[g, w] = value
                turned[g, lanes, :] = value.T.astype(BF16)
        return values

    def loaded(g, w, lanes):
        return to_groups(
            folded(grads, count, GAP + 2 * w), folded(grads, count, GAP + 2 * w + 1)
        )[g]

    values = slope(c2, loaded)
    write_folded(grads, count, groups, lambda g, lanes: values[g, lanes.start // (2 * CHAN)])
    for i in range(0, GAP, 8):
        buf[i : i + 8, :] = jnp.zeros((8, width), F32)
    for i in range(GAP + FOLD * count, buf.shape[0], 8):
        buf[i : i + 8, :] = jnp.zeros((8, width), F32)
    write_folded(buf, count, groups, lambda g, lanes: mish(c1[0, g, :, lanes]), live)
    spread_taps(x, buf, count)
    weight_sums(even, odd, 1, turned, x, groups)
    spread_taps(x, grads, count)
    back = [times(x[g], bands[1, g]) for g in range(groups)]

    def masked(g, w, lanes):
        alive = to_groups(
            folded(live, count, GAP + 2 * w), folded(live, count, GAP + 2 * w + 1)
        )[g]
        return back[g][:, lanes] * alive

    values = slope(c1, masked)
    write_folded(grads, count, groups, lambda g, lanes: values[g, lanes.start // (2 * CHAN)])
    place(buf, lambda at: u[0, pl.ds(at, CHUNK), :].astype(F32), seg, length)
    spread_taps(x, buf, count)
    weight_sums(even, odd, 0, turned, x, groups)
    spread_taps(x, grads, count)
    last = [times(x[g], bands[0, g]) for g in range(groups)]
    write_folded(buf, count, groups, lambda g, lanes: last[g][:, lanes])
    unplace(buf, dh, seg, length)

    @pl.when(row == pl.num_programs(0) - 1)
    def _():
        low = lax.broadcasted_iota(jnp.int32, (2 * CHAN, 2 * CHAN), 1) < CHAN
        part = width // nb
        each = CHAN // part
        for g in range(groups):
            for p in range(16):
                left = pltpu.roll(odd[g, p], CHAN, 1)
                right = pltpu.roll(odd[g, p + 1], CHAN, 1) if p < 15 else left
                total = (even[g, p] + jnp.where(low, left, right)).T.astype(BF16)
                for half in range(2):
                    k = 2 * p + half
                    if k < KERNEL:
                        for j in range(each):
                            first = half * CHAN + j * part
                            pieces[0, g * each + j, k] = total[first : first + part]


def conv_backward(d, u, seg, c1, c2, taps, nb):
    rows, length, width = u.shape
    groups = width // CHAN
    count, buffer = conv_sizes(length)
    pieces = (1, nb, KERNEL, width // nb, 2 * CHAN)
    sums = pltpu.VMEM((groups, 16, 2 * CHAN, 2 * CHAN), F32)
    frames = pltpu.VMEM((buffer, width), F32)
    return pl.pallas_call(
        functools.partial(conv_backward_kernel, count, length, groups, nb),
        grid=(rows,),
        in_specs=[
            by_row(d.shape),
            by_row(u.shape),
            by_row(seg.shape),
            by_row(c1.shape),
            by_row(c2.shape),
            whole(taps.shape),
        ],
        out_specs=[by_row(u.shape), whole(pieces)],
        out_shape=[
            jax.ShapeDtypeStruct(u.shape, BF16),
            jax.ShapeDtypeStruct(pieces, BF16),
        ],
        scratch_shapes=[
            frames,
            frames,
            frames,
            pltpu.VMEM((groups, count, DEPTH), BF16),
            pltpu.VMEM((groups, FOLDED, count), BF16),
            pltpu.VMEM((2, groups, DEPTH, FOLDED), BF16),
            sums,
            sums,
        ],
        compiler_params=params(),
    )(d, u, seg, c1, c2, taps)


def pair_swap(x):
    width = x.shape[1]
    if width % 128:
        x = jnp.concatenate([x, x], axis=1)
    lane = lax.broadcasted_iota(jnp.int32, x.shape, 1)
    after = pltpu.roll(x, x.shape[1] - 1, 1)
    before = pltpu.roll(x, 1, 1)
    return jnp.where(lax.rem(lane, 2) == 0, -after, before)[:, :width]


def qkv_kernel(width, x, w, cos, sin, q, k, v):
    got = lax.dot_general(
        x[0], w[...], (((1,), (1,)), ((), ())), preferred_element_type=F32
    )
    for p, out in enumerate((q, k)):
        part = got[:, p * width : (p + 1) * width]
        out[0] = (part * cos[0] + pair_swap(part) * sin[0]).astype(BF16)
    v[0] = got[:, 2 * width :].astype(BF16)


def qkv_forward(x, w, cos, sin):
    rows, length, depth = x.shape
    width = w.shape[0] // 3
    block = 512
    spec = pl.BlockSpec((1, block, width), lambda r, i: (r, i, 0))
    shape = jax.ShapeDtypeStruct((rows, length, width), BF16)
    return pl.pallas_call(
        functools.partial(qkv_kernel, width),
        grid=(rows, length // block),
        in_specs=[
            pl.BlockSpec((1, block, depth), lambda r, i: (r, i, 0)),
            whole(w.shape),
            spec,
            spec,
        ],
        out_specs=[spec] * 3,
        out_shape=[shape] * 3,
        compiler_params=params(),
    )(x, w, cos, sin)


def attention_forward_kernel(width, q, k, v, q_code, k_code, out, low, log_sum):
    heads = width // HEAD
    lane = lax.broadcasted_iota(jnp.int32, q.shape[1:], 1) // HEAD
    allowed = (q_code[0] & 7) == k_code[0]
    queries = q[0] * 0.125
    result, logs = None, None
    for h in range(heads):
        chosen = jnp.where(lane == h, queries, jnp.zeros_like(queries))
        scores = lax.dot_general(
            chosen, k[0], (((1,), (1,)), ((), ())), preferred_element_type=F32
        )
        scores = jnp.where(allowed, scores, MASKED)
        peak = jnp.max(scores, axis=1, keepdims=True)
        weights = jnp.exp(scores - peak)
        total = jnp.sum(weights, axis=1, keepdims=True)
        value = jnp.dot(weights.astype(BF16), v[0], preferred_element_type=F32) / total
        log = jnp.broadcast_to(peak + jnp.log(total), value.shape)
        result = value if h == 0 else jnp.where(lane == h, value, result)
        logs = log if h == 0 else jnp.where(lane == h, log, logs)
    out[0] = result
    low[0] = result.astype(BF16)
    log_sum[0] = logs


def attention_forward(q, k, v, q_code, k_code):
    rows, length, width = q.shape
    block = 256
    spec = pl.BlockSpec((1, block, width), lambda r, i: (r, i, 0))
    row = pl.BlockSpec((1, length, width), lambda r, i: (r, 0, 0))
    return pl.pallas_call(
        functools.partial(attention_forward_kernel, width),
        grid=(rows, length // block),
        in_specs=[
            spec,
            row,
            row,
            pl.BlockSpec((1, block, 1), lambda r, i: (r, i, 0)),
            pl.BlockSpec((1, 1, length), lambda r, i: (r, 0, 0)),
        ],
        out_specs=[spec] * 3,
        out_shape=[
            jax.ShapeDtypeStruct(q.shape, F32),
            jax.ShapeDtypeStruct(q.shape, BF16),
            jax.ShapeDtypeStruct(q.shape, F32),
        ],
        compiler_params=params(),
    )(q, k, v, q_code, k_code)


BLOCK = 256


def attention_backward_kernel(
    length, width, low_edge, high_edge, q, k, v, g, log_sum, delta, k_code, q_code, cos, sin, out, dq, dk, dv
):
    heads = width // HEAD
    row = pl.program_id(0)
    lane = lax.broadcasted_iota(jnp.int32, (BLOCK, width), 1) // HEAD
    dk[...] = jnp.zeros_like(dk)
    dv[...] = jnp.zeros_like(dv)

    def outer(i, carry):
        at = pl.ds(pl.multiple_of(i * BLOCK, BLOCK), BLOCK)
        queries = q[0, at, :] * 0.125
        grads = g[0, at, :]
        zero = jnp.zeros_like(queries)
        queries_of = [jnp.where(lane == h, queries, zero) for h in range(heads)]
        grads_of = [jnp.where(lane == h, grads, zero) for h in range(heads)]
        dq[...] = jnp.zeros_like(dq)

        def inner(j, carry):
            to = pl.ds(pl.multiple_of(j * BLOCK, BLOCK), BLOCK)
            keys, values = k[0, to, :], v[0, to, :]
            allowed = k_code[0, to, :] == q_code[0, :, at]
            dk_part, dv_part, dq_part = None, None, None
            for h in range(heads):
                keys_of = jnp.where(lane == h, keys, zero)
                scores = lax.dot_general(
                    keys, queries_of[h], (((1,), (1,)), ((), ())), preferred_element_type=F32
                )
                probs = jnp.where(allowed, jnp.exp(scores - log_sum[0, h : h + 1, at]), 0.0)
                grad_probs = lax.dot_general(
                    values, grads_of[h], (((1,), (1,)), ((), ())), preferred_element_type=F32
                )
                grad_scores = (probs * (grad_probs - delta[0, h : h + 1, at])).astype(BF16)
                a = jnp.dot(probs.astype(BF16), grads_of[h], preferred_element_type=F32)
                c = jnp.dot(grad_scores, queries_of[h], preferred_element_type=F32)
                e = lax.dot_general(
                    grad_scores, keys_of, (((0,), (0,)), ((), ())), preferred_element_type=F32
                )
                dv_part = a if h == 0 else dv_part + a
                dk_part = c if h == 0 else dk_part + c
                dq_part = e if h == 0 else dq_part + e
            dv[to, :] = dv[to, :] + dv_part
            dk[to, :] = dk[to, :] + dk_part
            dq[...] = dq[...] + dq_part
            return carry

        lax.fori_loop(low_edge[row, i], high_edge[row, i], inner, 0)
        grad = dq[...] * 0.125
        turned = grad * cos[0, at, :] - pair_swap(grad) * sin[0, at, :]
        out[0, at, 0:width] = turned.astype(BF16)
        return carry

    lax.fori_loop(0, length // BLOCK, outer, 0)

    def finish(i, carry):
        at = pl.ds(pl.multiple_of(i * BLOCK, BLOCK), BLOCK)
        grad = dk[at, :]
        turned = grad * cos[0, at, :] - pair_swap(grad) * sin[0, at, :]
        out[0, at, width : 2 * width] = turned.astype(BF16)
        out[0, at, 2 * width : 3 * width] = dv[at, :].astype(BF16)
        return carry

    lax.fori_loop(0, length // BLOCK, finish, 0)


def attention_backward(q, k, v, g, log_sum, delta, k_code, q_code, cos, sin, low_edge, high_edge):
    rows, length, width = q.shape

    def spec(shape):
        return pl.BlockSpec((1,) + tuple(shape[1:]), lambda r, *_: (r,) + (0,) * (len(shape) - 1))

    arrays = (q, k, v, g, log_sum, delta, k_code, q_code, cos, sin)
    out = (rows, length, 3 * width)
    return pl.pallas_call(
        functools.partial(attention_backward_kernel, length, width),
        grid_spec=pltpu.PrefetchScalarGridSpec(
            num_scalar_prefetch=2,
            grid=(rows,),
            in_specs=[spec(a.shape) for a in arrays],
            out_specs=spec(out),
            scratch_shapes=[
                pltpu.VMEM((BLOCK, width), F32),
                pltpu.VMEM((length, width), F32),
                pltpu.VMEM((length, width), F32),
            ],
        ),
        out_shape=jax.ShapeDtypeStruct(out, BF16),
        compiler_params=params(),
    )(low_edge, high_edge, *arrays)


def pick(ids, table, rows):
    value = table[SEGS - 1 : SEGS, :]
    for u in range(SEGS - 2, -1, -1):
        value = jnp.where(ids == u, table[u : u + 1, :], value)
    return jnp.broadcast_to(value, (rows, table.shape[1]))


def gelu_parts(v):
    c = 0.7978845608
    t = jnp.tanh(c * (v + 0.044715 * v * v * v))
    half = 0.5 * (1.0 + t)
    return v * half, half + 0.5 * v * (1.0 - t * t) * c * (1.0 + 0.134145 * v * v)


STEP = 32


def feed_kernel(
    rows,
    frames,
    part,
    att,
    embedded,
    late,
    ids,
    mod,
    cotangent,
    block_out,
    grad_att,
    late_grads,
    grad_middle,
    sums,
    branch,
    middle,
    scale,
    normed,
    bend,
    low,
    grad_up,
    feed,
    grad_feed,
    grad_normed,
    grad_branch,
):
    tokens = rows * frames
    wide = 256
    per = wide // part

    def each_step(body):
        for r in range(rows):

            def step(i, carry, r=r):
                at = pl.ds(pl.multiple_of(r * frames + i * STEP, STEP), STEP)
                body(r, at)
                return carry

            lax.fori_loop(0, frames // STEP, step, 0)

    def gate(r, at, which):
        return pick(ids[at, :], mod[r, which], STEP)

    def columns(first, count, j):
        n = wide // count
        return late[j * n : (j + 1) * n, first : first + count, :].reshape(wide, D)

    for j in range(D // wide):
        branch[:, j * wide : (j + 1) * wide] = times_t(att[...], columns(0, part, j))

    def to_normed(r, at):
        value = embedded[at, :] + gate(r, at, 2) * branch[at, :]
        middle[at, :] = value
        centre = value - jnp.mean(value, axis=1, keepdims=True)
        factor = lax.rsqrt(jnp.mean(centre * centre, axis=1, keepdims=True) + EPSILON)
        hat = centre * factor
        scale[at, :] = jnp.broadcast_to(factor, (STEP, 128))
        normed[at, :] = (hat * (1.0 + gate(r, at, 4)) + gate(r, at, 3)).astype(BF16)

    each_step(to_normed)
    for j in range(2 * D // wide):
        lanes = slice(j * wide, (j + 1) * wide)
        value, slope = gelu_parts(times_t(normed[...], columns(part, 2 * part, j)))
        low[:, lanes] = value.astype(BF16)
        bend[:, lanes] = slope
    for j in range(D // wide):
        feed[:, j * wide : (j + 1) * wide] = times_t(
            low[:, :D], columns(3 * part, part, j)
        ) + times_t(low[:, D:], columns(4 * part, part, j))

    def to_out(r, at):
        gate_feed = gate(r, at, 5)
        block_out[at, :] = (middle[at, :] + gate_feed * feed[at, :]).astype(BF16)
        grad_feed[at, :] = (gate_feed * cotangent[at, :].astype(F32)).astype(BF16)

    each_step(to_out)

    def inner(first, count, lanes):
        return late[:, first : first + count, lanes].reshape(-1, wide)

    for half in range(2):
        for j in range(D // wide):
            lanes = slice(half * D + j * wide, half * D + (j + 1) * wide)
            weights = inner((3 + half) * part, part, slice(j * wide, (j + 1) * wide))
            grad_up[:, lanes] = (times(grad_feed[...], weights) * bend[:, lanes]).astype(BF16)
    for j in range(D // wide):
        lanes = slice(j * wide, (j + 1) * wide)
        grad_normed[:, lanes] = times(grad_up[...], inner(part, 2 * part, lanes))

    sums[...] = jnp.zeros_like(sums)

    def back(r, at):
        value = middle[at, :]
        factor = scale[at, 0:1]
        hat = (value - jnp.mean(value, axis=1, keepdims=True)) * factor
        grad = grad_normed[at, :]
        e = grad * (1.0 + gate(r, at, 4))
        out = cotangent[at, :].astype(F32)
        total = out + factor * (
            e
            - jnp.mean(e, axis=1, keepdims=True)
            - hat * jnp.mean(e * hat, axis=1, keepdims=True)
        )
        grad_middle[at, :] = total
        grad_branch[at, :] = (gate(r, at, 2) * total).astype(BF16)
        first = ids[at, :] == ids[r * frames : r * frames + 1, :]
        for k, part_sum in enumerate(
            (total * branch[at, :], grad, grad * hat, out * feed[at, :])
        ):
            kept = jnp.where(first, part_sum, 0.0)
            other = part_sum - kept
            for side, piece in enumerate((kept, other)):
                folded = piece[0:8]
                for q in range(1, STEP // 8):
                    folded = folded + piece[8 * q : 8 * q + 8]
                sums[r, side, k] = sums[r, side, k] + folded

    each_step(back)
    for j in range(D // wide):
        lanes = slice(j * wide, (j + 1) * wide)
        grad_att[:, lanes] = times(grad_branch[...], inner(0, part, lanes)).astype(BF16)
        late_grads[j * per : (j + 1) * per, 0:part, :] = (
            rows_sum(grad_branch[:, lanes], att[...]).astype(BF16).reshape(per, part, D)
        )
        for half in range(2):
            late_grads[j * per : (j + 1) * per, (3 + half) * part : (4 + half) * part, :] = (
                rows_sum(grad_feed[:, lanes], low[:, half * D : (half + 1) * D])
                .astype(BF16)
                .reshape(per, part, D)
            )
    for j in range(2 * D // wide):
        lanes = slice(j * wide, (j + 1) * wide)
        late_grads[j * per // 2 : (j + 1) * per // 2, part : 3 * part, :] = (
            rows_sum(grad_up[:, lanes], normed[...]).astype(BF16).reshape(per // 2, 2 * part, D)
        )


def feed_both(att, embedded, late, ids, mod, cotangent, rows, frames, part):
    tokens = rows * frames
    vmem = pl.BlockSpec(memory_space=pltpu.VMEM)

    def scratch(width, dtype):
        return pltpu.VMEM((tokens, width), dtype)

    return pl.pallas_call(
        functools.partial(feed_kernel, rows, frames, part),
        in_specs=[vmem] * 6,
        out_specs=[vmem] * 5,
        out_shape=[
            jax.ShapeDtypeStruct((tokens, D), BF16),
            jax.ShapeDtypeStruct((tokens, D), BF16),
            jax.ShapeDtypeStruct(late.shape, BF16),
            jax.ShapeDtypeStruct((tokens, D), F32),
            jax.ShapeDtypeStruct((rows, 2, 4, 8, D), F32),
        ],
        scratch_shapes=[
            scratch(D, F32),
            scratch(D, F32),
            scratch(128, F32),
            scratch(D, BF16),
            scratch(2 * D, F32),
            scratch(2 * D, BF16),
            scratch(2 * D, BF16),
            scratch(D, F32),
            scratch(D, BF16),
            scratch(D, F32),
            scratch(D, BF16),
        ],
        compiler_params=params(),
    )(att, embedded, late, ids, mod, cotangent)


def layer_norm(field):
    centre = field - jnp.mean(field, axis=-1, keepdims=True)
    return centre * lax.rsqrt(jnp.mean(centre * centre, axis=-1, keepdims=True) + EPSILON)


def modulate(field, scaling, shifting):
    return layer_norm(field) * (1.0 + scaling) + shifting


def gelu_curve(inputs):
    return jax.nn.gelu(inputs, approximate=True)


def by_segment(ids, table):
    value = table[:, SEGS - 1][:, None, :]
    for u in range(SEGS - 2, -1, -1):
        value = jnp.where(ids[:, :, None] == u, table[:, u][:, None, :], value)
    return value


def rope_tables(segment_ids, starts, width):
    length = segment_ids.shape[1]
    pairs = (np.arange(width) % HEAD) // 2
    freq = 10000.0 ** (-2.0 * pairs / HEAD)
    angle = np.arange(length)[:, None] * freq[None, :]
    cos_t = jnp.asarray(np.cos(angle).astype(np.float32))[None]
    sin_t = jnp.asarray(np.sin(angle).astype(np.float32))[None]
    offset = starts.astype(F32)[:, :, None] * jnp.asarray(freq.astype(np.float32))
    cos_o = by_segment(segment_ids, jnp.cos(offset))
    sin_o = by_segment(segment_ids, jnp.sin(offset))
    return cos_t * cos_o + sin_t * sin_o, sin_t * cos_o - cos_t * sin_o


def on_device(
    mel_inputs,
    text_ids,
    segment_ids,
    key_mask,
    time_index,
    input_proj,
    conv_first,
    conv_second,
    time_table,
    adaln_proj,
    qkv_proj,
    out_proj,
    up_proj,
    down_proj,
    text_table,
    grad_out,
):
    nb, n = dims()
    ndev = nb * n
    rows, frames = mel_inputs.shape[:2]
    tokens = rows * frames
    length = frames * n
    width = D // n
    part = D // ndev
    mine = lax.axis_index("seq")
    first_frame = mine * frames

    out_t, up_t, down_t = out_proj.T, up_proj.T, down_proj.T
    wide_t = jnp.concatenate([out_t, up_t, down_t[:, :D], down_t[:, D:]], axis=0)
    per = wide_t.shape[0]
    (
        (full_in,),
        (full_text,),
        (full_time,),
        (all_index,),
        (got_convs,),
    ) = transfer(
        [
            spread_task(input_proj.T),
            spread_task(text_table.T),
            spread_task(time_table.T),
            spread_task(time_index),
            columns_out_task(jnp.concatenate([conv_first, conv_second], axis=2)[None]),
        ],
        0,
    )
    got_convs = got_convs[0]
    wide_t, _ = lax.optimization_barrier((wide_t, all_index))
    late = lax.all_gather(wide_t, ("batch", "seq"), axis=0, tiled=True).reshape(ndev, per, D)
    in_t = full_in.reshape(D, input_proj.shape[0])
    text_t = full_text.reshape(-1, VOCAB)
    time_t = full_time.reshape(D, STEPS)
    slot_steps = all_index[:, 0].reshape(nb * rows * SEGS)

    own_ids = lax.dynamic_slice_in_dim(segment_ids, first_frame, frames, 1)
    key_code = segment_ids + jnp.where(key_mask > 0, 0, 8)
    seg_column = key_code[:, :, None]
    seg_index = jnp.arange(SEGS, dtype=jnp.int32)
    starts = jnp.sum((segment_ids[:, None, :] < seg_index[None, :, None]).astype(jnp.int32), axis=2)

    text_hot = (
        text_ids.reshape(-1)[:, None] == jnp.arange(VOCAB, dtype=jnp.int32)[None, :]
    ).astype(BF16)
    text_embed = times_t(text_hot, text_t).astype(BF16)
    joined = jnp.concatenate([mel_inputs.reshape(tokens, 2 * MEL), text_embed], axis=1)
    hidden = times_t(joined, in_t).reshape(rows, frames, D)

    step_hot = (
        slot_steps[:, None] == jnp.arange(STEPS, dtype=jnp.int32)[None, :]
    ).astype(BF16)
    cond_value = times_t(step_hot, time_t)
    soft_cond = jax.nn.silu(cond_value).astype(BF16)
    own_mod = times(soft_cond, adaln_proj)
    task, arrange = to_channels(hidden.astype(BF16))
    got, (mod_got,) = transfer(
        [task, spray_task(own_mod.reshape(nb, rows * SEGS, 6 * part), True)], 2
    )
    hidden_c = arrange(got)
    modulation = mod_got.transpose(1, 0, 2).reshape(rows, SEGS, 6, D)
    shift_attn, scale_attn = (by_segment(own_ids, modulation[:, :, i]) for i in range(2))

    conv_one, conv_two, bump_c = conv_forward(hidden_c, seg_column, got_convs)
    task, arrange = to_frames(bump_c)
    bump = arrange(transfer([task], 3)[0])
    embedded = hidden + bump.astype(F32)

    normed = modulate(embedded, scale_attn, shift_attn).astype(BF16)
    gather = quad_gather_task if n == 8 else gather_task
    (normed_all,), (got_qkv,) = transfer(
        [gather(normed), columns_out_task(qkv_proj.T.reshape(3, part, D))], 4
    )
    normed_all = normed_all.reshape(rows, length, D)
    qkv_t = got_qkv.reshape(3 * width, D)
    cos, sin = rope_tables(segment_ids, starts, width)
    query, key, value = qkv_forward(normed_all, qkv_t, cos, sin)
    attended, attended_low, log_lanes = attention_forward(
        query, key, value, seg_column, key_code[:, None, :]
    )
    task, arrange = to_frames(attended_low)
    attended_own = arrange(transfer([task], 5)[0])
    attended_own = attended_own.reshape(tokens, D)

    block_out, grad_att, late_grads, grad_middle, feed_sums = feed_both(
        attended_own,
        embedded.reshape(tokens, D),
        late,
        own_ids.reshape(tokens, 1),
        modulation.transpose(0, 2, 1, 3),
        grad_out.reshape(tokens, D),
        rows,
        frames,
        part,
    )
    block_out = block_out.reshape(rows, frames, D)
    grad_att = grad_att.reshape(rows, frames, D)
    grad_middle = grad_middle.reshape(rows, frames, D)
    task, arrange = to_channels(grad_att)
    grad_att_c = arrange(transfer([task], 6)[0])
    heads = width // HEAD
    delta = jnp.sum(
        (grad_att_c.astype(F32) * attended).reshape(rows, length, heads, HEAD), axis=3
    ).transpose(0, 2, 1)
    log_rows = log_lanes.reshape(rows, length, heads, HEAD)[:, :, :, 0].transpose(0, 2, 1)
    block_first_ids = segment_ids[:, ::BLOCK]
    block_last_ids = segment_ids[:, BLOCK - 1 :: BLOCK]
    ends = jnp.sum((segment_ids[:, None, :] <= seg_index[None, :, None]).astype(jnp.int32), axis=2)
    low_edge = (
        jnp.sum(jnp.where(block_first_ids[:, :, None] == seg_index, starts[:, None, :], 0), axis=2)
        // BLOCK
    )
    high_edge = (
        jnp.sum(jnp.where(block_last_ids[:, :, None] == seg_index, ends[:, None, :], 0), axis=2)
        + BLOCK
        - 1
    ) // BLOCK
    grad_projected = attention_backward(
        query,
        key,
        value,
        grad_att_c,
        log_rows,
        delta,
        seg_column,
        segment_ids[:, None, :],
        cos,
        sin,
        low_edge,
        high_edge,
    ).reshape(rows * length, 3 * width)
    grad_qkv = rows_sum(grad_projected, normed_all.reshape(rows * length, D)).astype(BF16)
    partial = times(grad_projected, qkv_t).astype(BF16).reshape(rows, n, frames, D)
    (grad_normed,), (got_qkv_grads,) = transfer(
        [sum_task(partial), columns_back_task(grad_qkv.reshape(3, nb, part, D))], 7
    )
    late_grads, grad_normed = lax.optimization_barrier((late_grads, grad_normed))
    late_sum = lax.psum_scatter(
        late_grads, ("batch", "seq"), scatter_dimension=0, tiled=False
    ).astype(F32)

    grad_emb_part, grad_scale_attn, grad_shift_attn = jax.vjp(
        modulate, embedded, scale_attn, shift_attn
    )[1](grad_normed)
    grad_embedded = grad_middle + grad_emb_part

    first_ids, last_ids = own_ids[:, 0], own_ids[:, -1]
    first = (own_ids == first_ids[:, None])[:, :, None]
    attn_sums = [
        jnp.stack([jnp.sum(jnp.where(first, g, 0.0), axis=1), jnp.sum(jnp.where(first, 0.0, g), axis=1)], axis=1)
        for g in (grad_shift_attn, grad_scale_attn)
    ]
    feed_sums = jnp.sum(feed_sums, axis=3)
    sides = jnp.concatenate(
        [attn_sums[0], attn_sums[1]] + [feed_sums[:, :, i] for i in range(4)], axis=2
    )
    is_first = (first_ids[:, None] == seg_index).astype(F32)
    is_last = (last_ids[:, None] == seg_index).astype(F32)
    local_sums = is_first[:, :, None] * sides[:, :1] + is_last[:, :, None] * sides[:, 1:]
    slots = rows * SEGS
    sums_out = local_sums.reshape(slots, ndev, 6 * part).transpose(1, 0, 2)
    task, arrange = to_channels(grad_embedded.astype(BF16))
    got, (sums_got,) = transfer([task, spray_task(sums_out, False)], 10)
    grad_emb_c = arrange(got)
    sums_got = sums_got.reshape(nb, n, slots, 6 * part)
    grad_mod = jnp.sum(sums_got, axis=1).astype(BF16).reshape(nb * slots, 6 * part)
    grad_adaln = rows_sum(soft_cond, grad_mod)
    soft_part = times_t(grad_mod, adaln_proj)
    soft_out = soft_part.reshape(nb * slots, ndev, part).transpose(1, 0, 2)
    grad_hidden_c, conv_sums = conv_backward(
        grad_emb_c, hidden_c, seg_column, conv_one, conv_two, got_convs, nb
    )
    task, arrange = to_frames(grad_hidden_c)
    got, (soft_got,), (got_conv_grads,) = transfer(
        [task, spray_task(soft_out, False), columns_back_task(conv_sums)], 11
    )
    grad_hidden_conv = arrange(got)
    grad_soft = jnp.sum(soft_got, axis=0)
    own_cond = times(step_hot, time_table)
    grad_cond = jax.vjp(jax.nn.silu, own_cond)[1](grad_soft)[0]
    grad_time = jnp.dot(step_hot.astype(F32).T, grad_cond, precision=EXACT)
    grad_convs = jnp.sum(got_conv_grads.astype(F32), axis=0)[0]
    grad_first, grad_second = grad_convs[..., :CHAN], grad_convs[..., CHAN:]
    grad_qkv_own = jnp.sum(got_qkv_grads.astype(F32), axis=0).reshape(3 * part, D).T

    grad_hidden = (grad_embedded + grad_hidden_conv.astype(F32)).astype(BF16).reshape(tokens, D)
    grad_input = rows_sum(grad_hidden, joined).astype(BF16)
    grad_joined = times(grad_hidden, in_t)
    grad_mels = grad_joined[:, : 2 * MEL].reshape(rows, frames, 2 * MEL)
    grad_embed = grad_joined[:, 2 * MEL :].astype(BF16)
    grad_text = rows_sum(grad_embed, text_hot).astype(BF16)
    (in_sum,), (text_sum,) = transfer(
        [
            scatter_task(grad_input.reshape(nb, n, part, -1)),
            scatter_task(grad_text.reshape(nb, n, -1, VOCAB)),
        ],
        13,
    )
    grad_input_own = jnp.sum(in_sum.astype(F32), axis=0).T
    grad_text_own = jnp.sum(text_sum.astype(F32), axis=0).T
    grad_down_own = jnp.concatenate([late_sum[3 * part : 4 * part], late_sum[4 * part :]], axis=1)

    return (
        block_out,
        grad_mels,
        grad_input_own,
        grad_first,
        grad_second,
        grad_time,
        grad_adaln,
        grad_qkv_own,
        late_sum[:part].T,
        late_sum[part : 3 * part].T,
        grad_down_own.T,
        grad_text_own,
    )


def solution(mesh):
    frames = P("batch", "seq", None)
    columns = P(None, ("batch", "seq"))
    taps = P(None, ("batch", "seq"), None)
    in_specs = (
        frames,
        P("batch", "seq"),
        P("batch", None),
        P("batch", None),
        P("batch", None),
        columns,
        taps,
        taps,
        columns,
        columns,
        columns,
        columns,
        columns,
        columns,
        columns,
        frames,
    )
    out_specs = (
        frames,
        frames,
        columns,
        taps,
        taps,
        columns,
        columns,
        columns,
        columns,
        columns,
        columns,
        columns,
    )
    return jax.shard_map(
        on_device, mesh=mesh, in_specs=in_specs, out_specs=out_specs, check_vma=False
    )
```

```python
import functools

import jax
import jax.numpy as jnp
import numpy as np
from jax import lax
from jax.experimental import pallas as pl
from jax.experimental.pallas import tpu as pltpu
from jax.sharding import PartitionSpec as P

D = 1024
HEADS = 16
HEAD = 64
MEL = 100
VOCAB = 2546
KERNEL = 31
HALF = KERNEL // 2
CHAN = 64
STEPS = 32
SEGS = 4
GAP = 16
FOLD = 4
TAPS = KERNEL + FOLD - 1

EPSILON = 1e-06
MASKED = -1e30
EXACT = lax.Precision.HIGHEST
MESH = pl.DeviceIdType.MESH
ANY = pl.BlockSpec(memory_space=pl.ANY)
VMEM_LIMIT = 56 * 1024 * 1024
F32 = jnp.float32
BF16 = jnp.bfloat16


def dims():
    return lax.axis_size("batch"), lax.axis_size("seq")


def params(cid=None):
    if cid is None:
        return pltpu.CompilerParams(vmem_limit_bytes=VMEM_LIMIT)
    return pltpu.CompilerParams(
        collective_id=cid, has_side_effects=True, vmem_limit_bytes=VMEM_LIMIT
    )


def greet_all(nb, n, b, s):
    sem = pltpu.get_barrier_semaphore()
    me = b * n + s
    for d in range(1, nb * n):
        other = lax.rem(me + d, nb * n)
        pl.semaphore_signal(
            sem,
            inc=1,
            device_id={"batch": other // n, "seq": lax.rem(other, n)},
            device_id_type=MESH,
        )
    pl.semaphore_wait(sem, nb * n - 1)


def greet_group(n, s):
    sem = pltpu.get_barrier_semaphore()
    for d in range(1, n):
        pl.semaphore_signal(
            sem, inc=1, device_id={"seq": lax.rem(s + d, n)}, device_id_type=MESH
        )
    pl.semaphore_wait(sem, n - 1)


def block_of(b, s, n):
    chips, core = n // 2, lax.rem(s, 2)
    return 2 * lax.rem(s // 2 + b + (chips // 2) * core, chips) + core


def holder_of(b, m, n, nb):
    chips, core = n // 2, lax.rem(m, 2)
    turned = m // 2 + (nb + chips) * chips - b - (chips // 2) * core
    return 2 * lax.rem(turned, chips) + core


def remote(src, dst, send, recv, **where):
    return pltpu.make_async_remote_copy(
        src_ref=src,
        dst_ref=dst,
        send_sem=send,
        recv_sem=recv,
        device_id=where,
        device_id_type=MESH,
    )


class Task:
    def __init__(
        self, operands, outs, scratch, body, everyone=False, in_specs=None, out_specs=None
    ):
        self.operands, self.outs, self.scratch = list(operands), list(outs), list(scratch)
        self.body, self.everyone = body, everyone
        self.in_specs = in_specs or [ANY] * len(self.operands)
        self.out_specs = out_specs or [ANY] * len(self.outs)


def transfer_kernel(bodies, sizes, everyone, nb, n, *refs):
    b, s = lax.axis_index("batch"), lax.axis_index("seq")
    counts = [sum(size[i] for size in sizes) for i in range(3)]
    pools = [
        list(refs[: counts[0]]),
        list(refs[counts[0] : counts[0] + counts[1]]),
        list(refs[counts[0] + counts[1] :]),
    ]
    running = []
    for body, size in zip(bodies, sizes):
        taken = []
        for i in range(3):
            taken.append(pools[i][: size[i]])
            pools[i] = pools[i][size[i] :]
        running.append(body(*taken, b, s, nb, n))
    if everyone:
        greet_all(nb, n, b, s)
    else:
        greet_group(n, s)
    while running:
        left = []
        for task in running:
            try:
                next(task)
                left.append(task)
            except StopIteration:
                pass
        running = left


def transfer(tasks, cid):
    nb, n = dims()
    operands = [x for task in tasks for x in task.operands]
    outs = [x for task in tasks for x in task.outs]
    sizes = [(len(t.operands), len(t.outs), len(t.scratch)) for t in tasks]
    got = pl.pallas_call(
        functools.partial(
            transfer_kernel,
            [t.body for t in tasks],
            sizes,
            any(t.everyone for t in tasks),
            nb,
            n,
        ),
        out_shape=outs,
        in_specs=[x for task in tasks for x in task.in_specs],
        out_specs=[x for task in tasks for x in task.out_specs],
        scratch_shapes=[x for task in tasks for x in task.scratch],
        compiler_params=params(cid),
    )(*operands)
    got = list(got)
    result = []
    for size in sizes:
        result.append(got[: size[1]])
        got = got[size[1] :]
    return result


DMA = pltpu.SemaphoreType.DMA


def like(x, shape, dtype=None):
    return jax.ShapeDtypeStruct(tuple(shape), dtype or x.dtype)


def swap_task(x, shape, parts):
    n = dims()[1]

    def body(ins, outs, scratch, b, s, nb, n):
        send, recv, local = scratch
        src, dst = parts(ins[0], outs[0], b, s)
        copies = []
        for d in range(1, n):
            t = lax.rem(s + d, n)
            copy = remote(src(t), dst, send.at[d], recv.at[d], seq=t)
            copy.start()
            copies.append(copy)
        own = pltpu.make_async_copy(src(s), dst, local)
        own.start()
        copies.append(own)
        yield
        yield
        for copy in copies:
            copy.wait()

    return Task([x], [like(x, shape)], [DMA((n,)), DMA((n,)), DMA], body)


def to_channels(x):
    n = dims()[1]
    rows, frames = x.shape[:2]
    width = x.shape[2] // n
    if width % 128 == 0:

        def parts(x, o, b, s):
            first = pl.multiple_of(s * frames, 16)
            return (
                lambda t: x.at[
                    :, :, pl.ds(pl.multiple_of(block_of(b, t, n) * width, 128), width)
                ]
            ), o.at[:, pl.ds(first, frames), :]

        return swap_task(x, (rows, n * frames, width), parts), lambda got: got[0]

    def split_parts(x, o, b, s):
        return (lambda t: x.at[block_of(b, t, n)]), o.at[s]

    split = x.reshape(rows, frames, n, width).transpose(2, 0, 1, 3)
    return (
        swap_task(split, split.shape, split_parts),
        lambda got: got[0].transpose(1, 0, 2, 3).reshape(rows, n * frames, width),
    )


def to_frames(x):
    n = dims()[1]
    rows, length, width = x.shape
    frames = length // n
    if width % 128 == 0:

        def parts(x, o, b, s):
            first = pl.multiple_of(block_of(b, s, n) * width, 128)
            return (
                lambda t: x.at[:, pl.ds(pl.multiple_of(t * frames, 16), frames), :]
            ), o.at[:, :, pl.ds(first, width)]

        return swap_task(x, (rows, frames, n * width), parts), lambda got: got[0]

    def split_parts(x, o, b, s):
        return (lambda t: x.at[t]), o.at[block_of(b, s, n)]

    split = x.reshape(rows, n, frames, width).transpose(1, 0, 2, 3)
    return (
        swap_task(split, split.shape, split_parts),
        lambda got: got[0].transpose(1, 2, 0, 3).reshape(rows, frames, n * width),
    )


def spray_task(x, by_batch):
    nb, n = dims()
    ndev = nb * n

    def body(ins, outs, scratch, b, s, nb, n):
        send, recv, local = scratch
        x, o = ins[0], outs[0]
        me = b * n + s
        own = pltpu.make_async_copy(x.at[b if by_batch else me], o.at[me], local)
        own.start()
        copies = [own]
        for d in range(1, ndev):
            other = lax.rem(me + d, ndev)
            plane, where = other // n, lax.rem(other, n)
            copy = remote(
                x.at[plane if by_batch else other],
                o.at[me],
                send.at[d],
                recv.at[d],
                batch=plane,
                seq=where,
            )
            copy.start()
            copies.append(copy)
        yield
        yield
        for copy in copies:
            copy.wait()

    return Task(
        [x], [like(x, (ndev,) + x.shape[1:])], [DMA((ndev,)), DMA((ndev,)), DMA], body, True
    )


def gather_task(x):
    n = dims()[1]

    def body(ins, outs, scratch, b, s, nb, n):
        send, recv, local = scratch
        x, o = ins[0], outs[0]
        core = lax.rem(s, 2)
        sibling = s + 1 - 2 * core
        chips = n // 2
        far, near = [], []
        for d in range(1, chips):
            copy = remote(x, o.at[:, s], send.at[d], recv.at[d], seq=lax.rem(s + 2 * d, n))
            copy.start()
            far.append(copy)
        copy = remote(x, o.at[:, s], send.at[0], recv.at[0], seq=sibling)
        copy.start()
        near.append(copy)
        own = pltpu.make_async_copy(x, o.at[:, s], local)
        own.start()
        yield
        for d in range(1, chips):
            far[d - 1].wait_recv()
            source = lax.rem(s - 2 * d + n, n)
            copy = remote(
                o.at[:, source],
                o.at[:, source],
                send.at[chips + d],
                recv.at[chips + d],
                seq=sibling,
            )
            copy.start()
            near.append(copy)
        yield
        own.wait()
        for copy in far:
            copy.wait_send()
        for copy in near:
            copy.wait()

    out = like(x, (x.shape[0], n) + x.shape[1:])
    return Task([x], [out], [DMA((n,)), DMA((n,)), DMA], body)


def quad_gather_task(x):
    n = dims()[1]
    frames = x.shape[1]
    half = frames // 2

    def body(ins, outs, scratch, b, s, nb, n):
        send, recv, local = scratch
        x, o = ins[0], outs[0]
        core, chip = lax.rem(s, 2), s // 2
        sibling = s + 1 - 2 * core
        flip_x = chip + 1 - 2 * lax.rem(chip, 2)
        flip_y = lax.rem(chip + 2, 4)
        diagonal = lax.rem(flip_x + 2, 4)
        seat = lambda c: 2 * c + core
        parts = (pl.ds(0, half), pl.ds(half, half))
        k = iter(range(16))

        def push(piece, source, target):
            i = next(k)
            where = o.at[:, source, parts[piece]]
            copy = remote(
                x.at[:, parts[piece]] if source is s else where,
                where,
                send.at[i],
                recv.at[i],
                seq=target,
            )
            copy.start()
            return copy

        to_x = [push(p, s, seat(flip_x)) for p in (0, 1)]
        to_y = [push(p, s, seat(flip_y)) for p in (1, 0)]
        near = [push(p, s, sibling) for p in (0, 1)]
        own = pltpu.make_async_copy(x, o.at[:, s], local)
        own.start()
        yield
        far = []
        to_x[0].wait_recv()
        far.append(push(0, seat(flip_x), seat(flip_y)))
        near.append(push(0, seat(flip_x), sibling))
        to_y[0].wait_recv()
        far.append(push(1, seat(flip_y), seat(flip_x)))
        near.append(push(1, seat(flip_y), sibling))
        to_x[1].wait_recv()
        near.append(push(1, seat(flip_x), sibling))
        to_y[1].wait_recv()
        near.append(push(0, seat(flip_y), sibling))
        far[0].wait_recv()
        near.append(push(0, seat(diagonal), sibling))
        far[1].wait_recv()
        near.append(push(1, seat(diagonal), sibling))
        yield
        own.wait()
        for copy in to_x + to_y + far:
            copy.wait_send()
        for copy in near:
            copy.wait()

    out = like(x, (x.shape[0], n) + x.shape[1:])
    return Task([x], [out], [DMA((16,)), DMA((16,)), DMA], body)


def sum_task(x):
    n = dims()[1]
    rows, _, frames, width = x.shape
    chips = n // 2
    step = 16

    def body(ins, outs, scratch, b, s, nb, n):
        mine, first, passed, second, total, send, recv, local, out_sem = scratch
        x, o = ins[0], outs[0]
        core = lax.rem(s, 2)
        sibling = s + 1 - 2 * core
        chip = s // 2
        order = [lax.rem(chip + d, chips) for d in list(range(1, chips)) + [0]]
        pair, own, far = [], [], []
        for k, c in enumerate(order):
            copy = remote(
                x.at[:, 2 * c + 1 - core], first.at[k], send.at[k], recv.at[k], seq=sibling
            )
            copy.start()
            pair.append(copy)
            copy = pltpu.make_async_copy(x.at[:, 2 * c + core], mine.at[k], local.at[k])
            copy.start()
            own.append(copy)
        yield
        for k in range(chips):
            pair[k].wait_recv()
            own[k].wait()
            if k < chips - 1:

                def add(i, carry, k=k):
                    at = pl.ds(pl.multiple_of(i * step, step), step)
                    for r in range(rows):
                        passed[k, r, at, :] = (
                            mine[k, r, at, :].astype(F32) + first[k, r, at, :].astype(F32)
                        ).astype(BF16)
                    return carry

                lax.fori_loop(0, frames // step, add, 0)
                copy = remote(
                    passed.at[k],
                    second.at[k],
                    send.at[chips + k],
                    recv.at[chips + k],
                    seq=2 * order[k] + core,
                )
                copy.start()
                far.append(copy)
        yield
        for copy in far:
            copy.wait_recv()

        def finish(i, carry):
            at = pl.ds(pl.multiple_of(i * step, step), step)
            for r in range(rows):
                value = mine[chips - 1, r, at, :].astype(F32) + first[chips - 1, r, at, :].astype(F32)
                for k in range(chips - 1):
                    value = value + second[k, r, at, :].astype(F32)
                total[r, at, :] = value
            return carry

        lax.fori_loop(0, frames // step, finish, 0)
        out = pltpu.make_async_copy(total, o, out_sem)
        out.start()
        for copy in pair + far:
            copy.wait_send()
        out.wait()

    slots = pltpu.VMEM((chips, rows, frames, width), BF16)
    fewer = pltpu.VMEM((chips - 1, rows, frames, width), BF16)
    return Task(
        [x],
        [like(x, (rows, frames, width), F32)],
        [
            slots,
            slots,
            fewer,
            fewer,
            pltpu.VMEM((rows, frames, width), F32),
            DMA((n,)),
            DMA((n,)),
            DMA((chips,)),
            DMA,
        ],
        body,
    )


def quad_stages(s, x, mine, first, out, one, got_one, two, got_two, sems, add, total):
    send, recv, local = sems
    core, chip = lax.rem(s, 2), s // 2
    sibling = s + 1 - 2 * core
    flip_x = chip + 1 - 2 * lax.rem(chip, 2)
    flip_y = lax.rem(chip + 2, 4)
    places = [flip_x, flip_y, lax.rem(flip_x + 2, 4), chip]
    sent, own = {}, {}
    for k in (2, 0, 1, 3):
        copy = remote(
            out(x, 2 * places[k] + 1 - core), first.at[k], send.at[k], recv.at[k], seq=sibling
        )
        copy.start()
        sent[k] = copy
        copy = pltpu.make_async_copy(out(x, 2 * places[k] + core), mine.at[k], local.at[k])
        copy.start()
        own[k] = copy
    yield
    across = (2 * flip_x + core, 2 * flip_y + core)
    stage = {}
    waited = set()

    def ready(k):
        if k not in waited:
            waited.add(k)
            sent[k].wait_recv()
            own[k].wait()

    for half, i, k in ((0, 1, 2), (1, 1, 2), (0, 0, 0), (1, 0, 1)):
        ready(k)
        add(one.at[half, i], half, [mine.at[k], first.at[k]], [])
        q = 4 + 2 * half + i
        copy = remote(
            one.at[half, i], got_one.at[half, i], send.at[q], recv.at[q], seq=across[half]
        )
        copy.start()
        stage[half, i] = copy
    yield
    for half in (0, 1):
        k = 1 - half
        ready(k)
        stage[half, 1].wait_recv()
        add(two.at[half], half, [mine.at[k], first.at[k]], [got_one.at[half, 1]])
        q = 8 + half
        copy = remote(two.at[half], got_two.at[half], send.at[q], recv.at[q], seq=across[1 - half])
        copy.start()
        stage[half, 2] = copy
    yield
    ready(3)
    for half in (0, 1):
        stage[half, 0].wait_recv()
        stage[half, 2].wait_recv()
        total(half, [mine.at[3], first.at[3]], [got_one.at[half, 0], got_two.at[half]])
    for copy in list(sent.values()) + list(stage.values()):
        copy.wait_send()


def quad_scratch(block, half):
    return [
        pltpu.VMEM((4,) + block, BF16),
        pltpu.VMEM((4,) + block, BF16),
        pltpu.VMEM((2, 2) + half, BF16),
        pltpu.VMEM((2, 2) + half, BF16),
        pltpu.VMEM((2,) + half, BF16),
        pltpu.VMEM((2,) + half, BF16),
        DMA((10,)),
        DMA((10,)),
        DMA((4,)),
    ]


def quad_sum_task(x):
    rows, _, frames, width = x.shape
    half_len = frames // 2
    step = 16

    def body(ins, outs, scratch, b, s, nb, n):
        mine, first, one, got_one, two, got_two, send, recv, local, total, out_sem = scratch

        def each(work):
            def move(i, carry):
                at = pl.multiple_of(i * step, step)
                for r in range(rows):
                    work(r, at)
                return carry

            lax.fori_loop(0, half_len // step, move, 0)

        def value(half, whole_refs, half_refs, r, at):
            parts = [ref[r, pl.ds(half * half_len + at, step), :] for ref in whole_refs]
            parts += [ref[r, pl.ds(at, step), :] for ref in half_refs]
            result = parts[0].astype(F32)
            for p in parts[1:]:
                result = result + p.astype(F32)
            return result

        def add(target, half, whole_refs, half_refs):
            def work(r, at):
                target[r, pl.ds(at, step), :] = value(half, whole_refs, half_refs, r, at).astype(BF16)

            each(work)

        def finish(half, whole_refs, half_refs):
            def work(r, at):
                total[r, pl.ds(half * half_len + at, step), :] = value(
                    half, whole_refs, half_refs, r, at
                )

            each(work)

        yield from quad_stages(
            s,
            ins[0],
            mine,
            first,
            lambda ref, i: ref.at[:, i],
            one,
            got_one,
            two,
            got_two,
            (send, recv, local),
            add,
            finish,
        )
        out = pltpu.make_async_copy(total, outs[0], out_sem)
        out.start()
        out.wait()

    return Task(
        [x],
        [like(x, (rows, frames, width), F32)],
        quad_scratch((rows, frames, width), (rows, half_len, width))
        + [pltpu.VMEM((rows, frames, width), F32), DMA],
        body,
    )


def quad_scatter_task(x):
    nb, n = dims()
    block = (nb,) + x.shape[2:]

    def body(ins, outs, scratch, b, s, nb, n):
        mine, first, one, got_one, two, got_two, send, recv, local = scratch[:9]
        total, z_send, z_recv, z_local = scratch[9:]
        o = outs[0]

        def value(half, whole_refs, half_refs, i):
            parts = [ref[half * (nb // 2) + i] for ref in whole_refs]
            parts += [ref[i] for ref in half_refs]
            result = parts[0].astype(F32)
            for p in parts[1:]:
                result = result + p.astype(F32)
            return result.astype(BF16)

        def add(target, half, whole_refs, half_refs):
            def work(i, carry):
                target[i] = value(half, whole_refs, half_refs, i)
                return carry

            lax.fori_loop(0, nb // 2, work, 0)

        def finish(half, whole_refs, half_refs):
            def work(i, carry):
                total[half * (nb // 2) + i] = value(half, whole_refs, half_refs, i)
                return carry

            lax.fori_loop(0, nb // 2, work, 0)

        yield from quad_stages(
            s,
            ins[0],
            mine,
            first,
            lambda ref, i: ref.at[:, i],
            one,
            got_one,
            two,
            got_two,
            (send, recv, local),
            add,
            finish,
        )
        last = []
        for d in range(1, nb):
            plane = lax.rem(b + d, nb)
            copy = remote(
                total.at[plane], o.at[b], z_send.at[d], z_recv.at[d], batch=plane, seq=s
            )
            copy.start()
            last.append(copy)
        copy = pltpu.make_async_copy(total.at[b], o.at[b], z_local)
        copy.start()
        last.append(copy)
        yield
        for copy in last:
            copy.wait()

    return Task(
        [x],
        [like(x, block)],
        quad_scratch(block, (nb // 2,) + x.shape[2:])
        + [pltpu.VMEM(block, BF16), DMA((nb,)), DMA((nb,)), DMA],
        body,
        True,
    )


def spread_task(x):
    nb, n = dims()
    chips = n // 2

    def body(ins, outs, scratch, b, s, nb, n):
        z_send, z_recv, p_send, p_recv, c_send, c_recv, local = scratch
        x, o = ins[0], outs[0]
        core = lax.rem(s, 2)
        sibling = s + 1 - 2 * core
        own = pltpu.make_async_copy(x, o.at[b, s], local)
        own.start()
        along = []
        for d in range(1, nb):
            copy = remote(
                x, o.at[b, s], z_send.at[d], z_recv.at[d], batch=lax.rem(b + d, nb), seq=s
            )
            copy.start()
            along.append(copy)
        far, near = [], []

        def onward(d):
            plane = lax.rem(b - d + nb, nb)
            source = x if d == 0 else o.at[plane, s]
            for c in range(1, chips):
                copy = remote(
                    source,
                    o.at[plane, s],
                    p_send.at[d, c],
                    p_recv.at[d, c],
                    seq=lax.rem(s + 2 * c, n),
                )
                copy.start()
                far.append((d, c, plane, copy))
            copy = remote(source, o.at[plane, s], c_send.at[d, 0], c_recv.at[d, 0], seq=sibling)
            copy.start()
            near.append(copy)

        onward(0)
        yield
        for d in range(1, nb):
            along[d - 1].wait_recv()
            onward(d)
        yield
        for d, c, plane, copy in far:
            copy.wait_recv()
            source = lax.rem(s - 2 * c + n, n)
            last = remote(
                o.at[plane, source],
                o.at[plane, source],
                c_send.at[d, c],
                c_recv.at[d, c],
                seq=sibling,
            )
            last.start()
            near.append(last)
        yield
        own.wait()
        for copy in along:
            copy.wait_send()
        for entry in far:
            entry[3].wait_send()
        for copy in near:
            copy.wait()

    square = DMA((nb, chips))
    return Task(
        [x],
        [like(x, (nb, n) + x.shape)],
        [DMA((nb,)), DMA((nb,)), square, square, square, square, DMA],
        body,
        True,
    )


def columns_out_task(x, late=False):
    nb, n = dims()
    ndev = nb * n
    kinds = x.shape[0]

    def body(ins, outs, scratch, b, s, nb, n):
        send, recv = scratch
        x, o = ins[0], outs[0]
        me = b * n + s
        pieces = []
        for j in range(kinds):
            piece = kinds * me + j
            column = lax.rem(piece, ndev)
            pieces.append((j, piece // ndev, column // nb, lax.rem(column, nb)))
        if late:
            yield
        sent = []
        for j, part, block, slot in pieces:
            source, target, arrived = x.at[j], o.at[part, slot], recv.at[part, slot]
            for d in range(nb):
                plane = lax.rem(b + d, nb)
                owner = holder_of(plane, block, n, nb)
                if d == 0:

                    @pl.when(owner == s)
                    def _(source=source, target=target, arrived=arrived):
                        pltpu.make_async_copy(source, target, arrived).start()

                    @pl.when(owner != s)
                    def _(source=source, target=target, arrived=arrived, j=j, owner=owner):
                        remote(
                            source, target, send.at[j, 0], arrived, batch=b, seq=owner
                        ).start()
                else:
                    copy = remote(
                        source, target, send.at[j, d], arrived, batch=plane, seq=owner
                    )
                    copy.start()
                    sent.append(copy)
        yield
        yield
        yield
        for copy in sent:
            copy.wait_send()
        for j, part, block, slot in pieces:
            owner = holder_of(b, block, n, nb)

            @pl.when(owner != s)
            def _(j=j, part=part, slot=slot, owner=owner):
                remote(
                    x.at[j], o.at[part, slot], send.at[j, 0], recv.at[part, slot], batch=b, seq=owner
                ).wait_send()

        for p in range(kinds):
            for j in range(nb):
                pltpu.make_async_copy(x.at[0], o.at[p, j], recv.at[p, j]).wait()

    return Task(
        [x],
        [like(x, (kinds, nb) + x.shape[1:])],
        [DMA((kinds, nb)), DMA((kinds, nb))],
        body,
        True,
    )


def columns_back_task(x):
    nb, n = dims()
    ndev = nb * n
    kinds = x.shape[0]

    def body(ins, outs, scratch, b, s, nb, n):
        send, recv = scratch
        x, o = ins[0], outs[0]
        me = b * n + s
        pieces = []
        for p in range(kinds):
            for j in range(nb):
                column = p * ndev + block_of(b, s, n) * nb + j
                part = lax.rem(column, kinds)
                pieces.append(
                    (x.at[p, j], o.at[b, part], column // kinds, send.at[p, j], recv.at[b, part])
                )
        for source, target, owner, sent, arrived in pieces:

            @pl.when(owner == me)
            def _(source=source, target=target, arrived=arrived):
                pltpu.make_async_copy(source, target, arrived).start()

            @pl.when(owner != me)
            def _(source=source, target=target, owner=owner, sent=sent, arrived=arrived):
                remote(
                    source, target, sent, arrived, batch=owner // n, seq=lax.rem(owner, n)
                ).start()

        yield
        yield
        yield
        for source, target, owner, sent, arrived in pieces:

            @pl.when(owner != me)
            def _(source=source, target=target, owner=owner, sent=sent, arrived=arrived):
                remote(
                    source, target, sent, arrived, batch=owner // n, seq=lax.rem(owner, n)
                ).wait_send()

        for p in range(kinds):
            for j in range(nb):
                pltpu.make_async_copy(x.at[0, 0], o.at[j, p], recv.at[j, p]).wait()

    return Task(
        [x],
        [like(x, (nb, kinds) + x.shape[2:])],
        [DMA((kinds, nb)), DMA((nb, kinds))],
        body,
        True,
    )


def scatter_task(x):
    nb, n = dims()
    chips = n // 2

    def body(ins, outs, scratch, b, s, nb, n):
        mine, first, passed, second, total, send, recv, local, z_send, z_recv, z_local = scratch
        x, o = ins[0], outs[0]
        core = lax.rem(s, 2)
        sibling = s + 1 - 2 * core
        chip = s // 2
        order = [lax.rem(chip + d, chips) for d in list(range(1, chips)) + [0]]
        pair, own, far, last = [], [], [], []
        for k, c in enumerate(order):
            copy = remote(
                x.at[:, 2 * c + 1 - core], first.at[k], send.at[k], recv.at[k], seq=sibling
            )
            copy.start()
            pair.append(copy)
            copy = pltpu.make_async_copy(x.at[:, 2 * c + core], mine.at[k], local.at[k])
            copy.start()
            own.append(copy)
        yield
        for k in range(chips - 1):
            pair[k].wait_recv()
            own[k].wait()

            def add(i, carry, k=k):
                passed[k, i] = (mine[k, i].astype(F32) + first[k, i].astype(F32)).astype(BF16)
                return carry

            lax.fori_loop(0, nb, add, 0)
            copy = remote(
                passed.at[k],
                second.at[k],
                send.at[chips + k],
                recv.at[chips + k],
                seq=2 * order[k] + core,
            )
            copy.start()
            far.append(copy)
        yield
        pair[chips - 1].wait_recv()
        own[chips - 1].wait()
        for copy in far:
            copy.wait_recv()

        def finish(i, carry):
            value = mine[chips - 1, i].astype(F32) + first[chips - 1, i].astype(F32)
            for k in range(chips - 1):
                value = value + second[k, i].astype(F32)
            total[i] = value.astype(BF16)
            return carry

        lax.fori_loop(0, nb, finish, 0)
        for d in range(1, nb):
            plane = lax.rem(b + d, nb)
            copy = remote(
                total.at[plane], o.at[b], z_send.at[d], z_recv.at[d], batch=plane, seq=s
            )
            copy.start()
            last.append(copy)
        copy = pltpu.make_async_copy(total.at[b], o.at[b], z_local)
        copy.start()
        last.append(copy)
        yield
        for copy in pair + far:
            copy.wait_send()
        for copy in last:
            copy.wait()

    block = (nb,) + x.shape[2:]
    return Task(
        [x],
        [like(x, block)],
        [
            pltpu.VMEM((chips,) + block, BF16),
            pltpu.VMEM((chips,) + block, BF16),
            pltpu.VMEM((chips - 1,) + block, BF16),
            pltpu.VMEM((chips - 1,) + block, BF16),
            pltpu.VMEM(block, BF16),
            DMA((n,)),
            DMA((n,)),
            DMA((chips,)),
            DMA((nb,)),
            DMA((nb,)),
            DMA,
        ],
        body,
        True,
    )


def times(left, right):
    return lax.dot_general(left, right, (((1,), (0,)), ((), ())), preferred_element_type=F32)


def times_t(left, right):
    return lax.dot_general(left, right, (((1,), (1,)), ((), ())), preferred_element_type=F32)


def rows_sum(left, right):
    return lax.dot_general(left, right, (((0,), (0,)), ((), ())), preferred_element_type=F32)


def mish_parts(v):
    e = jnp.exp(jnp.minimum(v, 20.0))
    n = e * (e + 2.0)
    inverse = 1.0 / (n + 2.0)
    return e, n, inverse


def mish(v):
    e, n, inverse = mish_parts(v)
    return v * (n * inverse)


def mish_slope(v):
    e, n, inverse = mish_parts(v)
    return n * inverse + v * (4.0 * e * (1.0 + e)) * inverse * inverse


CHUNK = 128


def interleave(even, odd):
    low = lax.broadcasted_iota(jnp.int32, even.shape, 1) < CHAN
    return (
        jnp.where(low, even, pltpu.roll(odd, CHAN, 1)),
        jnp.where(low, pltpu.roll(even, CHAN, 1), odd),
    )


def to_groups(even, odd):
    if even.shape[1] == CHAN:
        return (jnp.concatenate([even, odd], axis=1),)
    return interleave(even, odd)


def to_pair(blocks):
    if len(blocks) == 1:
        return blocks[0][:, :CHAN], blocks[0][:, CHAN:]
    return interleave(*blocks)


def place(buf, source, seg, length):
    rows = buf.shape[0]

    def clear(i, carry):
        buf[pl.ds(pl.multiple_of(i * 16, 16), 16), :] = jnp.zeros((16, buf.shape[1]), F32)
        return carry

    lax.fori_loop(0, rows // 16, clear, 0)

    def move(i, carry):
        at = pl.multiple_of(i * CHUNK, CHUNK)
        value = source(at)
        ids = seg[0, pl.ds(at, CHUNK), :] & 7
        for u in range(SEGS):
            to = pl.ds(at + GAP * (u + 1), CHUNK)
            buf[to, :] = buf[to, :] + jnp.where(ids == u, value, 0.0)
        return carry

    lax.fori_loop(0, length // CHUNK, move, 0)


def unplace(buf, sink, seg, length):
    def move(i, carry):
        at = pl.multiple_of(i * CHUNK, CHUNK)
        ids = seg[0, pl.ds(at, CHUNK), :] & 7
        value = buf[pl.ds(at + GAP, CHUNK), :]
        for u in range(1, SEGS):
            value = jnp.where(ids == u, buf[pl.ds(at + GAP * (u + 1), CHUNK), :], value)
        sink[0, pl.ds(at, CHUNK), :] = value.astype(sink.dtype)
        return carry

    lax.fori_loop(0, length // CHUNK, move, 0)


def folded(buf, count, first):
    return buf[pl.ds(first, count, stride=FOLD), :]


def spread_taps(x, buf, count):
    for t in range(TAPS // 2):
        blocks = to_groups(folded(buf, count, 2 * t + 1), folded(buf, count, 2 * t + 2))
        for g, block in enumerate(blocks):
            x[g, :, 2 * CHAN * t : 2 * CHAN * (t + 1)] = block.astype(BF16)


def write_folded(buf, count, groups, value, live=None):
    for w in range(FOLD // 2):
        lanes = slice(2 * CHAN * w, 2 * CHAN * (w + 1))
        for half, part in enumerate(to_pair([value(g, lanes) for g in range(groups)])):
            at = pl.ds(GAP + 2 * w + half, count, stride=FOLD)
            buf[at, :] = part if live is None else part * live[at, :]


def fill_bands(bands, taps, groups, back):
    low = lax.broadcasted_iota(jnp.int32, (CHAN, 2 * CHAN), 1) < CHAN
    zero = jnp.zeros((CHAN, 2 * CHAN), F32)
    width = groups * CHAN

    def forms(k):
        if not 0 <= k < KERNEL:
            return None
        full = taps[:, KERNEL - 1 - k if back else k].astype(F32).reshape(width, 2 * CHAN)
        if back:
            full = full.T
            if groups == 1:
                full = jnp.concatenate([full, full], axis=1)
        turned = pltpu.roll(full, CHAN, 1)
        result = {}
        for c in range(2):
            for g in range(groups):
                if back:
                    rows, own = slice(c * CHAN, (c + 1) * CHAN), g
                else:
                    rows, own = slice(g * CHAN, (g + 1) * CHAN), c
                pair = (full[rows], turned[rows])
                result[c, g] = pair if own == 0 else pair[::-1]
        return result

    known = {}
    for tap in range(TAPS):
        known[tap] = forms(tap)
        known.pop(tap - FOLD, None)
        for w in range(FOLD // 2):
            left, right = known.get(tap - 2 * w), known.get(tap - 2 * w - 1)
            for c in range(2):
                for g in range(groups):
                    a = zero if left is None else left[c, g][0]
                    b = zero if right is None else right[c, g][1]
                    bands[
                        c, g, tap * CHAN : (tap + 1) * CHAN, 2 * CHAN * w : 2 * CHAN * (w + 1)
                    ] = jnp.where(low, a, b).astype(BF16)


FOLDED = FOLD * CHAN
DEPTH = TAPS * CHAN


def conv_forward_kernel(count, length, groups, u, seg, taps, c1, c2, out, buf, live, x, bands):
    @pl.when(pl.program_id(0) == 0)
    def _():
        fill_bands(bands, taps, groups, False)

    width = groups * CHAN
    place(live, lambda at: jnp.ones((CHUNK, width), F32), seg, length)
    place(buf, lambda at: u[0, pl.ds(at, CHUNK), :].astype(F32), seg, length)
    spread_taps(x, buf, count)
    for g in range(groups):
        c1[0, g] = times(x[g], bands[0, g])
    write_folded(buf, count, groups, lambda g, lanes: mish(c1[0, g, :, lanes]), live)
    spread_taps(x, buf, count)
    for g in range(groups):
        c2[0, g] = times(x[g], bands[1, g])
    write_folded(buf, count, groups, lambda g, lanes: mish(c2[0, g, :, lanes]))
    unplace(buf, out, seg, length)


def conv_sizes(length):
    count = -(-(length + GAP * (SEGS - 1)) // FOLD)
    count = -(-count // 16) * 16
    return count, FOLD * count + 48


def whole(shape):
    zeros = (0,) * len(shape)
    return pl.BlockSpec(shape, lambda *i: zeros)


def by_row(shape):
    return pl.BlockSpec((1,) + tuple(shape[1:]), lambda r: (r,) + (0,) * (len(shape) - 1))


def conv_forward(u, seg, taps):
    rows, length, width = u.shape
    groups = width // CHAN
    count, buffer = conv_sizes(length)
    kept = (rows, groups, count, FOLDED)
    return pl.pallas_call(
        functools.partial(conv_forward_kernel, count, length, groups),
        grid=(rows,),
        in_specs=[by_row(u.shape), by_row(seg.shape), whole(taps.shape)],
        out_specs=[by_row(kept), by_row(kept), by_row(u.shape)],
        out_shape=[
            jax.ShapeDtypeStruct(kept, F32),
            jax.ShapeDtypeStruct(kept, F32),
            jax.ShapeDtypeStruct(u.shape, BF16),
        ],
        scratch_shapes=[
            pltpu.VMEM((buffer, width), F32),
            pltpu.VMEM((buffer, width), F32),
            pltpu.VMEM((groups, count, DEPTH), BF16),
            pltpu.VMEM((2, groups, DEPTH, FOLDED), BF16),
        ],
        compiler_params=params(),
    )(u, seg, taps)


def weight_sums(even, odd, c, turned, x, groups):
    rows = slice(c * CHAN, (c + 1) * CHAN)
    blocks = TAPS // 2
    pair = 2 * CHAN
    for g in range(groups):
        for start in range(0, blocks, 2):
            stop = min(start + 2, blocks)
            product = times(turned[g], x[g, :, start * pair : stop * pair])
            for t in range(start, stop):
                part = product[:, (t - start) * pair : (t - start + 1) * pair]
                for m in range(FOLD):
                    to = t - m // 2
                    if 0 <= to < 16:
                        sums = odd if m % 2 else even
                        sums[g, to, rows] = sums[g, to, rows] + part[m * CHAN : (m + 1) * CHAN]


def conv_backward_kernel(
    count, length, groups, nb, d, u, seg, c1, c2, taps, dh, pieces, buf, grads, live, x, turned, bands, even, odd
):
    width = groups * CHAN
    row = pl.program_id(0)

    @pl.when(row == 0)
    def _():
        fill_bands(bands, taps, groups, True)
        even[...] = jnp.zeros_like(even)
        odd[...] = jnp.zeros_like(odd)

    place(live, lambda at: jnp.ones((CHUNK, width), F32), seg, length)
    place(grads, lambda at: d[0, pl.ds(at, CHUNK), :].astype(F32), seg, length)

    def slope(kept, scaled):
        values = {}
        for w in range(FOLD // 2):
            lanes = slice(2 * CHAN * w, 2 * CHAN * (w + 1))
            for g in range(groups):
                value = scaled(g, w, lanes) * mish_slope(kept[0, g, :, lanes])
                values[g, w] = value
                turned[g, lanes, :] = value.T.astype(BF16)
        return values

    def loaded(g, w, lanes):
        return to_groups(
            folded(grads, count, GAP + 2 * w), folded(grads, count, GAP + 2 * w + 1)
        )[g]

    values = slope(c2, loaded)
    write_folded(grads, count, groups, lambda g, lanes: values[g, lanes.start // (2 * CHAN)])
    for i in range(0, GAP, 8):
        buf[i : i + 8, :] = jnp.zeros((8, width), F32)
    for i in range(GAP + FOLD * count, buf.shape[0], 8):
        buf[i : i + 8, :] = jnp.zeros((8, width), F32)
    write_folded(buf, count, groups, lambda g, lanes: mish(c1[0, g, :, lanes]), live)
    spread_taps(x, buf, count)
    weight_sums(even, odd, 1, turned, x, groups)
    spread_taps(x, grads, count)
    back = [times(x[g], bands[1, g]) for g in range(groups)]

    def masked(g, w, lanes):
        alive = to_groups(
            folded(live, count, GAP + 2 * w), folded(live, count, GAP + 2 * w + 1)
        )[g]
        return back[g][:, lanes] * alive

    values = slope(c1, masked)
    write_folded(grads, count, groups, lambda g, lanes: values[g, lanes.start // (2 * CHAN)])
    place(buf, lambda at: u[0, pl.ds(at, CHUNK), :].astype(F32), seg, length)
    spread_taps(x, buf, count)
    weight_sums(even, odd, 0, turned, x, groups)
    spread_taps(x, grads, count)
    last = [times(x[g], bands[0, g]) for g in range(groups)]
    write_folded(buf, count, groups, lambda g, lanes: last[g][:, lanes])
    unplace(buf, dh, seg, length)

    @pl.when(row == pl.num_programs(0) - 1)
    def _():
        low = lax.broadcasted_iota(jnp.int32, (2 * CHAN, 2 * CHAN), 1) < CHAN
        part = width // nb
        each = CHAN // part
        for g in range(groups):
            for p in range(16):
                left = pltpu.roll(odd[g, p], CHAN, 1)
                right = pltpu.roll(odd[g, p + 1], CHAN, 1) if p < 15 else left
                total = (even[g, p] + jnp.where(low, left, right)).T.astype(BF16)
                for half in range(2):
                    k = 2 * p + half
                    if k < KERNEL:
                        for j in range(each):
                            first = half * CHAN + j * part
                            pieces[0, g * each + j, k] = total[first : first + part]


def conv_backward(d, u, seg, c1, c2, taps, nb):
    rows, length, width = u.shape
    groups = width // CHAN
    count, buffer = conv_sizes(length)
    pieces = (1, nb, KERNEL, width // nb, 2 * CHAN)
    sums = pltpu.VMEM((groups, 16, 2 * CHAN, 2 * CHAN), F32)
    frames = pltpu.VMEM((buffer, width), F32)
    return pl.pallas_call(
        functools.partial(conv_backward_kernel, count, length, groups, nb),
        grid=(rows,),
        in_specs=[
            by_row(d.shape),
            by_row(u.shape),
            by_row(seg.shape),
            by_row(c1.shape),
            by_row(c2.shape),
            whole(taps.shape),
        ],
        out_specs=[by_row(u.shape), whole(pieces)],
        out_shape=[
            jax.ShapeDtypeStruct(u.shape, BF16),
            jax.ShapeDtypeStruct(pieces, BF16),
        ],
        scratch_shapes=[
            frames,
            frames,
            frames,
            pltpu.VMEM((groups, count, DEPTH), BF16),
            pltpu.VMEM((groups, FOLDED, count), BF16),
            pltpu.VMEM((2, groups, DEPTH, FOLDED), BF16),
            sums,
            sums,
        ],
        compiler_params=params(),
    )(d, u, seg, c1, c2, taps)


def pair_swap(x):
    width = x.shape[1]
    if width % 128:
        x = jnp.concatenate([x, x], axis=1)
    lane = lax.broadcasted_iota(jnp.int32, x.shape, 1)
    after = pltpu.roll(x, x.shape[1] - 1, 1)
    before = pltpu.roll(x, 1, 1)
    return jnp.where(lax.rem(lane, 2) == 0, -after, before)[:, :width]


def qkv_kernel(width, x, w, cos, sin, q, k, v):
    got = lax.dot_general(
        x[0], w[...], (((1,), (1,)), ((), ())), preferred_element_type=F32
    )
    for p, out in enumerate((q, k)):
        part = got[:, p * width : (p + 1) * width]
        out[0] = (part * cos[0] + pair_swap(part) * sin[0]).astype(BF16)
    v[0] = got[:, 2 * width :].astype(BF16)


def qkv_forward(x, w, cos, sin):
    rows, length, depth = x.shape
    width = w.shape[0] // 3
    block = 512
    spec = pl.BlockSpec((1, block, width), lambda r, i: (r, i, 0))
    shape = jax.ShapeDtypeStruct((rows, length, width), BF16)
    return pl.pallas_call(
        functools.partial(qkv_kernel, width),
        grid=(rows, length // block),
        in_specs=[
            pl.BlockSpec((1, block, depth), lambda r, i: (r, i, 0)),
            whole(w.shape),
            spec,
            spec,
        ],
        out_specs=[spec] * 3,
        out_shape=[shape] * 3,
        compiler_params=params(),
    )(x, w, cos, sin)


def attention_forward_kernel(width, q, k, v, q_code, k_code, out, low, log_sum):
    heads = width // HEAD
    lane = lax.broadcasted_iota(jnp.int32, q.shape[1:], 1) // HEAD
    allowed = (q_code[0] & 7) == k_code[0]
    queries = q[0] * 0.125
    result, logs = None, None
    for h in range(heads):
        chosen = jnp.where(lane == h, queries, jnp.zeros_like(queries))
        scores = lax.dot_general(
            chosen, k[0], (((1,), (1,)), ((), ())), preferred_element_type=F32
        )
        scores = jnp.where(allowed, scores, MASKED)
        peak = jnp.max(scores, axis=1, keepdims=True)
        weights = jnp.exp(scores - peak)
        total = jnp.sum(weights, axis=1, keepdims=True)
        value = jnp.dot(weights.astype(BF16), v[0], preferred_element_type=F32) / total
        log = jnp.broadcast_to(peak + jnp.log(total), value.shape)
        result = value if h == 0 else jnp.where(lane == h, value, result)
        logs = log if h == 0 else jnp.where(lane == h, log, logs)
    out[0] = result
    low[0] = result.astype(BF16)
    log_sum[0] = logs


def attention_forward(q, k, v, q_code, k_code):
    rows, length, width = q.shape
    block = 256
    spec = pl.BlockSpec((1, block, width), lambda r, i: (r, i, 0))
    row = pl.BlockSpec((1, length, width), lambda r, i: (r, 0, 0))
    return pl.pallas_call(
        functools.partial(attention_forward_kernel, width),
        grid=(rows, length // block),
        in_specs=[
            spec,
            row,
            row,
            pl.BlockSpec((1, block, 1), lambda r, i: (r, i, 0)),
            pl.BlockSpec((1, 1, length), lambda r, i: (r, 0, 0)),
        ],
        out_specs=[spec] * 3,
        out_shape=[
            jax.ShapeDtypeStruct(q.shape, F32),
            jax.ShapeDtypeStruct(q.shape, BF16),
            jax.ShapeDtypeStruct(q.shape, F32),
        ],
        compiler_params=params(),
    )(q, k, v, q_code, k_code)


BLOCK = 256


def attention_backward_kernel(
    length, width, low_edge, high_edge, q, k, v, g, log_sum, delta, k_code, q_code, cos, sin, out, dq, dk, dv
):
    heads = width // HEAD
    row = pl.program_id(0)
    lane = lax.broadcasted_iota(jnp.int32, (BLOCK, width), 1) // HEAD
    dk[...] = jnp.zeros_like(dk)
    dv[...] = jnp.zeros_like(dv)

    def outer(i, carry):
        at = pl.ds(pl.multiple_of(i * BLOCK, BLOCK), BLOCK)
        queries = q[0, at, :] * 0.125
        grads = g[0, at, :]
        zero = jnp.zeros_like(queries)
        queries_of = [jnp.where(lane == h, queries, zero) for h in range(heads)]
        grads_of = [jnp.where(lane == h, grads, zero) for h in range(heads)]
        dq[...] = jnp.zeros_like(dq)

        def inner(j, carry):
            to = pl.ds(pl.multiple_of(j * BLOCK, BLOCK), BLOCK)
            keys, values = k[0, to, :], v[0, to, :]
            allowed = k_code[0, to, :] == q_code[0, :, at]
            dk_part, dv_part, dq_part = None, None, None
            for h in range(heads):
                keys_of = jnp.where(lane == h, keys, zero)
                scores = lax.dot_general(
                    keys, queries_of[h], (((1,), (1,)), ((), ())), preferred_element_type=F32
                )
                probs = jnp.where(allowed, jnp.exp(scores - log_sum[0, h : h + 1, at]), 0.0)
                grad_probs = lax.dot_general(
                    values, grads_of[h], (((1,), (1,)), ((), ())), preferred_element_type=F32
                )
                grad_scores = (probs * (grad_probs - delta[0, h : h + 1, at])).astype(BF16)
                a = jnp.dot(probs.astype(BF16), grads_of[h], preferred_element_type=F32)
                c = jnp.dot(grad_scores, queries_of[h], preferred_element_type=F32)
                e = lax.dot_general(
                    grad_scores, keys_of, (((0,), (0,)), ((), ())), preferred_element_type=F32
                )
                dv_part = a if h == 0 else dv_part + a
                dk_part = c if h == 0 else dk_part + c
                dq_part = e if h == 0 else dq_part + e
            dv[to, :] = dv[to, :] + dv_part
            dk[to, :] = dk[to, :] + dk_part
            dq[...] = dq[...] + dq_part
            return carry

        lax.fori_loop(low_edge[row, i], high_edge[row, i], inner, 0)
        grad = dq[...] * 0.125
        turned = grad * cos[0, at, :] - pair_swap(grad) * sin[0, at, :]
        out[0, at, 0:width] = turned.astype(BF16)
        return carry

    lax.fori_loop(0, length // BLOCK, outer, 0)

    def finish(i, carry):
        at = pl.ds(pl.multiple_of(i * BLOCK, BLOCK), BLOCK)
        grad = dk[at, :]
        turned = grad * cos[0, at, :] - pair_swap(grad) * sin[0, at, :]
        out[0, at, width : 2 * width] = turned.astype(BF16)
        out[0, at, 2 * width : 3 * width] = dv[at, :].astype(BF16)
        return carry

    lax.fori_loop(0, length // BLOCK, finish, 0)


def attention_backward(q, k, v, g, log_sum, delta, k_code, q_code, cos, sin, low_edge, high_edge):
    rows, length, width = q.shape

    def spec(shape):
        return pl.BlockSpec((1,) + tuple(shape[1:]), lambda r, *_: (r,) + (0,) * (len(shape) - 1))

    arrays = (q, k, v, g, log_sum, delta, k_code, q_code, cos, sin)
    out = (rows, length, 3 * width)
    return pl.pallas_call(
        functools.partial(attention_backward_kernel, length, width),
        grid_spec=pltpu.PrefetchScalarGridSpec(
            num_scalar_prefetch=2,
            grid=(rows,),
            in_specs=[spec(a.shape) for a in arrays],
            out_specs=spec(out),
            scratch_shapes=[
                pltpu.VMEM((BLOCK, width), F32),
                pltpu.VMEM((length, width), F32),
                pltpu.VMEM((length, width), F32),
            ],
        ),
        out_shape=jax.ShapeDtypeStruct(out, BF16),
        compiler_params=params(),
    )(low_edge, high_edge, *arrays)


def pick(ids, table, rows):
    value = table[SEGS - 1 : SEGS, :]
    for u in range(SEGS - 2, -1, -1):
        value = jnp.where(ids == u, table[u : u + 1, :], value)
    return jnp.broadcast_to(value, (rows, table.shape[1]))


def gelu_parts(v):
    c = 0.7978845608
    t = jnp.tanh(c * (v + 0.044715 * v * v * v))
    half = 0.5 * (1.0 + t)
    return v * half, half + 0.5 * v * (1.0 - t * t) * c * (1.0 + 0.134145 * v * v)


STEP = 32


def feed_kernel(
    rows,
    frames,
    part,
    att,
    embedded,
    late,
    ids,
    mod,
    cotangent,
    block_out,
    grad_att,
    grad_middle,
    sums,
    normed,
    low,
    grad_up,
    grad_feed,
    grad_branch,
    branch,
    middle,
    scale,
    bend,
    feed,
    grad_normed,
):
    tokens = rows * frames
    wide = 256
    per = wide // part

    def each_step(body):
        for r in range(rows):

            def step(i, carry, r=r):
                at = pl.ds(pl.multiple_of(r * frames + i * STEP, STEP), STEP)
                body(r, at)
                return carry

            lax.fori_loop(0, frames // STEP, step, 0)

    def gate(r, at, which):
        return pick(ids[at, :], mod[r, which], STEP)

    def columns(first, count, j):
        n = wide // count
        return late[j * n : (j + 1) * n, first : first + count, :].reshape(wide, D)

    for j in range(D // wide):
        branch[:, j * wide : (j + 1) * wide] = times_t(att[...], columns(0, part, j))

    def to_normed(r, at):
        value = embedded[at, :] + gate(r, at, 2) * branch[at, :]
        middle[at, :] = value
        centre = value - jnp.mean(value, axis=1, keepdims=True)
        factor = lax.rsqrt(jnp.mean(centre * centre, axis=1, keepdims=True) + EPSILON)
        hat = centre * factor
        scale[at, :] = jnp.broadcast_to(factor, (STEP, 128))
        normed[at, :] = (hat * (1.0 + gate(r, at, 4)) + gate(r, at, 3)).astype(BF16)

    each_step(to_normed)
    for j in range(2 * D // wide):
        lanes = slice(j * wide, (j + 1) * wide)
        value, slope = gelu_parts(times_t(normed[...], columns(part, 2 * part, j)))
        low[:, lanes] = value.astype(BF16)
        bend[:, lanes] = slope
    for j in range(D // wide):
        feed[:, j * wide : (j + 1) * wide] = times_t(
            low[:, :D], columns(3 * part, part, j)
        ) + times_t(low[:, D:], columns(4 * part, part, j))

    def to_out(r, at):
        gate_feed = gate(r, at, 5)
        block_out[at, :] = (middle[at, :] + gate_feed * feed[at, :]).astype(BF16)
        grad_feed[at, :] = (gate_feed * cotangent[at, :].astype(F32)).astype(BF16)

    each_step(to_out)

    def inner(first, count, lanes):
        return late[:, first : first + count, lanes].reshape(-1, wide)

    for half in range(2):
        for j in range(D // wide):
            lanes = slice(half * D + j * wide, half * D + (j + 1) * wide)
            weights = inner((3 + half) * part, part, slice(j * wide, (j + 1) * wide))
            grad_up[:, lanes] = (times(grad_feed[...], weights) * bend[:, lanes]).astype(BF16)
    for j in range(D // wide):
        lanes = slice(j * wide, (j + 1) * wide)
        grad_normed[:, lanes] = times(grad_up[...], inner(part, 2 * part, lanes))

    sums[...] = jnp.zeros_like(sums)

    def back(r, at):
        value = middle[at, :]
        factor = scale[at, 0:1]
        hat = (value - jnp.mean(value, axis=1, keepdims=True)) * factor
        grad = grad_normed[at, :]
        e = grad * (1.0 + gate(r, at, 4))
        out = cotangent[at, :].astype(F32)
        total = out + factor * (
            e
            - jnp.mean(e, axis=1, keepdims=True)
            - hat * jnp.mean(e * hat, axis=1, keepdims=True)
        )
        grad_middle[at, :] = total
        grad_branch[at, :] = (gate(r, at, 2) * total).astype(BF16)
        first = ids[at, :] == ids[r * frames : r * frames + 1, :]
        for k, part_sum in enumerate(
            (total * branch[at, :], grad, grad * hat, out * feed[at, :])
        ):
            kept = jnp.where(first, part_sum, 0.0)
            other = part_sum - kept
            for side, piece in enumerate((kept, other)):
                folded = piece[0:8]
                for q in range(1, STEP // 8):
                    folded = folded + piece[8 * q : 8 * q + 8]
                sums[r, side, k] = sums[r, side, k] + folded

    each_step(back)
    for j in range(D // wide):
        lanes = slice(j * wide, (j + 1) * wide)
        grad_att[:, lanes] = times(grad_branch[...], inner(0, part, lanes)).astype(BF16)


def feed_both(att, embedded, late, ids, mod, cotangent, rows, frames, part):
    tokens = rows * frames
    vmem = pl.BlockSpec(memory_space=pltpu.VMEM)

    def scratch(width):
        return pltpu.VMEM((tokens, width), F32)

    def out(width, dtype=BF16):
        return jax.ShapeDtypeStruct((tokens, width), dtype)

    return pl.pallas_call(
        functools.partial(feed_kernel, rows, frames, part),
        in_specs=[vmem] * 6,
        out_specs=[vmem] * 9,
        out_shape=[
            out(D),
            out(D),
            out(D, F32),
            jax.ShapeDtypeStruct((rows, 2, 4, 8, D), F32),
            out(D),
            out(2 * D),
            out(2 * D),
            out(D),
            out(D),
        ],
        scratch_shapes=[
            scratch(D),
            scratch(D),
            scratch(128),
            scratch(2 * D),
            scratch(D),
            scratch(D),
        ],
        compiler_params=params(),
    )(att, embedded, late, ids, mod, cotangent)


def lane_block(b, s, n, width):
    return pl.ds(pl.multiple_of(block_of(b, s, n) * width, 128), width)


def seat_rows(s, frames, first, count):
    return pl.ds(pl.multiple_of(s * frames + first, 16), count)


def norm_gather_task(bump_c, hidden, ids, mod, rows, frames):
    n = dims()[1]
    width = D // n
    half = frames // 2

    def body(ins, outs, scratch, b, s, nb, n):
        bump_in, hidden, ids, mod = ins
        embedded, o = outs
        bump, normed, send, recv, local, g_send, g_recv, g_local = scratch
        core, chip = lax.rem(s, 2), s // 2
        sibling = s + 1 - 2 * core
        flip_x = chip + 1 - 2 * lax.rem(chip, 2)
        flip_y = lax.rem(chip + 2, 4)
        seat_x, seat_y = 2 * flip_x + core, 2 * flip_y + core
        diagonal = 2 * lax.rem(flip_x + 2, 4) + core
        lanes = lane_block(b, s, n, width)
        swaps = {}
        for r in range(rows):
            for d in range(1, n):
                t = lax.rem(s + d, n)
                copy = remote(
                    bump_in.at[r, seat_rows(t, frames, 0, frames), :],
                    bump.at[r, :, lanes],
                    send.at[r, d],
                    recv.at[r, d],
                    seq=t,
                )
                copy.start()
                swaps[r, d] = copy
            copy = pltpu.make_async_copy(
                bump_in.at[r, seat_rows(s, frames, 0, frames), :], bump.at[r, :, lanes], local.at[r]
            )
            copy.start()
            swaps[r, 0] = copy
        yield
        parts = (pl.ds(0, half), pl.ds(half, half))
        pushes, near, far = {}, [], []

        def push(r, i, piece, source, target, fresh=False):
            where = o.at[r, source, parts[piece]]
            copy = remote(
                normed.at[r, parts[piece]] if fresh else where,
                where,
                g_send.at[r, i],
                g_recv.at[r, i],
                seq=target,
            )
            copy.start()
            return copy

        for r in range(rows):
            swaps[r, 0].wait()
            for d in range(1, n):
                swaps[r, d].wait_recv()

            def step(i, carry, r=r):
                inside = pl.ds(pl.multiple_of(i * STEP, STEP), STEP)
                at = pl.ds(pl.multiple_of(r * frames + i * STEP, STEP), STEP)
                value = hidden[at, :] + bump[r, inside, :].astype(F32)
                embedded[at, :] = value
                centre = value - jnp.mean(value, axis=1, keepdims=True)
                hat = centre * lax.rsqrt(
                    jnp.mean(centre * centre, axis=1, keepdims=True) + EPSILON
                )
                scale = pick(ids[at, :], mod[r, 1], STEP)
                shift = pick(ids[at, :], mod[r, 0], STEP)
                normed[r, inside, :] = (hat * (1.0 + scale) + shift).astype(BF16)
                return carry

            lax.fori_loop(0, frames // STEP, step, 0)
            pushes[r, "x0"] = push(r, 0, 0, s, seat_x, True)
            pushes[r, "y1"] = push(r, 1, 1, s, seat_y, True)
            pushes[r, "x1"] = push(r, 2, 1, s, seat_x, True)
            pushes[r, "y0"] = push(r, 3, 0, s, seat_y, True)
            near += [push(r, 4, 0, s, sibling, True), push(r, 5, 1, s, sibling, True)]
            copy = pltpu.make_async_copy(normed.at[r], o.at[r, s], g_local.at[r])
            copy.start()
            pushes[r, "own"] = copy
            yield
        for r in range(rows):
            pushes[r, "x0"].wait_recv()
            far.append(push(r, 6, 0, seat_x, seat_y))
            near.append(push(r, 7, 0, seat_x, sibling))
            pushes[r, "y1"].wait_recv()
            far.append(push(r, 8, 1, seat_y, seat_x))
            near.append(push(r, 9, 1, seat_y, sibling))
            pushes[r, "x1"].wait_recv()
            near.append(push(r, 10, 1, seat_x, sibling))
            pushes[r, "y0"].wait_recv()
            near.append(push(r, 11, 0, seat_y, sibling))
        for r in range(rows):
            far[2 * r].wait_recv()
            near.append(push(r, 12, 0, diagonal, sibling))
            far[2 * r + 1].wait_recv()
            near.append(push(r, 13, 1, diagonal, sibling))
        yield
        for r in range(rows):
            pushes[r, "own"].wait()
            for d in range(1, n):
                swaps[r, d].wait_send()
            for name in ("x0", "x1", "y0", "y1"):
                pushes[r, name].wait_send()
        for copy in far:
            copy.wait_send()
        for copy in near:
            copy.wait()

    vmem = pl.BlockSpec(memory_space=pltpu.VMEM)
    tokens = rows * frames
    return Task(
        [bump_c, hidden, ids, mod],
        [
            jax.ShapeDtypeStruct((tokens, D), F32),
            jax.ShapeDtypeStruct((rows, n, frames, D), BF16),
        ],
        [
            pltpu.VMEM((rows, frames, D), BF16),
            pltpu.VMEM((rows, frames, D), BF16),
            DMA((rows, n)),
            DMA((rows, n)),
            DMA((rows,)),
            DMA((rows, 14)),
            DMA((rows, 14)),
            DMA((rows,)),
        ],
        body,
        in_specs=[ANY, vmem, vmem, vmem],
        out_specs=[vmem, ANY],
    )


def fold_rows(piece):
    total = piece[0:8]
    for q in range(1, piece.shape[0] // 8):
        total = total + piece[8 * q : 8 * q + 8]
    return total


def sum_norm_task(partial, embedded, grad_middle, ids, mod, rows, frames):
    n = dims()[1]
    width = D // n
    half_len = frames // 2
    step = 16

    def body(ins, outs, scratch, b, s, nb, n):
        x, embedded, middle, ids, mod = ins
        grad, o, sums = outs
        mine, first, one, got_one, two, got_two, send, recv, local, low, c_send, c_recv, c_local = scratch
        copies = []
        sums[...] = jnp.zeros_like(sums)

        def value(half, whole_refs, half_refs, r, at):
            parts = [ref[r, pl.ds(half * half_len + at, step), :] for ref in whole_refs]
            parts += [ref[r, pl.ds(at, step), :] for ref in half_refs]
            result = parts[0].astype(F32)
            for p in parts[1:]:
                result = result + p.astype(F32)
            return result

        def each(work):
            def move(i, carry):
                at = pl.multiple_of(i * step, step)
                for r in range(rows):
                    work(r, at)
                return carry

            lax.fori_loop(0, half_len // step, move, 0)

        def add(target, half, whole_refs, half_refs):
            def work(r, at):
                target[r, pl.ds(at, step), :] = value(half, whole_refs, half_refs, r, at).astype(BF16)

            each(work)

        def finish(half, whole_refs, half_refs):
            def work(r, at):
                down = value(half, whole_refs, half_refs, r, at)
                where = pl.ds(pl.multiple_of(r * frames + half * half_len + at, step), step)
                field = embedded[where, :]
                centre = field - jnp.mean(field, axis=1, keepdims=True)
                factor = lax.rsqrt(jnp.mean(centre * centre, axis=1, keepdims=True) + EPSILON)
                hat = centre * factor
                e = down * (1.0 + pick(ids[where, :], mod[r, 1], step))
                result = middle[where, :] + factor * (
                    e
                    - jnp.mean(e, axis=1, keepdims=True)
                    - hat * jnp.mean(e * hat, axis=1, keepdims=True)
                )
                grad[where, :] = result
                low[r, pl.ds(half * half_len + at, step), :] = result.astype(BF16)
                begin = ids[where, :] == ids[r * frames : r * frames + 1, :]
                for k, part_sum in enumerate((down, down * hat)):
                    kept = jnp.where(begin, part_sum, 0.0)
                    sums[r, 0, k] = sums[r, 0, k] + fold_rows(kept)
                    sums[r, 1, k] = sums[r, 1, k] + fold_rows(part_sum - kept)

            each(work)
            rows_at = pl.ds(half * half_len, half_len)
            target = o.at[:, seat_rows(s, frames, half * half_len, half_len), :]
            for d in range(1, n):
                t = lax.rem(s + d, n)
                copy = remote(
                    low.at[:, rows_at, lane_block(b, t, n, width)],
                    target,
                    c_send.at[half, d],
                    c_recv.at[half, d],
                    seq=t,
                )
                copy.start()
                copies.append(copy)
            copy = pltpu.make_async_copy(
                low.at[:, rows_at, lane_block(b, s, n, width)], target, c_local.at[half]
            )
            copy.start()
            copies.append(copy)

        yield from quad_stages(
            s,
            x,
            mine,
            first,
            lambda ref, i: ref.at[:, i],
            one,
            got_one,
            two,
            got_two,
            (send, recv, local),
            add,
            finish,
        )
        for copy in copies:
            copy.wait()

    vmem = pl.BlockSpec(memory_space=pltpu.VMEM)
    tokens = rows * frames
    return Task(
        [partial, embedded, grad_middle, ids, mod],
        [
            jax.ShapeDtypeStruct((tokens, D), F32),
            jax.ShapeDtypeStruct((rows, n * frames, width), BF16),
            jax.ShapeDtypeStruct((rows, 2, 2, 8, D), F32),
        ],
        quad_scratch((rows, frames, D), (rows, half_len, D))
        + [pltpu.VMEM((rows, frames, D), BF16), DMA((2, n)), DMA((2, n)), DMA((2,))],
        body,
        in_specs=[ANY] + [vmem] * 4,
        out_specs=[vmem, ANY, vmem],
    )


def late_grads_task(att, grad_branch, grad_feed, low, grad_up, normed, ndev, part):
    def body(ins, outs, scratch, b, s, nb, n):
        yield
        late_work(*ins, outs[0], part)

    vmem = pl.BlockSpec(memory_space=pltpu.VMEM)
    return Task(
        [att, grad_branch, grad_feed, low, grad_up, normed],
        [jax.ShapeDtypeStruct((ndev, 5 * part, D), BF16)],
        [],
        body,
        in_specs=[vmem] * 6,
        out_specs=[vmem],
    )


def late_work(att, grad_branch, grad_feed, low, grad_up, normed, out, part):
    wide = 256
    per = wide // part
    for j in range(D // wide):
        lanes = slice(j * wide, (j + 1) * wide)
        out[j * per : (j + 1) * per, 0:part, :] = (
            rows_sum(grad_branch[:, lanes], att[...]).astype(BF16).reshape(per, part, D)
        )
        for half in range(2):
            out[j * per : (j + 1) * per, (3 + half) * part : (4 + half) * part, :] = (
                rows_sum(grad_feed[:, lanes], low[:, half * D : (half + 1) * D])
                .astype(BF16)
                .reshape(per, part, D)
            )
    for j in range(2 * D // wide):
        lanes = slice(j * wide, (j + 1) * wide)
        out[j * per // 2 : (j + 1) * per // 2, part : 3 * part, :] = (
            rows_sum(grad_up[:, lanes], normed[...]).astype(BF16).reshape(per // 2, 2 * part, D)
        )


def layer_norm(field):
    centre = field - jnp.mean(field, axis=-1, keepdims=True)
    return centre * lax.rsqrt(jnp.mean(centre * centre, axis=-1, keepdims=True) + EPSILON)


def modulate(field, scaling, shifting):
    return layer_norm(field) * (1.0 + scaling) + shifting


def gelu_curve(inputs):
    return jax.nn.gelu(inputs, approximate=True)


def by_segment(ids, table):
    value = table[:, SEGS - 1][:, None, :]
    for u in range(SEGS - 2, -1, -1):
        value = jnp.where(ids[:, :, None] == u, table[:, u][:, None, :], value)
    return value


def rope_tables(segment_ids, starts, width):
    length = segment_ids.shape[1]
    pairs = (np.arange(width) % HEAD) // 2
    freq = 10000.0 ** (-2.0 * pairs / HEAD)
    angle = np.arange(length)[:, None] * freq[None, :]
    cos_t = jnp.asarray(np.cos(angle).astype(np.float32))[None]
    sin_t = jnp.asarray(np.sin(angle).astype(np.float32))[None]
    offset = starts.astype(F32)[:, :, None] * jnp.asarray(freq.astype(np.float32))
    cos_o = by_segment(segment_ids, jnp.cos(offset))
    sin_o = by_segment(segment_ids, jnp.sin(offset))
    return cos_t * cos_o + sin_t * sin_o, sin_t * cos_o - cos_t * sin_o


def on_device(
    mel_inputs,
    text_ids,
    segment_ids,
    key_mask,
    time_index,
    input_proj,
    conv_first,
    conv_second,
    time_table,
    adaln_proj,
    qkv_proj,
    out_proj,
    up_proj,
    down_proj,
    text_table,
    grad_out,
):
    nb, n = dims()
    ndev = nb * n
    rows, frames = mel_inputs.shape[:2]
    tokens = rows * frames
    length = frames * n
    width = D // n
    part = D // ndev
    mine = lax.axis_index("seq")
    first_frame = mine * frames

    out_t, up_t, down_t = out_proj.T, up_proj.T, down_proj.T
    wide_t = jnp.concatenate([out_t, up_t, down_t[:, :D], down_t[:, D:]], axis=0)
    per = wide_t.shape[0]
    (
        (full_in,),
        (full_text,),
        (full_time,),
        (all_index,),
        (got_convs,),
    ) = transfer(
        [
            spread_task(input_proj.T),
            spread_task(text_table.T),
            spread_task(time_table.T),
            spread_task(time_index),
            columns_out_task(jnp.concatenate([conv_first, conv_second], axis=2)[None], True),
        ],
        0,
    )
    got_convs = got_convs[0]
    wide_t, _ = lax.optimization_barrier((wide_t, all_index))
    late = lax.all_gather(wide_t, ("batch", "seq"), axis=0, tiled=True).reshape(ndev, per, D)
    in_t = full_in.reshape(D, input_proj.shape[0])
    text_t = full_text.reshape(-1, VOCAB)
    time_t = full_time.reshape(D, STEPS)
    slot_steps = all_index[:, 0].reshape(nb * rows * SEGS)

    own_ids = lax.dynamic_slice_in_dim(segment_ids, first_frame, frames, 1)
    key_code = segment_ids + jnp.where(key_mask > 0, 0, 8)
    seg_column = key_code[:, :, None]
    seg_index = jnp.arange(SEGS, dtype=jnp.int32)
    starts = jnp.sum((segment_ids[:, None, :] < seg_index[None, :, None]).astype(jnp.int32), axis=2)

    text_hot = (
        text_ids.reshape(-1)[:, None] == jnp.arange(VOCAB, dtype=jnp.int32)[None, :]
    ).astype(BF16)
    text_embed = times_t(text_hot, text_t).astype(BF16)
    joined = jnp.concatenate([mel_inputs.reshape(tokens, 2 * MEL), text_embed], axis=1)
    hidden = times_t(joined, in_t).reshape(rows, frames, D)

    step_hot = (
        slot_steps[:, None] == jnp.arange(STEPS, dtype=jnp.int32)[None, :]
    ).astype(BF16)
    cond_value = times_t(step_hot, time_t)
    soft_cond = jax.nn.silu(cond_value).astype(BF16)
    own_mod = times(soft_cond, adaln_proj)
    task, arrange = to_channels(hidden.astype(BF16))
    got, (mod_got,) = transfer(
        [task, spray_task(own_mod.reshape(nb, rows * SEGS, 6 * part), True)], 2
    )
    hidden_c = arrange(got)
    modulation = mod_got.transpose(1, 0, 2).reshape(rows, SEGS, 6, D)
    mod_table = modulation.transpose(0, 2, 1, 3)
    ids_column = own_ids.reshape(tokens, 1)
    fused = n == 8 and width % 128 == 0
    shift_attn, scale_attn = (by_segment(own_ids, modulation[:, :, i]) for i in range(2))

    conv_one, conv_two, bump_c = conv_forward(hidden_c, seg_column, got_convs)
    qkv_task = columns_out_task(qkv_proj.T.reshape(3, part, D))
    if fused:
        (embedded, normed_all), (got_qkv,) = transfer(
            [
                norm_gather_task(
                    bump_c, hidden.reshape(tokens, D), ids_column, mod_table, rows, frames
                ),
                qkv_task,
            ],
            3,
        )
        embedded = embedded.reshape(rows, frames, D)
    else:
        task, arrange = to_frames(bump_c)
        bump = arrange(transfer([task], 3)[0])
        embedded = hidden + bump.astype(F32)
        normed = modulate(embedded, scale_attn, shift_attn).astype(BF16)
        (normed_all,), (got_qkv,) = transfer([gather_task(normed), qkv_task], 4)
    normed_all = normed_all.reshape(rows, length, D)
    qkv_t = got_qkv.reshape(3 * width, D)
    cos, sin = rope_tables(segment_ids, starts, width)
    query, key, value = qkv_forward(normed_all, qkv_t, cos, sin)
    attended, attended_low, log_lanes = attention_forward(
        query, key, value, seg_column, key_code[:, None, :]
    )
    task, arrange = to_frames(attended_low)
    attended_own = arrange(transfer([task], 5)[0])
    attended_own = attended_own.reshape(tokens, D)

    (
        block_out,
        grad_att,
        grad_middle,
        feed_sums,
        normed_feed,
        gelu_low,
        grad_up,
        grad_feed,
        grad_branch,
    ) = feed_both(
        attended_own,
        embedded.reshape(tokens, D),
        late,
        ids_column,
        mod_table,
        grad_out.reshape(tokens, D),
        rows,
        frames,
        part,
    )
    late_task = late_grads_task(
        attended_own, grad_branch, grad_feed, gelu_low, grad_up, normed_feed, ndev, part
    )
    block_out = block_out.reshape(rows, frames, D)
    grad_att = grad_att.reshape(rows, frames, D)
    grad_middle = grad_middle.reshape(rows, frames, D)
    task, arrange = to_channels(grad_att)
    grad_att_c = arrange(transfer([task], 6)[0])
    heads = width // HEAD
    delta = jnp.sum(
        (grad_att_c.astype(F32) * attended).reshape(rows, length, heads, HEAD), axis=3
    ).transpose(0, 2, 1)
    log_rows = log_lanes.reshape(rows, length, heads, HEAD)[:, :, :, 0].transpose(0, 2, 1)
    block_first_ids = segment_ids[:, ::BLOCK]
    block_last_ids = segment_ids[:, BLOCK - 1 :: BLOCK]
    ends = jnp.sum((segment_ids[:, None, :] <= seg_index[None, :, None]).astype(jnp.int32), axis=2)
    low_edge = (
        jnp.sum(jnp.where(block_first_ids[:, :, None] == seg_index, starts[:, None, :], 0), axis=2)
        // BLOCK
    )
    high_edge = (
        jnp.sum(jnp.where(block_last_ids[:, :, None] == seg_index, ends[:, None, :], 0), axis=2)
        + BLOCK
        - 1
    ) // BLOCK
    grad_projected = attention_backward(
        query,
        key,
        value,
        grad_att_c,
        log_rows,
        delta,
        seg_column,
        segment_ids[:, None, :],
        cos,
        sin,
        low_edge,
        high_edge,
    ).reshape(rows * length, 3 * width)
    grad_qkv = rows_sum(grad_projected, normed_all.reshape(rows * length, D)).astype(BF16)
    partial = times(grad_projected, qkv_t).astype(BF16).reshape(rows, n, frames, D)
    qkv_back = columns_back_task(grad_qkv.reshape(3, nb, part, D))
    if fused:
        (grad_embedded, grad_emb_c, attn_sums), (got_qkv_grads,), (late_grads,) = transfer(
            [
                sum_norm_task(
                    partial,
                    embedded.reshape(tokens, D),
                    grad_middle.reshape(tokens, D),
                    ids_column,
                    mod_table,
                    rows,
                    frames,
                ),
                qkv_back,
                late_task,
            ],
            7,
        )
        grad_embedded = grad_embedded.reshape(rows, frames, D)
        attn_sums = jnp.sum(attn_sums, axis=3)
        attn_sums = [attn_sums[:, :, 0], attn_sums[:, :, 1]]
    else:
        (grad_normed,), (got_qkv_grads,), (late_grads,) = transfer(
            [sum_task(partial), qkv_back, late_task], 7
        )
        grad_emb_part, grad_scale_attn, grad_shift_attn = jax.vjp(
            modulate, embedded, scale_attn, shift_attn
        )[1](grad_normed)
        grad_embedded = grad_middle + grad_emb_part
        task, arrange = to_channels(grad_embedded.astype(BF16))
        grad_emb_c = arrange(transfer([task], 10)[0])
    late_sum = lax.psum_scatter(
        late_grads, ("batch", "seq"), scatter_dimension=0, tiled=False
    ).astype(F32)

    first_ids, last_ids = own_ids[:, 0], own_ids[:, -1]
    if not fused:
        first = (own_ids == first_ids[:, None])[:, :, None]
        attn_sums = [
            jnp.stack(
                [jnp.sum(jnp.where(first, g, 0.0), axis=1), jnp.sum(jnp.where(first, 0.0, g), axis=1)],
                axis=1,
            )
            for g in (grad_shift_attn, grad_scale_attn)
        ]
    feed_sums = jnp.sum(feed_sums, axis=3)
    sides = jnp.concatenate(
        [attn_sums[0], attn_sums[1]] + [feed_sums[:, :, i] for i in range(4)], axis=2
    )
    is_first = (first_ids[:, None] == seg_index).astype(F32)
    is_last = (last_ids[:, None] == seg_index).astype(F32)
    local_sums = is_first[:, :, None] * sides[:, :1] + is_last[:, :, None] * sides[:, 1:]
    slots = rows * SEGS
    sums_out = local_sums.reshape(slots, ndev, 6 * part).transpose(1, 0, 2)
    grad_hidden_c, conv_sums = conv_backward(
        grad_emb_c, hidden_c, seg_column, conv_one, conv_two, got_convs, nb
    )
    task, arrange = to_frames(grad_hidden_c)
    got, (sums_got,), (got_conv_grads,) = transfer(
        [task, spray_task(sums_out, False), columns_back_task(conv_sums)], 11
    )
    grad_hidden_conv = arrange(got)
    sums_got = sums_got.reshape(nb, n, slots, 6 * part)
    grad_mod = jnp.sum(sums_got, axis=1).astype(BF16).reshape(nb * slots, 6 * part)
    grad_adaln = rows_sum(soft_cond, grad_mod)
    soft_part = times_t(grad_mod, adaln_proj)
    soft_out = soft_part.reshape(nb * slots, ndev, part).transpose(1, 0, 2)
    grad_convs = jnp.sum(got_conv_grads.astype(F32), axis=0)[0]
    grad_first, grad_second = grad_convs[..., :CHAN], grad_convs[..., CHAN:]
    grad_qkv_own = jnp.sum(got_qkv_grads.astype(F32), axis=0).reshape(3 * part, D).T

    grad_hidden = (grad_embedded + grad_hidden_conv.astype(F32)).astype(BF16).reshape(tokens, D)
    grad_input = rows_sum(grad_hidden, joined).astype(BF16)
    grad_joined = times(grad_hidden, in_t)
    grad_mels = grad_joined[:, : 2 * MEL].reshape(rows, frames, 2 * MEL)
    grad_embed = grad_joined[:, 2 * MEL :].astype(BF16)
    grad_text = rows_sum(grad_embed, text_hot).astype(BF16)
    scatter = quad_scatter_task if n == 8 and nb % 2 == 0 else scatter_task
    (in_sum,), (text_sum,), (soft_got,) = transfer(
        [
            scatter(grad_input.reshape(nb, n, part, -1)),
            scatter(grad_text.reshape(nb, n, -1, VOCAB)),
            spray_task(soft_out, False),
        ],
        13,
    )
    grad_soft = jnp.sum(soft_got, axis=0)
    own_cond = times(step_hot, time_table)
    grad_cond = jax.vjp(jax.nn.silu, own_cond)[1](grad_soft)[0]
    grad_time = jnp.dot(step_hot.astype(F32).T, grad_cond, precision=EXACT)
    grad_input_own = jnp.sum(in_sum.astype(F32), axis=0).T
    grad_text_own = jnp.sum(text_sum.astype(F32), axis=0).T
    grad_down_own = jnp.concatenate([late_sum[3 * part : 4 * part], late_sum[4 * part :]], axis=1)

    return (
        block_out,
        grad_mels,
        grad_input_own,
        grad_first,
        grad_second,
        grad_time,
        grad_adaln,
        grad_qkv_own,
        late_sum[:part].T,
        late_sum[part : 3 * part].T,
        grad_down_own.T,
        grad_text_own,
    )


def solution(mesh):
    frames = P("batch", "seq", None)
    columns = P(None, ("batch", "seq"))
    taps = P(None, ("batch", "seq"), None)
    in_specs = (
        frames,
        P("batch", "seq"),
        P("batch", None),
        P("batch", None),
        P("batch", None),
        columns,
        taps,
        taps,
        columns,
        columns,
        columns,
        columns,
        columns,
        columns,
        columns,
        frames,
    )
    out_specs = (
        frames,
        frames,
        columns,
        taps,
        taps,
        columns,
        columns,
        columns,
        columns,
        columns,
        columns,
        columns,
    )
    return jax.shard_map(
        on_device, mesh=mesh, in_specs=in_specs, out_specs=out_specs, check_vma=False
    )
```

```python
import functools

import jax
import jax.numpy as jnp
import numpy as np
from jax import lax
from jax.experimental import pallas as pl
from jax.experimental.pallas import tpu as pltpu
from jax.sharding import PartitionSpec as P

D = 1024
HEADS = 16
HEAD = 64
MEL = 100
VOCAB = 2546
KERNEL = 31
HALF = KERNEL // 2
CHAN = 64
STEPS = 32
SEGS = 4
GAP = 16
FOLD = 4
TAPS = KERNEL + FOLD - 1

EPSILON = 1e-06
MASKED = -1e30
EXACT = lax.Precision.HIGHEST
MESH = pl.DeviceIdType.MESH
ANY = pl.BlockSpec(memory_space=pl.ANY)
VMEM_LIMIT = 56 * 1024 * 1024
F32 = jnp.float32
BF16 = jnp.bfloat16


def dims():
    return lax.axis_size("batch"), lax.axis_size("seq")


def params(cid=None):
    if cid is None:
        return pltpu.CompilerParams(vmem_limit_bytes=VMEM_LIMIT)
    return pltpu.CompilerParams(
        collective_id=cid, has_side_effects=True, vmem_limit_bytes=VMEM_LIMIT
    )


def greet_all(nb, n, b, s):
    sem = pltpu.get_barrier_semaphore()
    me = b * n + s
    for d in range(1, nb * n):
        other = lax.rem(me + d, nb * n)
        pl.semaphore_signal(
            sem,
            inc=1,
            device_id={"batch": other // n, "seq": lax.rem(other, n)},
            device_id_type=MESH,
        )
    pl.semaphore_wait(sem, nb * n - 1)


def greet_group(n, s):
    sem = pltpu.get_barrier_semaphore()
    for d in range(1, n):
        pl.semaphore_signal(
            sem, inc=1, device_id={"seq": lax.rem(s + d, n)}, device_id_type=MESH
        )
    pl.semaphore_wait(sem, n - 1)


def block_of(b, s, n):
    chips, core = n // 2, lax.rem(s, 2)
    return 2 * lax.rem(s // 2 + b + (chips // 2) * core, chips) + core


def holder_of(b, m, n, nb):
    chips, core = n // 2, lax.rem(m, 2)
    turned = m // 2 + (nb + chips) * chips - b - (chips // 2) * core
    return 2 * lax.rem(turned, chips) + core


def remote(src, dst, send, recv, **where):
    return pltpu.make_async_remote_copy(
        src_ref=src,
        dst_ref=dst,
        send_sem=send,
        recv_sem=recv,
        device_id=where,
        device_id_type=MESH,
    )


class Task:
    def __init__(
        self, operands, outs, scratch, body, everyone=False, in_specs=None, out_specs=None
    ):
        self.operands, self.outs, self.scratch = list(operands), list(outs), list(scratch)
        self.body, self.everyone = body, everyone
        self.in_specs = in_specs or [ANY] * len(self.operands)
        self.out_specs = out_specs or [ANY] * len(self.outs)


def transfer_kernel(bodies, sizes, everyone, nb, n, *refs):
    b, s = lax.axis_index("batch"), lax.axis_index("seq")
    counts = [sum(size[i] for size in sizes) for i in range(3)]
    pools = [
        list(refs[: counts[0]]),
        list(refs[counts[0] : counts[0] + counts[1]]),
        list(refs[counts[0] + counts[1] :]),
    ]
    running = []
    for body, size in zip(bodies, sizes):
        taken = []
        for i in range(3):
            taken.append(pools[i][: size[i]])
            pools[i] = pools[i][size[i] :]
        running.append(body(*taken, b, s, nb, n))
    if everyone:
        greet_all(nb, n, b, s)
    else:
        greet_group(n, s)
    while running:
        left = []
        for task in running:
            try:
                next(task)
                left.append(task)
            except StopIteration:
                pass
        running = left


def transfer(tasks, cid):
    nb, n = dims()
    operands = [x for task in tasks for x in task.operands]
    outs = [x for task in tasks for x in task.outs]
    sizes = [(len(t.operands), len(t.outs), len(t.scratch)) for t in tasks]
    got = pl.pallas_call(
        functools.partial(
            transfer_kernel,
            [t.body for t in tasks],
            sizes,
            any(t.everyone for t in tasks),
            nb,
            n,
        ),
        out_shape=outs,
        in_specs=[x for task in tasks for x in task.in_specs],
        out_specs=[x for task in tasks for x in task.out_specs],
        scratch_shapes=[x for task in tasks for x in task.scratch],
        compiler_params=params(cid),
    )(*operands)
    got = list(got)
    result = []
    for size in sizes:
        result.append(got[: size[1]])
        got = got[size[1] :]
    return result


DMA = pltpu.SemaphoreType.DMA


def like(x, shape, dtype=None):
    return jax.ShapeDtypeStruct(tuple(shape), dtype or x.dtype)


def swap_task(x, shape, parts):
    n = dims()[1]

    def body(ins, outs, scratch, b, s, nb, n):
        send, recv, local = scratch
        src, dst = parts(ins[0], outs[0], b, s)
        copies = []
        for d in range(1, n):
            t = lax.rem(s + d, n)
            copy = remote(src(t), dst, send.at[d], recv.at[d], seq=t)
            copy.start()
            copies.append(copy)
        own = pltpu.make_async_copy(src(s), dst, local)
        own.start()
        copies.append(own)
        yield
        yield
        for copy in copies:
            copy.wait()

    return Task([x], [like(x, shape)], [DMA((n,)), DMA((n,)), DMA], body)


def to_channels(x):
    n = dims()[1]
    rows, frames = x.shape[:2]
    width = x.shape[2] // n
    if width % 128 == 0:

        def parts(x, o, b, s):
            first = pl.multiple_of(s * frames, 16)
            return (
                lambda t: x.at[
                    :, :, pl.ds(pl.multiple_of(block_of(b, t, n) * width, 128), width)
                ]
            ), o.at[:, pl.ds(first, frames), :]

        return swap_task(x, (rows, n * frames, width), parts), lambda got: got[0]

    def split_parts(x, o, b, s):
        return (lambda t: x.at[block_of(b, t, n)]), o.at[s]

    split = x.reshape(rows, frames, n, width).transpose(2, 0, 1, 3)
    return (
        swap_task(split, split.shape, split_parts),
        lambda got: got[0].transpose(1, 0, 2, 3).reshape(rows, n * frames, width),
    )


def to_frames(x):
    n = dims()[1]
    rows, length, width = x.shape
    frames = length // n
    if width % 128 == 0:

        def parts(x, o, b, s):
            first = pl.multiple_of(block_of(b, s, n) * width, 128)
            return (
                lambda t: x.at[:, pl.ds(pl.multiple_of(t * frames, 16), frames), :]
            ), o.at[:, :, pl.ds(first, width)]

        return swap_task(x, (rows, frames, n * width), parts), lambda got: got[0]

    def split_parts(x, o, b, s):
        return (lambda t: x.at[t]), o.at[block_of(b, s, n)]

    split = x.reshape(rows, n, frames, width).transpose(1, 0, 2, 3)
    return (
        swap_task(split, split.shape, split_parts),
        lambda got: got[0].transpose(1, 2, 0, 3).reshape(rows, frames, n * width),
    )


def spray_task(x, by_batch):
    nb, n = dims()
    ndev = nb * n

    def body(ins, outs, scratch, b, s, nb, n):
        send, recv, local = scratch
        x, o = ins[0], outs[0]
        me = b * n + s
        own = pltpu.make_async_copy(x.at[b if by_batch else me], o.at[me], local)
        own.start()
        copies = [own]
        for d in range(1, ndev):
            other = lax.rem(me + d, ndev)
            plane, where = other // n, lax.rem(other, n)
            copy = remote(
                x.at[plane if by_batch else other],
                o.at[me],
                send.at[d],
                recv.at[d],
                batch=plane,
                seq=where,
            )
            copy.start()
            copies.append(copy)
        yield
        yield
        for copy in copies:
            copy.wait()

    return Task(
        [x], [like(x, (ndev,) + x.shape[1:])], [DMA((ndev,)), DMA((ndev,)), DMA], body, True
    )


def gather_task(x):
    n = dims()[1]

    def body(ins, outs, scratch, b, s, nb, n):
        send, recv, local = scratch
        x, o = ins[0], outs[0]
        core = lax.rem(s, 2)
        sibling = s + 1 - 2 * core
        chips = n // 2
        far, near = [], []
        for d in range(1, chips):
            copy = remote(x, o.at[:, s], send.at[d], recv.at[d], seq=lax.rem(s + 2 * d, n))
            copy.start()
            far.append(copy)
        copy = remote(x, o.at[:, s], send.at[0], recv.at[0], seq=sibling)
        copy.start()
        near.append(copy)
        own = pltpu.make_async_copy(x, o.at[:, s], local)
        own.start()
        yield
        for d in range(1, chips):
            far[d - 1].wait_recv()
            source = lax.rem(s - 2 * d + n, n)
            copy = remote(
                o.at[:, source],
                o.at[:, source],
                send.at[chips + d],
                recv.at[chips + d],
                seq=sibling,
            )
            copy.start()
            near.append(copy)
        yield
        own.wait()
        for copy in far:
            copy.wait_send()
        for copy in near:
            copy.wait()

    out = like(x, (x.shape[0], n) + x.shape[1:])
    return Task([x], [out], [DMA((n,)), DMA((n,)), DMA], body)


def quad_gather_task(x):
    n = dims()[1]
    frames = x.shape[1]
    half = frames // 2

    def body(ins, outs, scratch, b, s, nb, n):
        send, recv, local = scratch
        x, o = ins[0], outs[0]
        core, chip = lax.rem(s, 2), s // 2
        sibling = s + 1 - 2 * core
        flip_x = chip + 1 - 2 * lax.rem(chip, 2)
        flip_y = lax.rem(chip + 2, 4)
        diagonal = lax.rem(flip_x + 2, 4)
        seat = lambda c: 2 * c + core
        parts = (pl.ds(0, half), pl.ds(half, half))
        k = iter(range(16))

        def push(piece, source, target):
            i = next(k)
            where = o.at[:, source, parts[piece]]
            copy = remote(
                x.at[:, parts[piece]] if source is s else where,
                where,
                send.at[i],
                recv.at[i],
                seq=target,
            )
            copy.start()
            return copy

        to_x = [push(p, s, seat(flip_x)) for p in (0, 1)]
        to_y = [push(p, s, seat(flip_y)) for p in (1, 0)]
        near = [push(p, s, sibling) for p in (0, 1)]
        own = pltpu.make_async_copy(x, o.at[:, s], local)
        own.start()
        yield
        far = []
        to_x[0].wait_recv()
        far.append(push(0, seat(flip_x), seat(flip_y)))
        near.append(push(0, seat(flip_x), sibling))
        to_y[0].wait_recv()
        far.append(push(1, seat(flip_y), seat(flip_x)))
        near.append(push(1, seat(flip_y), sibling))
        to_x[1].wait_recv()
        near.append(push(1, seat(flip_x), sibling))
        to_y[1].wait_recv()
        near.append(push(0, seat(flip_y), sibling))
        far[0].wait_recv()
        near.append(push(0, seat(diagonal), sibling))
        far[1].wait_recv()
        near.append(push(1, seat(diagonal), sibling))
        yield
        own.wait()
        for copy in to_x + to_y + far:
            copy.wait_send()
        for copy in near:
            copy.wait()

    out = like(x, (x.shape[0], n) + x.shape[1:])
    return Task([x], [out], [DMA((16,)), DMA((16,)), DMA], body)


def sum_task(x):
    n = dims()[1]
    rows, _, frames, width = x.shape
    chips = n // 2
    step = 16

    def body(ins, outs, scratch, b, s, nb, n):
        mine, first, passed, second, total, send, recv, local, out_sem = scratch
        x, o = ins[0], outs[0]
        core = lax.rem(s, 2)
        sibling = s + 1 - 2 * core
        chip = s // 2
        order = [lax.rem(chip + d, chips) for d in list(range(1, chips)) + [0]]
        pair, own, far = [], [], []
        for k, c in enumerate(order):
            copy = remote(
                x.at[:, 2 * c + 1 - core], first.at[k], send.at[k], recv.at[k], seq=sibling
            )
            copy.start()
            pair.append(copy)
            copy = pltpu.make_async_copy(x.at[:, 2 * c + core], mine.at[k], local.at[k])
            copy.start()
            own.append(copy)
        yield
        for k in range(chips):
            pair[k].wait_recv()
            own[k].wait()
            if k < chips - 1:

                def add(i, carry, k=k):
                    at = pl.ds(pl.multiple_of(i * step, step), step)
                    for r in range(rows):
                        passed[k, r, at, :] = (
                            mine[k, r, at, :].astype(F32) + first[k, r, at, :].astype(F32)
                        ).astype(BF16)
                    return carry

                lax.fori_loop(0, frames // step, add, 0)
                copy = remote(
                    passed.at[k],
                    second.at[k],
                    send.at[chips + k],
                    recv.at[chips + k],
                    seq=2 * order[k] + core,
                )
                copy.start()
                far.append(copy)
        yield
        for copy in far:
            copy.wait_recv()

        def finish(i, carry):
            at = pl.ds(pl.multiple_of(i * step, step), step)
            for r in range(rows):
                value = mine[chips - 1, r, at, :].astype(F32) + first[chips - 1, r, at, :].astype(F32)
                for k in range(chips - 1):
                    value = value + second[k, r, at, :].astype(F32)
                total[r, at, :] = value
            return carry

        lax.fori_loop(0, frames // step, finish, 0)
        out = pltpu.make_async_copy(total, o, out_sem)
        out.start()
        for copy in pair + far:
            copy.wait_send()
        out.wait()

    slots = pltpu.VMEM((chips, rows, frames, width), BF16)
    fewer = pltpu.VMEM((chips - 1, rows, frames, width), BF16)
    return Task(
        [x],
        [like(x, (rows, frames, width), F32)],
        [
            slots,
            slots,
            fewer,
            fewer,
            pltpu.VMEM((rows, frames, width), F32),
            DMA((n,)),
            DMA((n,)),
            DMA((chips,)),
            DMA,
        ],
        body,
    )


def quad_stages(s, x, mine, first, out, one, got_one, two, got_two, sems, add, total, rests=(0, 0, 0)):
    send, recv, local = sems
    core, chip = lax.rem(s, 2), s // 2
    sibling = s + 1 - 2 * core
    flip_x = chip + 1 - 2 * lax.rem(chip, 2)
    flip_y = lax.rem(chip + 2, 4)
    places = [flip_x, flip_y, lax.rem(flip_x + 2, 4), chip]
    sent, own = {}, {}
    for k in (2, 0, 1, 3):
        copy = remote(
            out(x, 2 * places[k] + 1 - core), first.at[k], send.at[k], recv.at[k], seq=sibling
        )
        copy.start()
        sent[k] = copy
        copy = pltpu.make_async_copy(out(x, 2 * places[k] + core), mine.at[k], local.at[k])
        copy.start()
        own[k] = copy
    yield
    for _ in range(rests[0]):
        yield
    across = (2 * flip_x + core, 2 * flip_y + core)
    stage = {}
    waited = set()

    def ready(k):
        if k not in waited:
            waited.add(k)
            sent[k].wait_recv()
            own[k].wait()

    for half, i, k in ((0, 1, 2), (1, 1, 2), (0, 0, 0), (1, 0, 1)):
        ready(k)
        add(one.at[half, i], half, [mine.at[k], first.at[k]], [])
        q = 4 + 2 * half + i
        copy = remote(
            one.at[half, i], got_one.at[half, i], send.at[q], recv.at[q], seq=across[half]
        )
        copy.start()
        stage[half, i] = copy
    yield
    for _ in range(rests[1]):
        yield
    for half in (0, 1):
        k = 1 - half
        ready(k)
        stage[half, 1].wait_recv()
        add(two.at[half], half, [mine.at[k], first.at[k]], [got_one.at[half, 1]])
        q = 8 + half
        copy = remote(two.at[half], got_two.at[half], send.at[q], recv.at[q], seq=across[1 - half])
        copy.start()
        stage[half, 2] = copy
    yield
    for _ in range(rests[2]):
        yield
    ready(3)
    for half in (0, 1):
        stage[half, 0].wait_recv()
        stage[half, 2].wait_recv()
        total(half, [mine.at[3], first.at[3]], [got_one.at[half, 0], got_two.at[half]])
    for copy in list(sent.values()) + list(stage.values()):
        copy.wait_send()


def quad_scratch(block, half):
    return [
        pltpu.VMEM((4,) + block, BF16),
        pltpu.VMEM((4,) + block, BF16),
        pltpu.VMEM((2, 2) + half, BF16),
        pltpu.VMEM((2, 2) + half, BF16),
        pltpu.VMEM((2,) + half, BF16),
        pltpu.VMEM((2,) + half, BF16),
        DMA((10,)),
        DMA((10,)),
        DMA((4,)),
    ]


def quad_sum_task(x):
    rows, _, frames, width = x.shape
    half_len = frames // 2
    step = 16

    def body(ins, outs, scratch, b, s, nb, n):
        mine, first, one, got_one, two, got_two, send, recv, local, total, out_sem = scratch

        def each(work):
            def move(i, carry):
                at = pl.multiple_of(i * step, step)
                for r in range(rows):
                    work(r, at)
                return carry

            lax.fori_loop(0, half_len // step, move, 0)

        def value(half, whole_refs, half_refs, r, at):
            parts = [ref[r, pl.ds(half * half_len + at, step), :] for ref in whole_refs]
            parts += [ref[r, pl.ds(at, step), :] for ref in half_refs]
            result = parts[0].astype(F32)
            for p in parts[1:]:
                result = result + p.astype(F32)
            return result

        def add(target, half, whole_refs, half_refs):
            def work(r, at):
                target[r, pl.ds(at, step), :] = value(half, whole_refs, half_refs, r, at).astype(BF16)

            each(work)

        def finish(half, whole_refs, half_refs):
            def work(r, at):
                total[r, pl.ds(half * half_len + at, step), :] = value(
                    half, whole_refs, half_refs, r, at
                )

            each(work)

        yield from quad_stages(
            s,
            ins[0],
            mine,
            first,
            lambda ref, i: ref.at[:, i],
            one,
            got_one,
            two,
            got_two,
            (send, recv, local),
            add,
            finish,
        )
        out = pltpu.make_async_copy(total, outs[0], out_sem)
        out.start()
        out.wait()

    return Task(
        [x],
        [like(x, (rows, frames, width), F32)],
        quad_scratch((rows, frames, width), (rows, half_len, width))
        + [pltpu.VMEM((rows, frames, width), F32), DMA],
        body,
    )


def quad_scatter_task(x, rests=(0, 0, 0), first_row=0, row_count=None):
    nb, n = dims()
    x_rows = row_count or x.shape[2]
    block = (nb, x_rows, x.shape[3])
    taken = pl.ds(first_row, x_rows)

    def body(ins, outs, scratch, b, s, nb, n):
        mine, first, one, got_one, two, got_two, send, recv, local = scratch[:9]
        total, z_send, z_recv, z_local = scratch[9:]
        o = outs[0]

        rows = x_rows
        step = 16 if rows % 16 == 0 else rows

        def value(half, whole_refs, half_refs, i, at):
            parts = [ref[half * (nb // 2) + i, at, :] for ref in whole_refs]
            parts += [ref[i, at, :] for ref in half_refs]
            result = parts[0].astype(F32)
            for p in parts[1:]:
                result = result + p.astype(F32)
            return result.astype(BF16)

        def each(work):
            def move(k, carry):
                if step == rows:
                    work(k, slice(None))
                else:
                    i, j = k // (rows // step), lax.rem(k, rows // step)
                    work(i, pl.ds(pl.multiple_of(j * step, step), step))
                return carry

            lax.fori_loop(0, (nb // 2) * (rows // step), move, 0)

        def add(target, half, whole_refs, half_refs):
            def work(i, at):
                target[i, at, :] = value(half, whole_refs, half_refs, i, at)

            each(work)

        def finish(half, whole_refs, half_refs):
            def work(i, at):
                total[half * (nb // 2) + i, at, :] = value(half, whole_refs, half_refs, i, at)

            each(work)

        yield from quad_stages(
            s,
            ins[0],
            mine,
            first,
            (lambda ref, i: ref.at[:, i]) if row_count is None else (lambda ref, i: ref.at[:, i, taken]),
            one,
            got_one,
            two,
            got_two,
            (send, recv, local),
            add,
            finish,
            rests,
        )
        last = []
        for d in range(1, nb):
            plane = lax.rem(b + d, nb)
            copy = remote(
                total.at[plane], o.at[b], z_send.at[d], z_recv.at[d], batch=plane, seq=s
            )
            copy.start()
            last.append(copy)
        copy = pltpu.make_async_copy(total.at[b], o.at[b], z_local)
        copy.start()
        last.append(copy)
        yield
        for copy in last:
            copy.wait()

    return Task(
        [x],
        [like(x, block)],
        quad_scratch(block, (nb // 2,) + block[1:])
        + [pltpu.VMEM(block, BF16), DMA((nb,)), DMA((nb,)), DMA],
        body,
        True,
    )


def spread_task(x):
    nb, n = dims()
    chips = n // 2

    def body(ins, outs, scratch, b, s, nb, n):
        z_send, z_recv, p_send, p_recv, c_send, c_recv, local = scratch
        x, o = ins[0], outs[0]
        core = lax.rem(s, 2)
        sibling = s + 1 - 2 * core
        own = pltpu.make_async_copy(x, o.at[b, s], local)
        own.start()
        along = []
        for d in range(1, nb):
            copy = remote(
                x, o.at[b, s], z_send.at[d], z_recv.at[d], batch=lax.rem(b + d, nb), seq=s
            )
            copy.start()
            along.append(copy)
        far, near = [], []

        def onward(d):
            plane = lax.rem(b - d + nb, nb)
            source = x if d == 0 else o.at[plane, s]
            for c in range(1, chips):
                copy = remote(
                    source,
                    o.at[plane, s],
                    p_send.at[d, c],
                    p_recv.at[d, c],
                    seq=lax.rem(s + 2 * c, n),
                )
                copy.start()
                far.append((d, c, plane, copy))
            copy = remote(source, o.at[plane, s], c_send.at[d, 0], c_recv.at[d, 0], seq=sibling)
            copy.start()
            near.append(copy)

        onward(0)
        yield
        for d in range(1, nb):
            along[d - 1].wait_recv()
            onward(d)
        yield
        for d, c, plane, copy in far:
            copy.wait_recv()
            source = lax.rem(s - 2 * c + n, n)
            last = remote(
                o.at[plane, source],
                o.at[plane, source],
                c_send.at[d, c],
                c_recv.at[d, c],
                seq=sibling,
            )
            last.start()
            near.append(last)
        yield
        own.wait()
        for copy in along:
            copy.wait_send()
        for entry in far:
            entry[3].wait_send()
        for copy in near:
            copy.wait()

    square = DMA((nb, chips))
    return Task(
        [x],
        [like(x, (nb, n) + x.shape)],
        [DMA((nb,)), DMA((nb,)), square, square, square, square, DMA],
        body,
        True,
    )


def columns_out_task(x, late=False):
    nb, n = dims()
    ndev = nb * n
    kinds = x.shape[0]

    def body(ins, outs, scratch, b, s, nb, n):
        send, recv = scratch
        x, o = ins[0], outs[0]
        me = b * n + s
        pieces = []
        for j in range(kinds):
            piece = kinds * me + j
            column = lax.rem(piece, ndev)
            pieces.append((j, piece // ndev, column // nb, lax.rem(column, nb)))
        if late:
            yield
        sent = []
        for j, part, block, slot in pieces:
            source, target, arrived = x.at[j], o.at[part, slot], recv.at[part, slot]
            for d in range(nb):
                plane = lax.rem(b + d, nb)
                owner = holder_of(plane, block, n, nb)
                if d == 0:

                    @pl.when(owner == s)
                    def _(source=source, target=target, arrived=arrived):
                        pltpu.make_async_copy(source, target, arrived).start()

                    @pl.when(owner != s)
                    def _(source=source, target=target, arrived=arrived, j=j, owner=owner):
                        remote(
                            source, target, send.at[j, 0], arrived, batch=b, seq=owner
                        ).start()
                else:
                    copy = remote(
                        source, target, send.at[j, d], arrived, batch=plane, seq=owner
                    )
                    copy.start()
                    sent.append(copy)
        yield
        yield
        yield
        for copy in sent:
            copy.wait_send()
        for j, part, block, slot in pieces:
            owner = holder_of(b, block, n, nb)

            @pl.when(owner != s)
            def _(j=j, part=part, slot=slot, owner=owner):
                remote(
                    x.at[j], o.at[part, slot], send.at[j, 0], recv.at[part, slot], batch=b, seq=owner
                ).wait_send()

        for p in range(kinds):
            for j in range(nb):
                pltpu.make_async_copy(x.at[0], o.at[p, j], recv.at[p, j]).wait()

    return Task(
        [x],
        [like(x, (kinds, nb) + x.shape[1:])],
        [DMA((kinds, nb)), DMA((kinds, nb))],
        body,
        True,
    )


def columns_back_task(x):
    nb, n = dims()
    ndev = nb * n
    kinds = x.shape[0]

    def body(ins, outs, scratch, b, s, nb, n):
        send, recv = scratch
        x, o = ins[0], outs[0]
        me = b * n + s
        pieces = []
        for p in range(kinds):
            for j in range(nb):
                column = p * ndev + block_of(b, s, n) * nb + j
                part = lax.rem(column, kinds)
                pieces.append(
                    (x.at[p, j], o.at[b, part], column // kinds, send.at[p, j], recv.at[b, part])
                )
        for source, target, owner, sent, arrived in pieces:

            @pl.when(owner == me)
            def _(source=source, target=target, arrived=arrived):
                pltpu.make_async_copy(source, target, arrived).start()

            @pl.when(owner != me)
            def _(source=source, target=target, owner=owner, sent=sent, arrived=arrived):
                remote(
                    source, target, sent, arrived, batch=owner // n, seq=lax.rem(owner, n)
                ).start()

        yield
        yield
        yield
        for source, target, owner, sent, arrived in pieces:

            @pl.when(owner != me)
            def _(source=source, target=target, owner=owner, sent=sent, arrived=arrived):
                remote(
                    source, target, sent, arrived, batch=owner // n, seq=lax.rem(owner, n)
                ).wait_send()

        for p in range(kinds):
            for j in range(nb):
                pltpu.make_async_copy(x.at[0, 0], o.at[j, p], recv.at[j, p]).wait()

    return Task(
        [x],
        [like(x, (nb, kinds) + x.shape[2:])],
        [DMA((kinds, nb)), DMA((nb, kinds))],
        body,
        True,
    )


def scatter_task(x):
    nb, n = dims()
    chips = n // 2

    def body(ins, outs, scratch, b, s, nb, n):
        mine, first, passed, second, total, send, recv, local, z_send, z_recv, z_local = scratch
        x, o = ins[0], outs[0]
        core = lax.rem(s, 2)
        sibling = s + 1 - 2 * core
        chip = s // 2
        order = [lax.rem(chip + d, chips) for d in list(range(1, chips)) + [0]]
        pair, own, far, last = [], [], [], []
        for k, c in enumerate(order):
            copy = remote(
                x.at[:, 2 * c + 1 - core], first.at[k], send.at[k], recv.at[k], seq=sibling
            )
            copy.start()
            pair.append(copy)
            copy = pltpu.make_async_copy(x.at[:, 2 * c + core], mine.at[k], local.at[k])
            copy.start()
            own.append(copy)
        yield
        for k in range(chips - 1):
            pair[k].wait_recv()
            own[k].wait()

            def add(i, carry, k=k):
                passed[k, i] = (mine[k, i].astype(F32) + first[k, i].astype(F32)).astype(BF16)
                return carry

            lax.fori_loop(0, nb, add, 0)
            copy = remote(
                passed.at[k],
                second.at[k],
                send.at[chips + k],
                recv.at[chips + k],
                seq=2 * order[k] + core,
            )
            copy.start()
            far.append(copy)
        yield
        pair[chips - 1].wait_recv()
        own[chips - 1].wait()
        for copy in far:
            copy.wait_recv()

        def finish(i, carry):
            value = mine[chips - 1, i].astype(F32) + first[chips - 1, i].astype(F32)
            for k in range(chips - 1):
                value = value + second[k, i].astype(F32)
            total[i] = value.astype(BF16)
            return carry

        lax.fori_loop(0, nb, finish, 0)
        for d in range(1, nb):
            plane = lax.rem(b + d, nb)
            copy = remote(
                total.at[plane], o.at[b], z_send.at[d], z_recv.at[d], batch=plane, seq=s
            )
            copy.start()
            last.append(copy)
        copy = pltpu.make_async_copy(total.at[b], o.at[b], z_local)
        copy.start()
        last.append(copy)
        yield
        for copy in pair + far:
            copy.wait_send()
        for copy in last:
            copy.wait()

    block = (nb,) + x.shape[2:]
    return Task(
        [x],
        [like(x, block)],
        [
            pltpu.VMEM((chips,) + block, BF16),
            pltpu.VMEM((chips,) + block, BF16),
            pltpu.VMEM((chips - 1,) + block, BF16),
            pltpu.VMEM((chips - 1,) + block, BF16),
            pltpu.VMEM(block, BF16),
            DMA((n,)),
            DMA((n,)),
            DMA((chips,)),
            DMA((nb,)),
            DMA((nb,)),
            DMA,
        ],
        body,
        True,
    )


def times(left, right):
    return lax.dot_general(left, right, (((1,), (0,)), ((), ())), preferred_element_type=F32)


def times_t(left, right):
    return lax.dot_general(left, right, (((1,), (1,)), ((), ())), preferred_element_type=F32)


def rows_sum(left, right):
    return lax.dot_general(left, right, (((0,), (0,)), ((), ())), preferred_element_type=F32)


def mish_parts(v):
    e = jnp.exp(jnp.minimum(v, 20.0))
    n = e * (e + 2.0)
    inverse = 1.0 / (n + 2.0)
    return e, n, inverse


def mish(v):
    e, n, inverse = mish_parts(v)
    return v * (n * inverse)


def mish_slope(v):
    e, n, inverse = mish_parts(v)
    return n * inverse + v * (4.0 * e * (1.0 + e)) * inverse * inverse


CHUNK = 128


def interleave(even, odd):
    low = lax.broadcasted_iota(jnp.int32, even.shape, 1) < CHAN
    return (
        jnp.where(low, even, pltpu.roll(odd, CHAN, 1)),
        jnp.where(low, pltpu.roll(even, CHAN, 1), odd),
    )


def to_groups(even, odd):
    if even.shape[1] == CHAN:
        return (jnp.concatenate([even, odd], axis=1),)
    return interleave(even, odd)


def to_pair(blocks):
    if len(blocks) == 1:
        return blocks[0][:, :CHAN], blocks[0][:, CHAN:]
    return interleave(*blocks)


def place(buf, source, seg, length):
    rows = buf.shape[0]

    def clear(i, carry):
        buf[pl.ds(pl.multiple_of(i * 16, 16), 16), :] = jnp.zeros((16, buf.shape[1]), F32)
        return carry

    lax.fori_loop(0, rows // 16, clear, 0)

    def move(i, carry):
        at = pl.multiple_of(i * CHUNK, CHUNK)
        value = source(at)
        ids = seg[0, pl.ds(at, CHUNK), :] & 7
        for u in range(SEGS):
            to = pl.ds(at + GAP * (u + 1), CHUNK)
            buf[to, :] = buf[to, :] + jnp.where(ids == u, value, 0.0)
        return carry

    lax.fori_loop(0, length // CHUNK, move, 0)


def unplace(buf, sink, seg, length):
    def move(i, carry):
        at = pl.multiple_of(i * CHUNK, CHUNK)
        ids = seg[0, pl.ds(at, CHUNK), :] & 7
        value = buf[pl.ds(at + GAP, CHUNK), :]
        for u in range(1, SEGS):
            value = jnp.where(ids == u, buf[pl.ds(at + GAP * (u + 1), CHUNK), :], value)
        sink[0, pl.ds(at, CHUNK), :] = value.astype(sink.dtype)
        return carry

    lax.fori_loop(0, length // CHUNK, move, 0)


def folded(buf, count, first):
    return buf[pl.ds(first, count, stride=FOLD), :]


def spread_taps(x, buf, count):
    for t in range(TAPS // 2):
        blocks = to_groups(folded(buf, count, 2 * t + 1), folded(buf, count, 2 * t + 2))
        for g, block in enumerate(blocks):
            x[g, :, 2 * CHAN * t : 2 * CHAN * (t + 1)] = block.astype(BF16)


def write_folded(buf, count, groups, value, live=None):
    for w in range(FOLD // 2):
        lanes = slice(2 * CHAN * w, 2 * CHAN * (w + 1))
        for half, part in enumerate(to_pair([value(g, lanes) for g in range(groups)])):
            at = pl.ds(GAP + 2 * w + half, count, stride=FOLD)
            buf[at, :] = part if live is None else part * live[at, :]


def fill_bands(bands, taps, groups, back):
    low = lax.broadcasted_iota(jnp.int32, (CHAN, 2 * CHAN), 1) < CHAN
    zero = jnp.zeros((CHAN, 2 * CHAN), F32)
    width = groups * CHAN

    def forms(k):
        if not 0 <= k < KERNEL:
            return None
        full = taps[:, KERNEL - 1 - k if back else k].astype(F32).reshape(width, 2 * CHAN)
        if back:
            full = full.T
            if groups == 1:
                full = jnp.concatenate([full, full], axis=1)
        turned = pltpu.roll(full, CHAN, 1)
        result = {}
        for c in range(2):
            for g in range(groups):
                if back:
                    rows, own = slice(c * CHAN, (c + 1) * CHAN), g
                else:
                    rows, own = slice(g * CHAN, (g + 1) * CHAN), c
                pair = (full[rows], turned[rows])
                result[c, g] = pair if own == 0 else pair[::-1]
        return result

    known = {}
    for tap in range(TAPS):
        known[tap] = forms(tap)
        known.pop(tap - FOLD, None)
        for w in range(FOLD // 2):
            left, right = known.get(tap - 2 * w), known.get(tap - 2 * w - 1)
            for c in range(2):
                for g in range(groups):
                    a = zero if left is None else left[c, g][0]
                    b = zero if right is None else right[c, g][1]
                    bands[
                        c, g, tap * CHAN : (tap + 1) * CHAN, 2 * CHAN * w : 2 * CHAN * (w + 1)
                    ] = jnp.where(low, a, b).astype(BF16)


FOLDED = FOLD * CHAN
DEPTH = TAPS * CHAN


def conv_forward_kernel(count, length, groups, u, seg, taps, c1, c2, out, buf, live, x, bands):
    @pl.when(pl.program_id(0) == 0)
    def _():
        fill_bands(bands, taps, groups, False)

    width = groups * CHAN
    place(live, lambda at: jnp.ones((CHUNK, width), F32), seg, length)
    place(buf, lambda at: u[0, pl.ds(at, CHUNK), :].astype(F32), seg, length)
    spread_taps(x, buf, count)
    for g in range(groups):
        c1[0, g] = times(x[g], bands[0, g])
    write_folded(buf, count, groups, lambda g, lanes: mish(c1[0, g, :, lanes]), live)
    spread_taps(x, buf, count)
    for g in range(groups):
        c2[0, g] = times(x[g], bands[1, g])
    write_folded(buf, count, groups, lambda g, lanes: mish(c2[0, g, :, lanes]))
    unplace(buf, out, seg, length)


def conv_sizes(length):
    count = -(-(length + GAP * (SEGS - 1)) // FOLD)
    count = -(-count // 16) * 16
    return count, FOLD * count + 48


def whole(shape):
    zeros = (0,) * len(shape)
    return pl.BlockSpec(shape, lambda *i: zeros)


def by_row(shape):
    return pl.BlockSpec((1,) + tuple(shape[1:]), lambda r: (r,) + (0,) * (len(shape) - 1))


def conv_forward(u, seg, taps):
    rows, length, width = u.shape
    groups = width // CHAN
    count, buffer = conv_sizes(length)
    kept = (rows, groups, count, FOLDED)
    return pl.pallas_call(
        functools.partial(conv_forward_kernel, count, length, groups),
        grid=(rows,),
        in_specs=[by_row(u.shape), by_row(seg.shape), whole(taps.shape)],
        out_specs=[by_row(kept), by_row(kept), by_row(u.shape)],
        out_shape=[
            jax.ShapeDtypeStruct(kept, F32),
            jax.ShapeDtypeStruct(kept, F32),
            jax.ShapeDtypeStruct(u.shape, BF16),
        ],
        scratch_shapes=[
            pltpu.VMEM((buffer, width), F32),
            pltpu.VMEM((buffer, width), F32),
            pltpu.VMEM((groups, count, DEPTH), BF16),
            pltpu.VMEM((2, groups, DEPTH, FOLDED), BF16),
        ],
        compiler_params=params(),
    )(u, seg, taps)


def weight_sums(even, odd, c, turned, x, groups):
    rows = slice(c * CHAN, (c + 1) * CHAN)
    blocks = TAPS // 2
    pair = 2 * CHAN
    for g in range(groups):
        for start in range(0, blocks, 2):
            stop = min(start + 2, blocks)
            product = times(turned[g], x[g, :, start * pair : stop * pair])
            for t in range(start, stop):
                part = product[:, (t - start) * pair : (t - start + 1) * pair]
                for m in range(FOLD):
                    to = t - m // 2
                    if 0 <= to < 16:
                        sums = odd if m % 2 else even
                        sums[g, to, rows] = sums[g, to, rows] + part[m * CHAN : (m + 1) * CHAN]


def conv_chain(
    d, seg, c1, c2, dh, buf, grads, live, x, turned2, turned1, bands, count, length, groups
):
    width = groups * CHAN
    place(live, lambda at: jnp.ones((CHUNK, width), F32), seg, length)
    place(grads, lambda at: d[0, pl.ds(at, CHUNK), :].astype(F32), seg, length)

    def slope(kept, turned, scaled):
        values = {}
        for w in range(FOLD // 2):
            lanes = slice(2 * CHAN * w, 2 * CHAN * (w + 1))
            for g in range(groups):
                value = scaled(g, w, lanes) * mish_slope(kept[0, g, :, lanes])
                values[g, w] = value
                turned[g, lanes, :] = value.T.astype(BF16)
        write_folded(grads, count, groups, lambda g, lanes: values[g, lanes.start // (2 * CHAN)])

    def both(source, g, w):
        return to_groups(
            folded(source, count, GAP + 2 * w), folded(source, count, GAP + 2 * w + 1)
        )[g]

    slope(c2, turned2, lambda g, w, lanes: both(grads, g, w))
    yield
    spread_taps(x, grads, count)
    back = [times(x[g], bands[1, g]) for g in range(groups)]
    slope(c1, turned1, lambda g, w, lanes: back[g][:, lanes] * both(live, g, w))
    yield
    spread_taps(x, grads, count)
    last = [times(x[g], bands[0, g]) for g in range(groups)]
    write_folded(buf, count, groups, lambda g, lanes: last[g][:, lanes])
    unplace(buf, dh, seg, length)


def conv_weights(
    u, seg, c1, buf, live, x, turned2, turned1, even, odd, count, length, groups
):
    width = groups * CHAN
    place(live, lambda at: jnp.ones((CHUNK, width), F32), seg, length)
    for i in range(0, GAP, 8):
        buf[i : i + 8, :] = jnp.zeros((8, width), F32)
    for i in range(GAP + FOLD * count, buf.shape[0], 8):
        buf[i : i + 8, :] = jnp.zeros((8, width), F32)
    write_folded(buf, count, groups, lambda g, lanes: mish(c1[0, g, :, lanes]), live)
    spread_taps(x, buf, count)
    weight_sums(even, odd, 1, turned2, x, groups)
    yield
    place(buf, lambda at: u[0, pl.ds(at, CHUNK), :].astype(F32), seg, length)
    spread_taps(x, buf, count)
    weight_sums(even, odd, 0, turned1, x, groups)


def conv_pieces(pieces, even, odd, groups, nb):
    low = lax.broadcasted_iota(jnp.int32, (2 * CHAN, 2 * CHAN), 1) < CHAN
    part = groups * CHAN // nb
    each = CHAN // part
    for g in range(groups):
        for p in range(16):
            left = pltpu.roll(odd[g, p], CHAN, 1)
            right = pltpu.roll(odd[g, p + 1], CHAN, 1) if p < 15 else left
            total = (even[g, p] + jnp.where(low, left, right)).T.astype(BF16)
            for half in range(2):
                k = 2 * p + half
                if k < KERNEL:
                    for j in range(each):
                        first = half * CHAN + j * part
                        pieces[0, g * each + j, k] = total[first : first + part]


def conv_backward_kernel(
    count, length, groups, nb, d, u, seg, c1, c2, taps, dh, pieces, buf, grads, live, x, turned2, turned1, bands, even, odd
):
    row = pl.program_id(0)

    @pl.when(row == 0)
    def _():
        fill_bands(bands, taps, groups, True)
        even[...] = jnp.zeros_like(even)
        odd[...] = jnp.zeros_like(odd)

    for _ in conv_chain(
        d, seg, c1, c2, dh, buf, grads, live, x, turned2, turned1, bands, count, length, groups
    ):
        pass
    for _ in conv_weights(
        u, seg, c1, buf, live, x, turned2, turned1, even, odd, count, length, groups
    ):
        pass

    @pl.when(row == pl.num_programs(0) - 1)
    def _():
        conv_pieces(pieces, even, odd, groups, nb)


def conv_backward(d, u, seg, c1, c2, taps, nb):
    rows, length, width = u.shape
    groups = width // CHAN
    count, buffer = conv_sizes(length)
    pieces = (1, nb, KERNEL, width // nb, 2 * CHAN)
    sums = pltpu.VMEM((groups, 16, 2 * CHAN, 2 * CHAN), F32)
    frames = pltpu.VMEM((buffer, width), F32)
    return pl.pallas_call(
        functools.partial(conv_backward_kernel, count, length, groups, nb),
        grid=(rows,),
        in_specs=[
            by_row(d.shape),
            by_row(u.shape),
            by_row(seg.shape),
            by_row(c1.shape),
            by_row(c2.shape),
            whole(taps.shape),
        ],
        out_specs=[by_row(u.shape), whole(pieces)],
        out_shape=[
            jax.ShapeDtypeStruct(u.shape, BF16),
            jax.ShapeDtypeStruct(pieces, BF16),
        ],
        scratch_shapes=[
            frames,
            frames,
            frames,
            pltpu.VMEM((groups, count, DEPTH), BF16),
            pltpu.VMEM((groups, FOLDED, count), BF16),
            pltpu.VMEM((groups, FOLDED, count), BF16),
            pltpu.VMEM((2, groups, DEPTH, FOLDED), BF16),
            sums,
            sums,
        ],
        compiler_params=params(),
    )(d, u, seg, c1, c2, taps)


def pair_swap(x):
    width = x.shape[1]
    if width % 128:
        x = jnp.concatenate([x, x], axis=1)
    lane = lax.broadcasted_iota(jnp.int32, x.shape, 1)
    after = pltpu.roll(x, x.shape[1] - 1, 1)
    before = pltpu.roll(x, 1, 1)
    return jnp.where(lax.rem(lane, 2) == 0, -after, before)[:, :width]


def qkv_kernel(width, x, w, cos, sin, q, k, v):
    got = lax.dot_general(
        x[0], w[...], (((1,), (1,)), ((), ())), preferred_element_type=F32
    )
    for p, out in enumerate((q, k)):
        part = got[:, p * width : (p + 1) * width]
        out[0] = (part * cos[0] + pair_swap(part) * sin[0]).astype(BF16)
    v[0] = got[:, 2 * width :].astype(BF16)


def qkv_forward(x, w, cos, sin):
    rows, length, depth = x.shape
    width = w.shape[0] // 3
    block = 512
    spec = pl.BlockSpec((1, block, width), lambda r, i: (r, i, 0))
    shape = jax.ShapeDtypeStruct((rows, length, width), BF16)
    return pl.pallas_call(
        functools.partial(qkv_kernel, width),
        grid=(rows, length // block),
        in_specs=[
            pl.BlockSpec((1, block, depth), lambda r, i: (r, i, 0)),
            whole(w.shape),
            spec,
            spec,
        ],
        out_specs=[spec] * 3,
        out_shape=[shape] * 3,
        compiler_params=params(),
    )(x, w, cos, sin)


def attention_forward_kernel(width, q, k, v, q_code, k_code, out, low, log_sum):
    heads = width // HEAD
    lane = lax.broadcasted_iota(jnp.int32, q.shape[1:], 1) // HEAD
    allowed = (q_code[0] & 7) == k_code[0]
    queries = q[0] * 0.125
    result, logs = None, None
    for h in range(heads):
        chosen = jnp.where(lane == h, queries, jnp.zeros_like(queries))
        scores = lax.dot_general(
            chosen, k[0], (((1,), (1,)), ((), ())), preferred_element_type=F32
        )
        scores = jnp.where(allowed, scores, MASKED)
        peak = jnp.max(scores, axis=1, keepdims=True)
        weights = jnp.exp(scores - peak)
        total = jnp.sum(weights, axis=1, keepdims=True)
        value = jnp.dot(weights.astype(BF16), v[0], preferred_element_type=F32) / total
        log = jnp.broadcast_to(peak + jnp.log(total), value.shape)
        result = value if h == 0 else jnp.where(lane == h, value, result)
        logs = log if h == 0 else jnp.where(lane == h, log, logs)
    out[0] = result
    low[0] = result.astype(BF16)
    log_sum[0] = logs


def attention_forward(q, k, v, q_code, k_code):
    rows, length, width = q.shape
    block = 256
    spec = pl.BlockSpec((1, block, width), lambda r, i: (r, i, 0))
    row = pl.BlockSpec((1, length, width), lambda r, i: (r, 0, 0))
    return pl.pallas_call(
        functools.partial(attention_forward_kernel, width),
        grid=(rows, length // block),
        in_specs=[
            spec,
            row,
            row,
            pl.BlockSpec((1, block, 1), lambda r, i: (r, i, 0)),
            pl.BlockSpec((1, 1, length), lambda r, i: (r, 0, 0)),
        ],
        out_specs=[spec] * 3,
        out_shape=[
            jax.ShapeDtypeStruct(q.shape, F32),
            jax.ShapeDtypeStruct(q.shape, BF16),
            jax.ShapeDtypeStruct(q.shape, F32),
        ],
        compiler_params=params(),
    )(q, k, v, q_code, k_code)


BLOCK = 256


def attention_backward_kernel(
    length, width, low_edge, high_edge, q, k, v, g, log_sum, delta, k_code, q_code, cos, sin, out, dq, dk, dv
):
    heads = width // HEAD
    row = pl.program_id(0)
    lane = lax.broadcasted_iota(jnp.int32, (BLOCK, width), 1) // HEAD
    dk[...] = jnp.zeros_like(dk)
    dv[...] = jnp.zeros_like(dv)

    def outer(i, carry):
        at = pl.ds(pl.multiple_of(i * BLOCK, BLOCK), BLOCK)
        queries = q[0, at, :] * 0.125
        grads = g[0, at, :]
        zero = jnp.zeros_like(queries)
        queries_of = [jnp.where(lane == h, queries, zero) for h in range(heads)]
        grads_of = [jnp.where(lane == h, grads, zero) for h in range(heads)]
        dq[...] = jnp.zeros_like(dq)

        def inner(j, carry):
            to = pl.ds(pl.multiple_of(j * BLOCK, BLOCK), BLOCK)
            keys, values = k[0, to, :], v[0, to, :]
            allowed = k_code[0, to, :] == q_code[0, :, at]
            dk_part, dv_part, dq_part = None, None, None
            for h in range(heads):
                keys_of = jnp.where(lane == h, keys, zero)
                scores = lax.dot_general(
                    keys, queries_of[h], (((1,), (1,)), ((), ())), preferred_element_type=F32
                )
                probs = jnp.where(allowed, jnp.exp(scores - log_sum[0, h : h + 1, at]), 0.0)
                grad_probs = lax.dot_general(
                    values, grads_of[h], (((1,), (1,)), ((), ())), preferred_element_type=F32
                )
                grad_scores = (probs * (grad_probs - delta[0, h : h + 1, at])).astype(BF16)
                a = jnp.dot(probs.astype(BF16), grads_of[h], preferred_element_type=F32)
                c = jnp.dot(grad_scores, queries_of[h], preferred_element_type=F32)
                e = lax.dot_general(
                    grad_scores, keys_of, (((0,), (0,)), ((), ())), preferred_element_type=F32
                )
                dv_part = a if h == 0 else dv_part + a
                dk_part = c if h == 0 else dk_part + c
                dq_part = e if h == 0 else dq_part + e
            dv[to, :] = dv[to, :] + dv_part
            dk[to, :] = dk[to, :] + dk_part
            dq[...] = dq[...] + dq_part
            return carry

        lax.fori_loop(low_edge[row, i], high_edge[row, i], inner, 0)
        grad = dq[...] * 0.125
        turned = grad * cos[0, at, :] - pair_swap(grad) * sin[0, at, :]
        out[0, at, 0:width] = turned.astype(BF16)
        return carry

    lax.fori_loop(0, length // BLOCK, outer, 0)

    def finish(i, carry):
        at = pl.ds(pl.multiple_of(i * BLOCK, BLOCK), BLOCK)
        grad = dk[at, :]
        turned = grad * cos[0, at, :] - pair_swap(grad) * sin[0, at, :]
        out[0, at, width : 2 * width] = turned.astype(BF16)
        out[0, at, 2 * width : 3 * width] = dv[at, :].astype(BF16)
        return carry

    lax.fori_loop(0, length // BLOCK, finish, 0)


def attention_backward(q, k, v, g, log_sum, delta, k_code, q_code, cos, sin, low_edge, high_edge):
    rows, length, width = q.shape

    def spec(shape):
        return pl.BlockSpec((1,) + tuple(shape[1:]), lambda r, *_: (r,) + (0,) * (len(shape) - 1))

    arrays = (q, k, v, g, log_sum, delta, k_code, q_code, cos, sin)
    out = (rows, length, 3 * width)
    return pl.pallas_call(
        functools.partial(attention_backward_kernel, length, width),
        grid_spec=pltpu.PrefetchScalarGridSpec(
            num_scalar_prefetch=2,
            grid=(rows,),
            in_specs=[spec(a.shape) for a in arrays],
            out_specs=spec(out),
            scratch_shapes=[
                pltpu.VMEM((BLOCK, width), F32),
                pltpu.VMEM((length, width), F32),
                pltpu.VMEM((length, width), F32),
            ],
        ),
        out_shape=jax.ShapeDtypeStruct(out, BF16),
        compiler_params=params(),
    )(low_edge, high_edge, *arrays)


def pick(ids, table, rows):
    value = table[SEGS - 1 : SEGS, :]
    for u in range(SEGS - 2, -1, -1):
        value = jnp.where(ids == u, table[u : u + 1, :], value)
    return jnp.broadcast_to(value, (rows, table.shape[1]))


def gelu_parts(v):
    c = 0.7978845608
    t = jnp.tanh(c * (v + 0.044715 * v * v * v))
    half = 0.5 * (1.0 + t)
    return v * half, half + 0.5 * v * (1.0 - t * t) * c * (1.0 + 0.134145 * v * v)


STEP = 32
LATE_RESTS = ((0, 1, 3), (0, 2, 3), (1, 3, 2), (1, 4, 2))


def feed_kernel(
    rows,
    frames,
    part,
    att,
    embedded,
    late,
    ids,
    mod,
    cotangent,
    block_out,
    grad_att,
    grad_middle,
    sums,
    normed,
    low,
    grad_up,
    grad_feed,
    grad_branch,
    branch,
    middle,
    scale,
    bend,
    feed,
    grad_normed,
):
    tokens = rows * frames
    wide = 256
    per = wide // part

    def each_step(body):
        for r in range(rows):

            def step(i, carry, r=r):
                at = pl.ds(pl.multiple_of(r * frames + i * STEP, STEP), STEP)
                body(r, at)
                return carry

            lax.fori_loop(0, frames // STEP, step, 0)

    def gate(r, at, which):
        return pick(ids[at, :], mod[r, which], STEP)

    def columns(first, count, j):
        n = wide // count
        return late[j * n : (j + 1) * n, first : first + count, :].reshape(wide, D)

    for j in range(D // wide):
        branch[:, j * wide : (j + 1) * wide] = times_t(att[...], columns(0, part, j))

    def to_normed(r, at):
        value = embedded[at, :] + gate(r, at, 2) * branch[at, :]
        middle[at, :] = value
        centre = value - jnp.mean(value, axis=1, keepdims=True)
        factor = lax.rsqrt(jnp.mean(centre * centre, axis=1, keepdims=True) + EPSILON)
        hat = centre * factor
        scale[at, :] = jnp.broadcast_to(factor, (STEP, 128))
        normed[at, :] = (hat * (1.0 + gate(r, at, 4)) + gate(r, at, 3)).astype(BF16)

    each_step(to_normed)
    for j in range(2 * D // wide):
        lanes = slice(j * wide, (j + 1) * wide)
        value, slope = gelu_parts(times_t(normed[...], columns(part, 2 * part, j)))
        low[:, lanes] = value.astype(BF16)
        bend[:, lanes] = slope
    for j in range(D // wide):
        feed[:, j * wide : (j + 1) * wide] = times_t(
            low[:, :D], columns(3 * part, part, j)
        ) + times_t(low[:, D:], columns(4 * part, part, j))

    def to_out(r, at):
        gate_feed = gate(r, at, 5)
        block_out[at, :] = (middle[at, :] + gate_feed * feed[at, :]).astype(BF16)
        grad_feed[at, :] = (gate_feed * cotangent[at, :].astype(F32)).astype(BF16)

    each_step(to_out)

    def inner(first, count, lanes):
        return late[:, first : first + count, lanes].reshape(-1, wide)

    for half in range(2):
        for j in range(D // wide):
            lanes = slice(half * D + j * wide, half * D + (j + 1) * wide)
            weights = inner((3 + half) * part, part, slice(j * wide, (j + 1) * wide))
            grad_up[:, lanes] = (times(grad_feed[...], weights) * bend[:, lanes]).astype(BF16)
    for j in range(D // wide):
        lanes = slice(j * wide, (j + 1) * wide)
        grad_normed[:, lanes] = times(grad_up[...], inner(part, 2 * part, lanes))

    sums[...] = jnp.zeros_like(sums)

    def back(r, at):
        value = middle[at, :]
        factor = scale[at, 0:1]
        hat = (value - jnp.mean(value, axis=1, keepdims=True)) * factor
        grad = grad_normed[at, :]
        e = grad * (1.0 + gate(r, at, 4))
        out = cotangent[at, :].astype(F32)
        total = out + factor * (
            e
            - jnp.mean(e, axis=1, keepdims=True)
            - hat * jnp.mean(e * hat, axis=1, keepdims=True)
        )
        grad_middle[at, :] = total
        grad_branch[at, :] = (gate(r, at, 2) * total).astype(BF16)
        first = ids[at, :] == ids[r * frames : r * frames + 1, :]
        for k, part_sum in enumerate(
            (total * branch[at, :], grad, grad * hat, out * feed[at, :])
        ):
            kept = jnp.where(first, part_sum, 0.0)
            other = part_sum - kept
            for side, piece in enumerate((kept, other)):
                folded = piece[0:8]
                for q in range(1, STEP // 8):
                    folded = folded + piece[8 * q : 8 * q + 8]
                sums[r, side, k] = sums[r, side, k] + folded

    each_step(back)
    for j in range(D // wide):
        lanes = slice(j * wide, (j + 1) * wide)
        grad_att[:, lanes] = times(grad_branch[...], inner(0, part, lanes)).astype(BF16)


def feed_both(att, embedded, late, ids, mod, cotangent, rows, frames, part):
    tokens = rows * frames
    vmem = pl.BlockSpec(memory_space=pltpu.VMEM)

    def scratch(width):
        return pltpu.VMEM((tokens, width), F32)

    def out(width, dtype=BF16):
        return jax.ShapeDtypeStruct((tokens, width), dtype)

    return pl.pallas_call(
        functools.partial(feed_kernel, rows, frames, part),
        in_specs=[vmem] * 6,
        out_specs=[vmem] * 9,
        out_shape=[
            out(D),
            out(D),
            out(D, F32),
            jax.ShapeDtypeStruct((rows, 2, 4, 8, D), F32),
            out(D),
            out(2 * D),
            out(2 * D),
            out(D),
            out(D),
        ],
        scratch_shapes=[
            scratch(D),
            scratch(D),
            scratch(128),
            scratch(2 * D),
            scratch(D),
            scratch(D),
        ],
        compiler_params=params(),
    )(att, embedded, late, ids, mod, cotangent)


def lane_block(b, s, n, width):
    return pl.ds(pl.multiple_of(block_of(b, s, n) * width, 128), width)


def seat_rows(s, frames, first, count):
    return pl.ds(pl.multiple_of(s * frames + first, 16), count)


def norm_gather_task(bump_c, hidden, ids, mod, rows, frames):
    n = dims()[1]
    width = D // n
    half = frames // 2

    def body(ins, outs, scratch, b, s, nb, n):
        bump_in, hidden, ids, mod = ins
        embedded, o = outs
        bump, normed, send, recv, local, g_send, g_recv, g_local = scratch
        core, chip = lax.rem(s, 2), s // 2
        sibling = s + 1 - 2 * core
        flip_x = chip + 1 - 2 * lax.rem(chip, 2)
        flip_y = lax.rem(chip + 2, 4)
        seat_x, seat_y = 2 * flip_x + core, 2 * flip_y + core
        diagonal = 2 * lax.rem(flip_x + 2, 4) + core
        lanes = lane_block(b, s, n, width)
        swaps = {}
        for r in range(rows):
            for d in range(1, n):
                t = lax.rem(s + d, n)
                copy = remote(
                    bump_in.at[r, seat_rows(t, frames, 0, frames), :],
                    bump.at[r, :, lanes],
                    send.at[r, d],
                    recv.at[r, d],
                    seq=t,
                )
                copy.start()
                swaps[r, d] = copy
            copy = pltpu.make_async_copy(
                bump_in.at[r, seat_rows(s, frames, 0, frames), :], bump.at[r, :, lanes], local.at[r]
            )
            copy.start()
            swaps[r, 0] = copy
        yield
        parts = (pl.ds(0, half), pl.ds(half, half))
        pushes, near, far = {}, [], []

        def push(r, i, piece, source, target, fresh=False):
            where = o.at[r, source, parts[piece]]
            copy = remote(
                normed.at[r, parts[piece]] if fresh else where,
                where,
                g_send.at[r, i],
                g_recv.at[r, i],
                seq=target,
            )
            copy.start()
            return copy

        for r in range(rows):
            swaps[r, 0].wait()
            for d in range(1, n):
                swaps[r, d].wait_recv()

            def step(i, carry, r=r):
                inside = pl.ds(pl.multiple_of(i * STEP, STEP), STEP)
                at = pl.ds(pl.multiple_of(r * frames + i * STEP, STEP), STEP)
                value = hidden[at, :] + bump[r, inside, :].astype(F32)
                embedded[at, :] = value
                centre = value - jnp.mean(value, axis=1, keepdims=True)
                hat = centre * lax.rsqrt(
                    jnp.mean(centre * centre, axis=1, keepdims=True) + EPSILON
                )
                scale = pick(ids[at, :], mod[r, 1], STEP)
                shift = pick(ids[at, :], mod[r, 0], STEP)
                normed[r, inside, :] = (hat * (1.0 + scale) + shift).astype(BF16)
                return carry

            lax.fori_loop(0, frames // STEP, step, 0)
            pushes[r, "x0"] = push(r, 0, 0, s, seat_x, True)
            pushes[r, "y1"] = push(r, 1, 1, s, seat_y, True)
            pushes[r, "x1"] = push(r, 2, 1, s, seat_x, True)
            pushes[r, "y0"] = push(r, 3, 0, s, seat_y, True)
            near += [push(r, 4, 0, s, sibling, True), push(r, 5, 1, s, sibling, True)]
            copy = pltpu.make_async_copy(normed.at[r], o.at[r, s], g_local.at[r])
            copy.start()
            pushes[r, "own"] = copy
            yield
        for r in range(rows):
            pushes[r, "x0"].wait_recv()
            far.append(push(r, 6, 0, seat_x, seat_y))
            near.append(push(r, 7, 0, seat_x, sibling))
            pushes[r, "y1"].wait_recv()
            far.append(push(r, 8, 1, seat_y, seat_x))
            near.append(push(r, 9, 1, seat_y, sibling))
            pushes[r, "x1"].wait_recv()
            near.append(push(r, 10, 1, seat_x, sibling))
            pushes[r, "y0"].wait_recv()
            near.append(push(r, 11, 0, seat_y, sibling))
        for r in range(rows):
            far[2 * r].wait_recv()
            near.append(push(r, 12, 0, diagonal, sibling))
            far[2 * r + 1].wait_recv()
            near.append(push(r, 13, 1, diagonal, sibling))
        yield
        for r in range(rows):
            pushes[r, "own"].wait()
            for d in range(1, n):
                swaps[r, d].wait_send()
            for name in ("x0", "x1", "y0", "y1"):
                pushes[r, name].wait_send()
        for copy in far:
            copy.wait_send()
        for copy in near:
            copy.wait()

    vmem = pl.BlockSpec(memory_space=pltpu.VMEM)
    tokens = rows * frames
    return Task(
        [bump_c, hidden, ids, mod],
        [
            jax.ShapeDtypeStruct((tokens, D), F32),
            jax.ShapeDtypeStruct((rows, n, frames, D), BF16),
        ],
        [
            pltpu.VMEM((rows, frames, D), BF16),
            pltpu.VMEM((rows, frames, D), BF16),
            DMA((rows, n)),
            DMA((rows, n)),
            DMA((rows,)),
            DMA((rows, 14)),
            DMA((rows, 14)),
            DMA((rows,)),
        ],
        body,
        in_specs=[ANY, vmem, vmem, vmem],
        out_specs=[vmem, ANY],
    )


def fold_rows(piece):
    total = piece[0:8]
    for q in range(1, piece.shape[0] // 8):
        total = total + piece[8 * q : 8 * q + 8]
    return total


def sum_norm_task(partial, embedded, grad_middle, ids, mod, rows, frames):
    n = dims()[1]
    width = D // n
    half_len = frames // 2
    step = 16

    def body(ins, outs, scratch, b, s, nb, n):
        x, embedded, middle, ids, mod = ins
        grad, o, sums = outs
        mine, first, one, got_one, two, got_two, send, recv, local, low, c_send, c_recv, c_local = scratch
        copies = []
        sums[...] = jnp.zeros_like(sums)

        def value(half, whole_refs, half_refs, r, at):
            parts = [ref[r, pl.ds(half * half_len + at, step), :] for ref in whole_refs]
            parts += [ref[r, pl.ds(at, step), :] for ref in half_refs]
            result = parts[0].astype(F32)
            for p in parts[1:]:
                result = result + p.astype(F32)
            return result

        def each(work):
            def move(i, carry):
                at = pl.multiple_of(i * step, step)
                for r in range(rows):
                    work(r, at)
                return carry

            lax.fori_loop(0, half_len // step, move, 0)

        def add(target, half, whole_refs, half_refs):
            def work(r, at):
                target[r, pl.ds(at, step), :] = value(half, whole_refs, half_refs, r, at).astype(BF16)

            each(work)

        def finish(half, whole_refs, half_refs):
            def work(r, at):
                down = value(half, whole_refs, half_refs, r, at)
                where = pl.ds(pl.multiple_of(r * frames + half * half_len + at, step), step)
                field = embedded[where, :]
                centre = field - jnp.mean(field, axis=1, keepdims=True)
                factor = lax.rsqrt(jnp.mean(centre * centre, axis=1, keepdims=True) + EPSILON)
                hat = centre * factor
                e = down * (1.0 + pick(ids[where, :], mod[r, 1], step))
                result = middle[where, :] + factor * (
                    e
                    - jnp.mean(e, axis=1, keepdims=True)
                    - hat * jnp.mean(e * hat, axis=1, keepdims=True)
                )
                grad[where, :] = result
                low[r, pl.ds(half * half_len + at, step), :] = result.astype(BF16)
                begin = ids[where, :] == ids[r * frames : r * frames + 1, :]
                for k, part_sum in enumerate((down, down * hat)):
                    kept = jnp.where(begin, part_sum, 0.0)
                    sums[r, 0, k] = sums[r, 0, k] + fold_rows(kept)
                    sums[r, 1, k] = sums[r, 1, k] + fold_rows(part_sum - kept)

            each(work)
            rows_at = pl.ds(half * half_len, half_len)
            target = o.at[:, seat_rows(s, frames, half * half_len, half_len), :]
            for d in range(1, n):
                t = lax.rem(s + d, n)
                copy = remote(
                    low.at[:, rows_at, lane_block(b, t, n, width)],
                    target,
                    c_send.at[half, d],
                    c_recv.at[half, d],
                    seq=t,
                )
                copy.start()
                copies.append(copy)
            copy = pltpu.make_async_copy(
                low.at[:, rows_at, lane_block(b, s, n, width)], target, c_local.at[half]
            )
            copy.start()
            copies.append(copy)

        yield from quad_stages(
            s,
            x,
            mine,
            first,
            lambda ref, i: ref.at[:, i],
            one,
            got_one,
            two,
            got_two,
            (send, recv, local),
            add,
            finish,
        )
        for copy in copies:
            copy.wait()

    vmem = pl.BlockSpec(memory_space=pltpu.VMEM)
    tokens = rows * frames
    return Task(
        [partial, embedded, grad_middle, ids, mod],
        [
            jax.ShapeDtypeStruct((tokens, D), F32),
            jax.ShapeDtypeStruct((rows, n * frames, width), BF16),
            jax.ShapeDtypeStruct((rows, 2, 2, 8, D), F32),
        ],
        quad_scratch((rows, frames, D), (rows, half_len, D))
        + [pltpu.VMEM((rows, frames, D), BF16), DMA((2, n)), DMA((2, n)), DMA((2,))],
        body,
        in_specs=[ANY] + [vmem] * 4,
        out_specs=[vmem, ANY, vmem],
    )


def late_grads_task(att, grad_branch, grad_feed, low, grad_up, normed, ndev, part):
    def body(ins, outs, scratch, b, s, nb, n):
        yield
        late_work(*ins, *outs, part)

    vmem = pl.BlockSpec(memory_space=pltpu.VMEM)
    return Task(
        [att, grad_branch, grad_feed, low, grad_up, normed],
        [
            jax.ShapeDtypeStruct((ndev, 3 * part, D), BF16),
            jax.ShapeDtypeStruct((ndev, 2 * part, D), BF16),
        ],
        [],
        body,
        in_specs=[vmem] * 6,
        out_specs=[vmem] * 2,
    )


def late_work(att, grad_branch, grad_feed, low, grad_up, normed, out, down, part):
    wide = 256
    per = wide // part
    for j in range(D // wide):
        lanes = slice(j * wide, (j + 1) * wide)
        out[j * per : (j + 1) * per, 0:part, :] = (
            rows_sum(grad_branch[:, lanes], att[...]).astype(BF16).reshape(per, part, D)
        )
        for half in range(2):
            down[j * per : (j + 1) * per, half * part : (half + 1) * part, :] = (
                rows_sum(grad_feed[:, lanes], low[:, half * D : (half + 1) * D])
                .astype(BF16)
                .reshape(per, part, D)
            )
    for j in range(2 * D // wide):
        lanes = slice(j * wide, (j + 1) * wide)
        out[j * per // 2 : (j + 1) * per // 2, part : 3 * part, :] = (
            rows_sum(grad_up[:, lanes], normed[...]).astype(BF16).reshape(per // 2, 2 * part, D)
        )


def conv_back_task(d, u, seg, c1, c2, taps, frames):
    nb, n = dims()
    rows, length, width = u.shape
    groups = width // CHAN
    count, buffer = conv_sizes(length)
    pieces_shape = (1, nb, KERNEL, width // nb, 2 * CHAN)

    def body(ins, outs, scratch, b, s, nb, n):
        d, u, seg, c1, c2, taps = ins
        o, pieces = outs
        buf, grads, live, x, turned2, turned1, bands, even, odd, dh, send, recv, local = scratch
        yield
        fill_bands(bands, taps, groups, True)
        even[...] = jnp.zeros_like(even)
        odd[...] = jnp.zeros_like(odd)
        copies = []
        for r in range(rows):
            row = pl.ds(r, 1)
            yield from conv_chain(
                d.at[row], seg.at[row], c1.at[row], c2.at[row], dh.at[row], buf, grads, live, x,
                turned2.at[r], turned1.at[r], bands, count, length, groups,
            )
            target = o.at[r, :, lane_block(b, s, n, width)]
            for k in range(1, n):
                t = lax.rem(s + k, n)
                copy = remote(
                    dh.at[r, seat_rows(t, frames, 0, frames), :],
                    target,
                    send.at[r, k],
                    recv.at[r, k],
                    seq=t,
                )
                copy.start()
                copies.append(copy)
            copy = pltpu.make_async_copy(
                dh.at[r, seat_rows(s, frames, 0, frames), :], target, local.at[r]
            )
            copy.start()
            copies.append(copy)
            yield
        for r in range(rows):
            row = pl.ds(r, 1)
            yield from conv_weights(
                u.at[row], seg.at[row], c1.at[row], buf, live, x, turned2.at[r], turned1.at[r],
                even, odd, count, length, groups,
            )
            yield
        conv_pieces(pieces, even, odd, groups, nb)
        yield
        for copy in copies:
            copy.wait()

    vmem = pl.BlockSpec(memory_space=pltpu.VMEM)
    frames_buf = pltpu.VMEM((buffer, width), F32)
    turned = pltpu.VMEM((rows, groups, FOLDED, count), BF16)
    sums = pltpu.VMEM((groups, 16, 2 * CHAN, 2 * CHAN), F32)
    return Task(
        [d, u, seg, c1, c2, taps],
        [
            jax.ShapeDtypeStruct((rows, frames, n * width), BF16),
            jax.ShapeDtypeStruct(pieces_shape, BF16),
        ],
        [
            frames_buf,
            frames_buf,
            frames_buf,
            pltpu.VMEM((groups, count, DEPTH), BF16),
            turned,
            turned,
            pltpu.VMEM((2, groups, DEPTH, FOLDED), BF16),
            sums,
            sums,
            pltpu.VMEM(u.shape, BF16),
            DMA((rows, n)),
            DMA((rows, n)),
            DMA((rows,)),
        ],
        body,
        in_specs=[vmem] * 6,
        out_specs=[ANY, vmem],
    )


def layer_norm(field):
    centre = field - jnp.mean(field, axis=-1, keepdims=True)
    return centre * lax.rsqrt(jnp.mean(centre * centre, axis=-1, keepdims=True) + EPSILON)


def modulate(field, scaling, shifting):
    return layer_norm(field) * (1.0 + scaling) + shifting


def gelu_curve(inputs):
    return jax.nn.gelu(inputs, approximate=True)


def by_segment(ids, table):
    value = table[:, SEGS - 1][:, None, :]
    for u in range(SEGS - 2, -1, -1):
        value = jnp.where(ids[:, :, None] == u, table[:, u][:, None, :], value)
    return value


def rope_tables(segment_ids, starts, width):
    length = segment_ids.shape[1]
    pairs = (np.arange(width) % HEAD) // 2
    freq = 10000.0 ** (-2.0 * pairs / HEAD)
    angle = np.arange(length)[:, None] * freq[None, :]
    cos_t = jnp.asarray(np.cos(angle).astype(np.float32))[None]
    sin_t = jnp.asarray(np.sin(angle).astype(np.float32))[None]
    offset = starts.astype(F32)[:, :, None] * jnp.asarray(freq.astype(np.float32))
    cos_o = by_segment(segment_ids, jnp.cos(offset))
    sin_o = by_segment(segment_ids, jnp.sin(offset))
    return cos_t * cos_o + sin_t * sin_o, sin_t * cos_o - cos_t * sin_o


def on_device(
    mel_inputs,
    text_ids,
    segment_ids,
    key_mask,
    time_index,
    input_proj,
    conv_first,
    conv_second,
    time_table,
    adaln_proj,
    qkv_proj,
    out_proj,
    up_proj,
    down_proj,
    text_table,
    grad_out,
):
    nb, n = dims()
    ndev = nb * n
    rows, frames = mel_inputs.shape[:2]
    tokens = rows * frames
    length = frames * n
    width = D // n
    part = D // ndev
    mine = lax.axis_index("seq")
    first_frame = mine * frames

    out_t, up_t, down_t = out_proj.T, up_proj.T, down_proj.T
    wide_t = jnp.concatenate([out_t, up_t, down_t[:, :D], down_t[:, D:]], axis=0)
    per = wide_t.shape[0]
    (
        (full_in,),
        (full_text,),
        (full_time,),
        (all_index,),
        (got_convs,),
    ) = transfer(
        [
            spread_task(input_proj.T),
            spread_task(text_table.T),
            spread_task(time_table.T),
            spread_task(time_index),
            columns_out_task(jnp.concatenate([conv_first, conv_second], axis=2)[None], True),
        ],
        0,
    )
    got_convs = got_convs[0]
    wide_t, _ = lax.optimization_barrier((wide_t, all_index))
    late = lax.all_gather(wide_t, ("batch", "seq"), axis=0, tiled=True).reshape(ndev, per, D)
    in_t = full_in.reshape(D, input_proj.shape[0])
    text_t = full_text.reshape(-1, VOCAB)
    time_t = full_time.reshape(D, STEPS)
    slot_steps = all_index[:, 0].reshape(nb * rows * SEGS)

    own_ids = lax.dynamic_slice_in_dim(segment_ids, first_frame, frames, 1)
    key_code = segment_ids + jnp.where(key_mask > 0, 0, 8)
    seg_column = key_code[:, :, None]
    seg_index = jnp.arange(SEGS, dtype=jnp.int32)
    starts = jnp.sum((segment_ids[:, None, :] < seg_index[None, :, None]).astype(jnp.int32), axis=2)

    text_hot = (
        text_ids.reshape(-1)[:, None] == jnp.arange(VOCAB, dtype=jnp.int32)[None, :]
    ).astype(BF16)
    text_embed = times_t(text_hot, text_t).astype(BF16)
    joined = jnp.concatenate([mel_inputs.reshape(tokens, 2 * MEL), text_embed], axis=1)
    hidden = times_t(joined, in_t).reshape(rows, frames, D)

    step_hot = (
        slot_steps[:, None] == jnp.arange(STEPS, dtype=jnp.int32)[None, :]
    ).astype(BF16)
    cond_value = times_t(step_hot, time_t)
    soft_cond = jax.nn.silu(cond_value).astype(BF16)
    own_mod = times(soft_cond, adaln_proj)
    task, arrange = to_channels(hidden.astype(BF16))
    got, (mod_got,) = transfer(
        [task, spray_task(own_mod.reshape(nb, rows * SEGS, 6 * part), True)], 2
    )
    hidden_c = arrange(got)
    modulation = mod_got.transpose(1, 0, 2).reshape(rows, SEGS, 6, D)
    mod_table = modulation.transpose(0, 2, 1, 3)
    ids_column = own_ids.reshape(tokens, 1)
    fused = n == 8 and width % 128 == 0
    shift_attn, scale_attn = (by_segment(own_ids, modulation[:, :, i]) for i in range(2))

    conv_one, conv_two, bump_c = conv_forward(hidden_c, seg_column, got_convs)
    qkv_task = columns_out_task(qkv_proj.T.reshape(3, part, D))
    if fused:
        (embedded, normed_all), (got_qkv,) = transfer(
            [
                norm_gather_task(
                    bump_c, hidden.reshape(tokens, D), ids_column, mod_table, rows, frames
                ),
                qkv_task,
            ],
            3,
        )
        embedded = embedded.reshape(rows, frames, D)
    else:
        task, arrange = to_frames(bump_c)
        bump = arrange(transfer([task], 3)[0])
        embedded = hidden + bump.astype(F32)
        normed = modulate(embedded, scale_attn, shift_attn).astype(BF16)
        (normed_all,), (got_qkv,) = transfer([gather_task(normed), qkv_task], 4)
    normed_all = normed_all.reshape(rows, length, D)
    qkv_t = got_qkv.reshape(3 * width, D)
    cos, sin = rope_tables(segment_ids, starts, width)
    query, key, value = qkv_forward(normed_all, qkv_t, cos, sin)
    attended, attended_low, log_lanes = attention_forward(
        query, key, value, seg_column, key_code[:, None, :]
    )
    task, arrange = to_frames(attended_low)
    attended_own = arrange(transfer([task], 5)[0])
    attended_own = attended_own.reshape(tokens, D)

    (
        block_out,
        grad_att,
        grad_middle,
        feed_sums,
        normed_feed,
        gelu_low,
        grad_up,
        grad_feed,
        grad_branch,
    ) = feed_both(
        attended_own,
        embedded.reshape(tokens, D),
        late,
        ids_column,
        mod_table,
        grad_out.reshape(tokens, D),
        rows,
        frames,
        part,
    )
    late_task = late_grads_task(
        attended_own, grad_branch, grad_feed, gelu_low, grad_up, normed_feed, ndev, part
    )
    block_out = block_out.reshape(rows, frames, D)
    grad_att = grad_att.reshape(rows, frames, D)
    grad_middle = grad_middle.reshape(rows, frames, D)
    task, arrange = to_channels(grad_att)
    grad_att_c = arrange(transfer([task], 6)[0])
    heads = width // HEAD
    delta = jnp.sum(
        (grad_att_c.astype(F32) * attended).reshape(rows, length, heads, HEAD), axis=3
    ).transpose(0, 2, 1)
    log_rows = log_lanes.reshape(rows, length, heads, HEAD)[:, :, :, 0].transpose(0, 2, 1)
    block_first_ids = segment_ids[:, ::BLOCK]
    block_last_ids = segment_ids[:, BLOCK - 1 :: BLOCK]
    ends = jnp.sum((segment_ids[:, None, :] <= seg_index[None, :, None]).astype(jnp.int32), axis=2)
    low_edge = (
        jnp.sum(jnp.where(block_first_ids[:, :, None] == seg_index, starts[:, None, :], 0), axis=2)
        // BLOCK
    )
    high_edge = (
        jnp.sum(jnp.where(block_last_ids[:, :, None] == seg_index, ends[:, None, :], 0), axis=2)
        + BLOCK
        - 1
    ) // BLOCK
    grad_projected = attention_backward(
        query,
        key,
        value,
        grad_att_c,
        log_rows,
        delta,
        seg_column,
        segment_ids[:, None, :],
        cos,
        sin,
        low_edge,
        high_edge,
    ).reshape(rows * length, 3 * width)
    grad_qkv = rows_sum(grad_projected, normed_all.reshape(rows * length, D)).astype(BF16)
    partial = times(grad_projected, qkv_t).astype(BF16).reshape(rows, n, frames, D)
    qkv_back = columns_back_task(grad_qkv.reshape(3, nb, part, D))
    if fused:
        (grad_embedded, grad_emb_c, attn_sums), (got_qkv_grads,), late_grads = transfer(
            [
                sum_norm_task(
                    partial,
                    embedded.reshape(tokens, D),
                    grad_middle.reshape(tokens, D),
                    ids_column,
                    mod_table,
                    rows,
                    frames,
                ),
                qkv_back,
                late_task,
            ],
            7,
        )
        grad_embedded = grad_embedded.reshape(rows, frames, D)
        attn_sums = jnp.sum(attn_sums, axis=3)
        attn_sums = [attn_sums[:, :, 0], attn_sums[:, :, 1]]
    else:
        (grad_normed,), (got_qkv_grads,), late_grads = transfer(
            [sum_task(partial), qkv_back, late_task], 7
        )
        grad_emb_part, grad_scale_attn, grad_shift_attn = jax.vjp(
            modulate, embedded, scale_attn, shift_attn
        )[1](grad_normed)
        grad_embedded = grad_middle + grad_emb_part
        task, arrange = to_channels(grad_embedded.astype(BF16))
        grad_emb_c = arrange(transfer([task], 10)[0])
    first_ids, last_ids = own_ids[:, 0], own_ids[:, -1]
    if not fused:
        first = (own_ids == first_ids[:, None])[:, :, None]
        attn_sums = [
            jnp.stack(
                [jnp.sum(jnp.where(first, g, 0.0), axis=1), jnp.sum(jnp.where(first, 0.0, g), axis=1)],
                axis=1,
            )
            for g in (grad_shift_attn, grad_scale_attn)
        ]
    feed_sums = jnp.sum(feed_sums, axis=3)
    sides = jnp.concatenate(
        [attn_sums[0], attn_sums[1]] + [feed_sums[:, :, i] for i in range(4)], axis=2
    )
    is_first = (first_ids[:, None] == seg_index).astype(F32)
    is_last = (last_ids[:, None] == seg_index).astype(F32)
    local_sums = is_first[:, :, None] * sides[:, :1] + is_last[:, :, None] * sides[:, 1:]
    slots = rows * SEGS
    sums_out = local_sums.reshape(slots, ndev, 6 * part).transpose(1, 0, 2)
    if fused:
        late_parts = [(0, 0), (0, 1), (1, 0), (1, 1)]
        late_tasks = []
        for k, (which, side) in enumerate(late_parts):
            x = late_grads[which].reshape(nb, n, -1, D)
            size = x.shape[2] // 2
            late_tasks.append(quad_scatter_task(x, LATE_RESTS[k], side * size, size))
        *late_got, (sums_got,), (grad_hidden_conv, conv_sums) = transfer(
            late_tasks
            + [
                spray_task(sums_out, False),
                conv_back_task(
                    grad_emb_c, hidden_c, seg_column, conv_one, conv_two, got_convs, frames
                ),
            ],
            11,
        )
        late_sum = jnp.concatenate([jnp.sum(x[0].astype(F32), axis=0) for x in late_got], axis=0)
    else:
        late_sum = lax.psum_scatter(
            jnp.concatenate(late_grads, axis=1), ("batch", "seq"), scatter_dimension=0, tiled=False
        ).astype(F32)
        grad_hidden_c, conv_sums = conv_backward(
            grad_emb_c, hidden_c, seg_column, conv_one, conv_two, got_convs, nb
        )
        task, arrange = to_frames(grad_hidden_c)
        got, (sums_got,) = transfer([task, spray_task(sums_out, False)], 11)
        grad_hidden_conv = arrange(got)
    sums_got = sums_got.reshape(nb, n, slots, 6 * part)
    grad_mod = jnp.sum(sums_got, axis=1).astype(BF16).reshape(nb * slots, 6 * part)
    grad_adaln = rows_sum(soft_cond, grad_mod)
    soft_part = times_t(grad_mod, adaln_proj)
    soft_out = soft_part.reshape(nb * slots, ndev, part).transpose(1, 0, 2)
    grad_qkv_own = jnp.sum(got_qkv_grads.astype(F32), axis=0).reshape(3 * part, D).T

    grad_hidden = (grad_embedded + grad_hidden_conv.astype(F32)).astype(BF16).reshape(tokens, D)
    grad_input = rows_sum(grad_hidden, joined).astype(BF16)
    grad_joined = times(grad_hidden, in_t)
    grad_mels = grad_joined[:, : 2 * MEL].reshape(rows, frames, 2 * MEL)
    grad_embed = grad_joined[:, 2 * MEL :].astype(BF16)
    grad_text = rows_sum(grad_embed, text_hot).astype(BF16)
    scatter = quad_scatter_task if n == 8 and nb % 2 == 0 else scatter_task
    (in_sum,), (text_sum,), (soft_got,), (got_conv_grads,) = transfer(
        [
            scatter(grad_input.reshape(nb, n, part, -1)),
            scatter(grad_text.reshape(nb, n, -1, VOCAB)),
            spray_task(soft_out, False),
            columns_back_task(conv_sums),
        ],
        13,
    )
    grad_convs = jnp.sum(got_conv_grads.astype(F32), axis=0)[0]
    grad_first, grad_second = grad_convs[..., :CHAN], grad_convs[..., CHAN:]
    grad_soft = jnp.sum(soft_got, axis=0)
    own_cond = times(step_hot, time_table)
    grad_cond = jax.vjp(jax.nn.silu, own_cond)[1](grad_soft)[0]
    grad_time = jnp.dot(step_hot.astype(F32).T, grad_cond, precision=EXACT)
    grad_input_own = jnp.sum(in_sum.astype(F32), axis=0).T
    grad_text_own = jnp.sum(text_sum.astype(F32), axis=0).T
    grad_down_own = jnp.concatenate([late_sum[3 * part : 4 * part], late_sum[4 * part :]], axis=1)

    return (
        block_out,
        grad_mels,
        grad_input_own,
        grad_first,
        grad_second,
        grad_time,
        grad_adaln,
        grad_qkv_own,
        late_sum[:part].T,
        late_sum[part : 3 * part].T,
        grad_down_own.T,
        grad_text_own,
    )


def solution(mesh):
    frames = P("batch", "seq", None)
    columns = P(None, ("batch", "seq"))
    taps = P(None, ("batch", "seq"), None)
    in_specs = (
        frames,
        P("batch", "seq"),
        P("batch", None),
        P("batch", None),
        P("batch", None),
        columns,
        taps,
        taps,
        columns,
        columns,
        columns,
        columns,
        columns,
        columns,
        columns,
        frames,
    )
    out_specs = (
        frames,
        frames,
        columns,
        taps,
        taps,
        columns,
        columns,
        columns,
        columns,
        columns,
        columns,
        columns,
    )
    return jax.shard_map(
        on_device, mesh=mesh, in_specs=in_specs, out_specs=out_specs, check_vma=False
    )
```

```python
import functools

import jax
import jax.numpy as jnp
import numpy as np
from jax import lax
from jax.experimental import pallas as pl
from jax.experimental.pallas import tpu as pltpu
from jax.sharding import PartitionSpec as P

D = 1024
HEADS = 16
HEAD = 64
MEL = 100
VOCAB = 2546
KERNEL = 31
HALF = KERNEL // 2
CHAN = 64
STEPS = 32
SEGS = 4
GAP = 16
FOLD = 4
TAPS = KERNEL + FOLD - 1

EPSILON = 1e-06
MASKED = -1e30
EXACT = lax.Precision.HIGHEST
MESH = pl.DeviceIdType.MESH
ANY = pl.BlockSpec(memory_space=pl.ANY)
VMEM_LIMIT = 56 * 1024 * 1024
F32 = jnp.float32
BF16 = jnp.bfloat16


def dims():
    return lax.axis_size("batch"), lax.axis_size("seq")


def params(cid=None):
    if cid is None:
        return pltpu.CompilerParams(vmem_limit_bytes=VMEM_LIMIT)
    return pltpu.CompilerParams(
        collective_id=cid, has_side_effects=True, vmem_limit_bytes=VMEM_LIMIT
    )


def greet_all(nb, n, b, s):
    sem = pltpu.get_barrier_semaphore()
    me = b * n + s
    for d in range(1, nb * n):
        other = lax.rem(me + d, nb * n)
        pl.semaphore_signal(
            sem,
            inc=1,
            device_id={"batch": other // n, "seq": lax.rem(other, n)},
            device_id_type=MESH,
        )
    pl.semaphore_wait(sem, nb * n - 1)


def greet_group(n, s):
    sem = pltpu.get_barrier_semaphore()
    for d in range(1, n):
        pl.semaphore_signal(
            sem, inc=1, device_id={"seq": lax.rem(s + d, n)}, device_id_type=MESH
        )
    pl.semaphore_wait(sem, n - 1)


def block_of(b, s, n):
    chips, core = n // 2, lax.rem(s, 2)
    return 2 * lax.rem(s // 2 + b + (chips // 2) * core, chips) + core


def holder_of(b, m, n, nb):
    chips, core = n // 2, lax.rem(m, 2)
    turned = m // 2 + (nb + chips) * chips - b - (chips // 2) * core
    return 2 * lax.rem(turned, chips) + core


def remote(src, dst, send, recv, **where):
    return pltpu.make_async_remote_copy(
        src_ref=src,
        dst_ref=dst,
        send_sem=send,
        recv_sem=recv,
        device_id=where,
        device_id_type=MESH,
    )


class Task:
    def __init__(
        self, operands, outs, scratch, body, everyone=False, in_specs=None, out_specs=None
    ):
        self.operands, self.outs, self.scratch = list(operands), list(outs), list(scratch)
        self.body, self.everyone = body, everyone
        self.in_specs = in_specs or [ANY] * len(self.operands)
        self.out_specs = out_specs or [ANY] * len(self.outs)


def transfer_kernel(bodies, sizes, everyone, nb, n, *refs):
    b, s = lax.axis_index("batch"), lax.axis_index("seq")
    counts = [sum(size[i] for size in sizes) for i in range(3)]
    pools = [
        list(refs[: counts[0]]),
        list(refs[counts[0] : counts[0] + counts[1]]),
        list(refs[counts[0] + counts[1] :]),
    ]
    running = []
    for body, size in zip(bodies, sizes):
        taken = []
        for i in range(3):
            taken.append(pools[i][: size[i]])
            pools[i] = pools[i][size[i] :]
        running.append(body(*taken, b, s, nb, n))
    if everyone:
        greet_all(nb, n, b, s)
    else:
        greet_group(n, s)
    while running:
        left = []
        for task in running:
            try:
                next(task)
                left.append(task)
            except StopIteration:
                pass
        running = left


def transfer(tasks, cid):
    nb, n = dims()
    operands = [x for task in tasks for x in task.operands]
    outs = [x for task in tasks for x in task.outs]
    sizes = [(len(t.operands), len(t.outs), len(t.scratch)) for t in tasks]
    got = pl.pallas_call(
        functools.partial(
            transfer_kernel,
            [t.body for t in tasks],
            sizes,
            any(t.everyone for t in tasks),
            nb,
            n,
        ),
        out_shape=outs,
        in_specs=[x for task in tasks for x in task.in_specs],
        out_specs=[x for task in tasks for x in task.out_specs],
        scratch_shapes=[x for task in tasks for x in task.scratch],
        compiler_params=params(cid),
    )(*operands)
    got = list(got)
    result = []
    for size in sizes:
        result.append(got[: size[1]])
        got = got[size[1] :]
    return result


DMA = pltpu.SemaphoreType.DMA


def like(x, shape, dtype=None):
    return jax.ShapeDtypeStruct(tuple(shape), dtype or x.dtype)


def swap_task(x, shape, parts):
    n = dims()[1]

    def body(ins, outs, scratch, b, s, nb, n):
        send, recv, local = scratch
        src, dst = parts(ins[0], outs[0], b, s)
        copies = []
        for d in range(1, n):
            t = lax.rem(s + d, n)
            copy = remote(src(t), dst, send.at[d], recv.at[d], seq=t)
            copy.start()
            copies.append(copy)
        own = pltpu.make_async_copy(src(s), dst, local)
        own.start()
        copies.append(own)
        yield
        yield
        for copy in copies:
            copy.wait()

    return Task([x], [like(x, shape)], [DMA((n,)), DMA((n,)), DMA], body)


def to_channels(x):
    n = dims()[1]
    rows, frames = x.shape[:2]
    width = x.shape[2] // n
    if width % 128 == 0:

        def parts(x, o, b, s):
            first = pl.multiple_of(s * frames, 16)
            return (
                lambda t: x.at[
                    :, :, pl.ds(pl.multiple_of(block_of(b, t, n) * width, 128), width)
                ]
            ), o.at[:, pl.ds(first, frames), :]

        return swap_task(x, (rows, n * frames, width), parts), lambda got: got[0]

    def split_parts(x, o, b, s):
        return (lambda t: x.at[block_of(b, t, n)]), o.at[s]

    split = x.reshape(rows, frames, n, width).transpose(2, 0, 1, 3)
    return (
        swap_task(split, split.shape, split_parts),
        lambda got: got[0].transpose(1, 0, 2, 3).reshape(rows, n * frames, width),
    )


def to_frames(x):
    n = dims()[1]
    rows, length, width = x.shape
    frames = length // n
    if width % 128 == 0:

        def parts(x, o, b, s):
            first = pl.multiple_of(block_of(b, s, n) * width, 128)
            return (
                lambda t: x.at[:, pl.ds(pl.multiple_of(t * frames, 16), frames), :]
            ), o.at[:, :, pl.ds(first, width)]

        return swap_task(x, (rows, frames, n * width), parts), lambda got: got[0]

    def split_parts(x, o, b, s):
        return (lambda t: x.at[t]), o.at[block_of(b, s, n)]

    split = x.reshape(rows, n, frames, width).transpose(1, 0, 2, 3)
    return (
        swap_task(split, split.shape, split_parts),
        lambda got: got[0].transpose(1, 2, 0, 3).reshape(rows, frames, n * width),
    )


def spray_task(x, by_batch):
    nb, n = dims()
    ndev = nb * n

    def body(ins, outs, scratch, b, s, nb, n):
        send, recv, local = scratch
        x, o = ins[0], outs[0]
        me = b * n + s
        own = pltpu.make_async_copy(x.at[b if by_batch else me], o.at[me], local)
        own.start()
        copies = [own]
        for d in range(1, ndev):
            other = lax.rem(me + d, ndev)
            plane, where = other // n, lax.rem(other, n)
            copy = remote(
                x.at[plane if by_batch else other],
                o.at[me],
                send.at[d],
                recv.at[d],
                batch=plane,
                seq=where,
            )
            copy.start()
            copies.append(copy)
        yield
        yield
        for copy in copies:
            copy.wait()

    return Task(
        [x], [like(x, (ndev,) + x.shape[1:])], [DMA((ndev,)), DMA((ndev,)), DMA], body, True
    )


def gather_task(x):
    n = dims()[1]

    def body(ins, outs, scratch, b, s, nb, n):
        send, recv, local = scratch
        x, o = ins[0], outs[0]
        core = lax.rem(s, 2)
        sibling = s + 1 - 2 * core
        chips = n // 2
        far, near = [], []
        for d in range(1, chips):
            copy = remote(x, o.at[:, s], send.at[d], recv.at[d], seq=lax.rem(s + 2 * d, n))
            copy.start()
            far.append(copy)
        copy = remote(x, o.at[:, s], send.at[0], recv.at[0], seq=sibling)
        copy.start()
        near.append(copy)
        own = pltpu.make_async_copy(x, o.at[:, s], local)
        own.start()
        yield
        for d in range(1, chips):
            far[d - 1].wait_recv()
            source = lax.rem(s - 2 * d + n, n)
            copy = remote(
                o.at[:, source],
                o.at[:, source],
                send.at[chips + d],
                recv.at[chips + d],
                seq=sibling,
            )
            copy.start()
            near.append(copy)
        yield
        own.wait()
        for copy in far:
            copy.wait_send()
        for copy in near:
            copy.wait()

    out = like(x, (x.shape[0], n) + x.shape[1:])
    return Task([x], [out], [DMA((n,)), DMA((n,)), DMA], body)


def quad_gather_task(x):
    n = dims()[1]
    frames = x.shape[1]
    half = frames // 2

    def body(ins, outs, scratch, b, s, nb, n):
        send, recv, local = scratch
        x, o = ins[0], outs[0]
        core, chip = lax.rem(s, 2), s // 2
        sibling = s + 1 - 2 * core
        flip_x = chip + 1 - 2 * lax.rem(chip, 2)
        flip_y = lax.rem(chip + 2, 4)
        diagonal = lax.rem(flip_x + 2, 4)
        seat = lambda c: 2 * c + core
        parts = (pl.ds(0, half), pl.ds(half, half))
        k = iter(range(16))

        def push(piece, source, target):
            i = next(k)
            where = o.at[:, source, parts[piece]]
            copy = remote(
                x.at[:, parts[piece]] if source is s else where,
                where,
                send.at[i],
                recv.at[i],
                seq=target,
            )
            copy.start()
            return copy

        to_x = [push(p, s, seat(flip_x)) for p in (0, 1)]
        to_y = [push(p, s, seat(flip_y)) for p in (1, 0)]
        near = [push(p, s, sibling) for p in (0, 1)]
        own = pltpu.make_async_copy(x, o.at[:, s], local)
        own.start()
        yield
        far = []
        to_x[0].wait_recv()
        far.append(push(0, seat(flip_x), seat(flip_y)))
        near.append(push(0, seat(flip_x), sibling))
        to_y[0].wait_recv()
        far.append(push(1, seat(flip_y), seat(flip_x)))
        near.append(push(1, seat(flip_y), sibling))
        to_x[1].wait_recv()
        near.append(push(1, seat(flip_x), sibling))
        to_y[1].wait_recv()
        near.append(push(0, seat(flip_y), sibling))
        far[0].wait_recv()
        near.append(push(0, seat(diagonal), sibling))
        far[1].wait_recv()
        near.append(push(1, seat(diagonal), sibling))
        yield
        own.wait()
        for copy in to_x + to_y + far:
            copy.wait_send()
        for copy in near:
            copy.wait()

    out = like(x, (x.shape[0], n) + x.shape[1:])
    return Task([x], [out], [DMA((16,)), DMA((16,)), DMA], body)


def sum_task(x):
    n = dims()[1]
    rows, _, frames, width = x.shape
    chips = n // 2
    step = 16

    def body(ins, outs, scratch, b, s, nb, n):
        mine, first, passed, second, total, send, recv, local, out_sem = scratch
        x, o = ins[0], outs[0]
        core = lax.rem(s, 2)
        sibling = s + 1 - 2 * core
        chip = s // 2
        order = [lax.rem(chip + d, chips) for d in list(range(1, chips)) + [0]]
        pair, own, far = [], [], []
        for k, c in enumerate(order):
            copy = remote(
                x.at[:, 2 * c + 1 - core], first.at[k], send.at[k], recv.at[k], seq=sibling
            )
            copy.start()
            pair.append(copy)
            copy = pltpu.make_async_copy(x.at[:, 2 * c + core], mine.at[k], local.at[k])
            copy.start()
            own.append(copy)
        yield
        for k in range(chips):
            pair[k].wait_recv()
            own[k].wait()
            if k < chips - 1:

                def add(i, carry, k=k):
                    at = pl.ds(pl.multiple_of(i * step, step), step)
                    for r in range(rows):
                        passed[k, r, at, :] = (
                            mine[k, r, at, :].astype(F32) + first[k, r, at, :].astype(F32)
                        ).astype(BF16)
                    return carry

                lax.fori_loop(0, frames // step, add, 0)
                copy = remote(
                    passed.at[k],
                    second.at[k],
                    send.at[chips + k],
                    recv.at[chips + k],
                    seq=2 * order[k] + core,
                )
                copy.start()
                far.append(copy)
        yield
        for copy in far:
            copy.wait_recv()

        def finish(i, carry):
            at = pl.ds(pl.multiple_of(i * step, step), step)
            for r in range(rows):
                value = mine[chips - 1, r, at, :].astype(F32) + first[chips - 1, r, at, :].astype(F32)
                for k in range(chips - 1):
                    value = value + second[k, r, at, :].astype(F32)
                total[r, at, :] = value
            return carry

        lax.fori_loop(0, frames // step, finish, 0)
        out = pltpu.make_async_copy(total, o, out_sem)
        out.start()
        for copy in pair + far:
            copy.wait_send()
        out.wait()

    slots = pltpu.VMEM((chips, rows, frames, width), BF16)
    fewer = pltpu.VMEM((chips - 1, rows, frames, width), BF16)
    return Task(
        [x],
        [like(x, (rows, frames, width), F32)],
        [
            slots,
            slots,
            fewer,
            fewer,
            pltpu.VMEM((rows, frames, width), F32),
            DMA((n,)),
            DMA((n,)),
            DMA((chips,)),
            DMA,
        ],
        body,
    )


def quad_stages(s, x, mine, first, out, one, got_one, two, got_two, sems, add, total, rests=(0, 0, 0)):
    send, recv, local = sems
    core, chip = lax.rem(s, 2), s // 2
    sibling = s + 1 - 2 * core
    flip_x = chip + 1 - 2 * lax.rem(chip, 2)
    flip_y = lax.rem(chip + 2, 4)
    places = [flip_x, flip_y, lax.rem(flip_x + 2, 4), chip]
    sent, own = {}, {}
    for k in (2, 0, 1, 3):
        copy = remote(
            out(x, 2 * places[k] + 1 - core), first.at[k], send.at[k], recv.at[k], seq=sibling
        )
        copy.start()
        sent[k] = copy
        copy = pltpu.make_async_copy(out(x, 2 * places[k] + core), mine.at[k], local.at[k])
        copy.start()
        own[k] = copy
    yield
    for _ in range(rests[0]):
        yield
    across = (2 * flip_x + core, 2 * flip_y + core)
    stage = {}
    waited = set()

    def ready(k):
        if k not in waited:
            waited.add(k)
            sent[k].wait_recv()
            own[k].wait()

    for half, i, k in ((0, 1, 2), (1, 1, 2), (0, 0, 0), (1, 0, 1)):
        ready(k)
        add(one.at[half, i], half, [mine.at[k], first.at[k]], [])
        q = 4 + 2 * half + i
        copy = remote(
            one.at[half, i], got_one.at[half, i], send.at[q], recv.at[q], seq=across[half]
        )
        copy.start()
        stage[half, i] = copy
    yield
    for _ in range(rests[1]):
        yield
    for half in (0, 1):
        k = 1 - half
        ready(k)
        stage[half, 1].wait_recv()
        add(two.at[half], half, [mine.at[k], first.at[k]], [got_one.at[half, 1]])
        q = 8 + half
        copy = remote(two.at[half], got_two.at[half], send.at[q], recv.at[q], seq=across[1 - half])
        copy.start()
        stage[half, 2] = copy
    yield
    for _ in range(rests[2]):
        yield
    ready(3)
    for half in (0, 1):
        stage[half, 0].wait_recv()
        stage[half, 2].wait_recv()
        total(half, [mine.at[3], first.at[3]], [got_one.at[half, 0], got_two.at[half]])
    for copy in list(sent.values()) + list(stage.values()):
        copy.wait_send()


def quad_scratch(block, half):
    return [
        pltpu.VMEM((4,) + block, BF16),
        pltpu.VMEM((4,) + block, BF16),
        pltpu.VMEM((2, 2) + half, BF16),
        pltpu.VMEM((2, 2) + half, BF16),
        pltpu.VMEM((2,) + half, BF16),
        pltpu.VMEM((2,) + half, BF16),
        DMA((10,)),
        DMA((10,)),
        DMA((4,)),
    ]


def quad_sum_task(x):
    rows, _, frames, width = x.shape
    half_len = frames // 2
    step = 16

    def body(ins, outs, scratch, b, s, nb, n):
        mine, first, one, got_one, two, got_two, send, recv, local, total, out_sem = scratch

        def each(work):
            def move(i, carry):
                at = pl.multiple_of(i * step, step)
                for r in range(rows):
                    work(r, at)
                return carry

            lax.fori_loop(0, half_len // step, move, 0)

        def value(half, whole_refs, half_refs, r, at):
            parts = [ref[r, pl.ds(half * half_len + at, step), :] for ref in whole_refs]
            parts += [ref[r, pl.ds(at, step), :] for ref in half_refs]
            result = parts[0].astype(F32)
            for p in parts[1:]:
                result = result + p.astype(F32)
            return result

        def add(target, half, whole_refs, half_refs):
            def work(r, at):
                target[r, pl.ds(at, step), :] = value(half, whole_refs, half_refs, r, at).astype(BF16)

            each(work)

        def finish(half, whole_refs, half_refs):
            def work(r, at):
                total[r, pl.ds(half * half_len + at, step), :] = value(
                    half, whole_refs, half_refs, r, at
                )

            each(work)

        yield from quad_stages(
            s,
            ins[0],
            mine,
            first,
            lambda ref, i: ref.at[:, i],
            one,
            got_one,
            two,
            got_two,
            (send, recv, local),
            add,
            finish,
        )
        out = pltpu.make_async_copy(total, outs[0], out_sem)
        out.start()
        out.wait()

    return Task(
        [x],
        [like(x, (rows, frames, width), F32)],
        quad_scratch((rows, frames, width), (rows, half_len, width))
        + [pltpu.VMEM((rows, frames, width), F32), DMA],
        body,
    )


def quad_scatter_task(x, rests=(0, 0, 0), first_row=0, row_count=None):
    nb, n = dims()
    x_rows = row_count or x.shape[2]
    block = (nb, x_rows, x.shape[3])
    taken = pl.ds(first_row, x_rows)

    def body(ins, outs, scratch, b, s, nb, n):
        mine, first, one, got_one, two, got_two, send, recv, local = scratch[:9]
        total, z_send, z_recv, z_local = scratch[9:]
        o = outs[0]

        rows = x_rows
        step = 16 if rows % 16 == 0 else rows

        def value(half, whole_refs, half_refs, i, at):
            parts = [ref[half * (nb // 2) + i, at, :] for ref in whole_refs]
            parts += [ref[i, at, :] for ref in half_refs]
            result = parts[0].astype(F32)
            for p in parts[1:]:
                result = result + p.astype(F32)
            return result.astype(BF16)

        def each(work):
            def move(k, carry):
                if step == rows:
                    work(k, slice(None))
                else:
                    i, j = k // (rows // step), lax.rem(k, rows // step)
                    work(i, pl.ds(pl.multiple_of(j * step, step), step))
                return carry

            lax.fori_loop(0, (nb // 2) * (rows // step), move, 0)

        def add(target, half, whole_refs, half_refs):
            def work(i, at):
                target[i, at, :] = value(half, whole_refs, half_refs, i, at)

            each(work)

        def finish(half, whole_refs, half_refs):
            def work(i, at):
                total[half * (nb // 2) + i, at, :] = value(half, whole_refs, half_refs, i, at)

            each(work)

        yield from quad_stages(
            s,
            ins[0],
            mine,
            first,
            (lambda ref, i: ref.at[:, i]) if row_count is None else (lambda ref, i: ref.at[:, i, taken]),
            one,
            got_one,
            two,
            got_two,
            (send, recv, local),
            add,
            finish,
            rests,
        )
        last = []
        for d in range(1, nb):
            plane = lax.rem(b + d, nb)
            copy = remote(
                total.at[plane], o.at[b], z_send.at[d], z_recv.at[d], batch=plane, seq=s
            )
            copy.start()
            last.append(copy)
        copy = pltpu.make_async_copy(total.at[b], o.at[b], z_local)
        copy.start()
        last.append(copy)
        yield
        for copy in last:
            copy.wait()

    return Task(
        [x],
        [like(x, block)],
        quad_scratch(block, (nb // 2,) + block[1:])
        + [pltpu.VMEM(block, BF16), DMA((nb,)), DMA((nb,)), DMA],
        body,
        True,
    )


def spread_task(x):
    nb, n = dims()
    chips = n // 2

    def body(ins, outs, scratch, b, s, nb, n):
        z_send, z_recv, p_send, p_recv, c_send, c_recv, local = scratch
        x, o = ins[0], outs[0]
        core = lax.rem(s, 2)
        sibling = s + 1 - 2 * core
        own = pltpu.make_async_copy(x, o.at[b, s], local)
        own.start()
        along = []
        for d in range(1, nb):
            copy = remote(
                x, o.at[b, s], z_send.at[d], z_recv.at[d], batch=lax.rem(b + d, nb), seq=s
            )
            copy.start()
            along.append(copy)
        far, near = [], []

        def onward(d):
            plane = lax.rem(b - d + nb, nb)
            source = x if d == 0 else o.at[plane, s]
            for c in range(1, chips):
                copy = remote(
                    source,
                    o.at[plane, s],
                    p_send.at[d, c],
                    p_recv.at[d, c],
                    seq=lax.rem(s + 2 * c, n),
                )
                copy.start()
                far.append((d, c, plane, copy))
            copy = remote(source, o.at[plane, s], c_send.at[d, 0], c_recv.at[d, 0], seq=sibling)
            copy.start()
            near.append(copy)

        onward(0)
        yield
        for d in range(1, nb):
            along[d - 1].wait_recv()
            onward(d)
        yield
        for d, c, plane, copy in far:
            copy.wait_recv()
            source = lax.rem(s - 2 * c + n, n)
            last = remote(
                o.at[plane, source],
                o.at[plane, source],
                c_send.at[d, c],
                c_recv.at[d, c],
                seq=sibling,
            )
            last.start()
            near.append(last)
        yield
        own.wait()
        for copy in along:
            copy.wait_send()
        for entry in far:
            entry[3].wait_send()
        for copy in near:
            copy.wait()

    square = DMA((nb, chips))
    return Task(
        [x],
        [like(x, (nb, n) + x.shape)],
        [DMA((nb,)), DMA((nb,)), square, square, square, square, DMA],
        body,
        True,
    )


def columns_out_task(x, late=False):
    nb, n = dims()
    ndev = nb * n
    kinds = x.shape[0]

    def body(ins, outs, scratch, b, s, nb, n):
        send, recv = scratch
        x, o = ins[0], outs[0]
        me = b * n + s
        pieces = []
        for j in range(kinds):
            piece = kinds * me + j
            column = lax.rem(piece, ndev)
            pieces.append((j, piece // ndev, column // nb, lax.rem(column, nb)))
        if late:
            yield
        sent = []
        for j, part, block, slot in pieces:
            source, target, arrived = x.at[j], o.at[part, slot], recv.at[part, slot]
            for d in range(nb):
                plane = lax.rem(b + d, nb)
                owner = holder_of(plane, block, n, nb)
                if d == 0:

                    @pl.when(owner == s)
                    def _(source=source, target=target, arrived=arrived):
                        pltpu.make_async_copy(source, target, arrived).start()

                    @pl.when(owner != s)
                    def _(source=source, target=target, arrived=arrived, j=j, owner=owner):
                        remote(
                            source, target, send.at[j, 0], arrived, batch=b, seq=owner
                        ).start()
                else:
                    copy = remote(
                        source, target, send.at[j, d], arrived, batch=plane, seq=owner
                    )
                    copy.start()
                    sent.append(copy)
        yield
        yield
        yield
        for copy in sent:
            copy.wait_send()
        for j, part, block, slot in pieces:
            owner = holder_of(b, block, n, nb)

            @pl.when(owner != s)
            def _(j=j, part=part, slot=slot, owner=owner):
                remote(
                    x.at[j], o.at[part, slot], send.at[j, 0], recv.at[part, slot], batch=b, seq=owner
                ).wait_send()

        for p in range(kinds):
            for j in range(nb):
                pltpu.make_async_copy(x.at[0], o.at[p, j], recv.at[p, j]).wait()

    return Task(
        [x],
        [like(x, (kinds, nb) + x.shape[1:])],
        [DMA((kinds, nb)), DMA((kinds, nb))],
        body,
        True,
    )


def columns_back_task(x):
    nb, n = dims()
    ndev = nb * n
    kinds = x.shape[0]

    def body(ins, outs, scratch, b, s, nb, n):
        send, recv = scratch
        x, o = ins[0], outs[0]
        me = b * n + s
        pieces = []
        for p in range(kinds):
            for j in range(nb):
                column = p * ndev + block_of(b, s, n) * nb + j
                part = lax.rem(column, kinds)
                pieces.append(
                    (x.at[p, j], o.at[b, part], column // kinds, send.at[p, j], recv.at[b, part])
                )
        for source, target, owner, sent, arrived in pieces:

            @pl.when(owner == me)
            def _(source=source, target=target, arrived=arrived):
                pltpu.make_async_copy(source, target, arrived).start()

            @pl.when(owner != me)
            def _(source=source, target=target, owner=owner, sent=sent, arrived=arrived):
                remote(
                    source, target, sent, arrived, batch=owner // n, seq=lax.rem(owner, n)
                ).start()

        yield
        yield
        yield
        for source, target, owner, sent, arrived in pieces:

            @pl.when(owner != me)
            def _(source=source, target=target, owner=owner, sent=sent, arrived=arrived):
                remote(
                    source, target, sent, arrived, batch=owner // n, seq=lax.rem(owner, n)
                ).wait_send()

        for p in range(kinds):
            for j in range(nb):
                pltpu.make_async_copy(x.at[0, 0], o.at[j, p], recv.at[j, p]).wait()

    return Task(
        [x],
        [like(x, (nb, kinds) + x.shape[2:])],
        [DMA((kinds, nb)), DMA((nb, kinds))],
        body,
        True,
    )


def scatter_task(x):
    nb, n = dims()
    chips = n // 2

    def body(ins, outs, scratch, b, s, nb, n):
        mine, first, passed, second, total, send, recv, local, z_send, z_recv, z_local = scratch
        x, o = ins[0], outs[0]
        core = lax.rem(s, 2)
        sibling = s + 1 - 2 * core
        chip = s // 2
        order = [lax.rem(chip + d, chips) for d in list(range(1, chips)) + [0]]
        pair, own, far, last = [], [], [], []
        for k, c in enumerate(order):
            copy = remote(
                x.at[:, 2 * c + 1 - core], first.at[k], send.at[k], recv.at[k], seq=sibling
            )
            copy.start()
            pair.append(copy)
            copy = pltpu.make_async_copy(x.at[:, 2 * c + core], mine.at[k], local.at[k])
            copy.start()
            own.append(copy)
        yield
        for k in range(chips - 1):
            pair[k].wait_recv()
            own[k].wait()

            def add(i, carry, k=k):
                passed[k, i] = (mine[k, i].astype(F32) + first[k, i].astype(F32)).astype(BF16)
                return carry

            lax.fori_loop(0, nb, add, 0)
            copy = remote(
                passed.at[k],
                second.at[k],
                send.at[chips + k],
                recv.at[chips + k],
                seq=2 * order[k] + core,
            )
            copy.start()
            far.append(copy)
        yield
        pair[chips - 1].wait_recv()
        own[chips - 1].wait()
        for copy in far:
            copy.wait_recv()

        def finish(i, carry):
            value = mine[chips - 1, i].astype(F32) + first[chips - 1, i].astype(F32)
            for k in range(chips - 1):
                value = value + second[k, i].astype(F32)
            total[i] = value.astype(BF16)
            return carry

        lax.fori_loop(0, nb, finish, 0)
        for d in range(1, nb):
            plane = lax.rem(b + d, nb)
            copy = remote(
                total.at[plane], o.at[b], z_send.at[d], z_recv.at[d], batch=plane, seq=s
            )
            copy.start()
            last.append(copy)
        copy = pltpu.make_async_copy(total.at[b], o.at[b], z_local)
        copy.start()
        last.append(copy)
        yield
        for copy in pair + far:
            copy.wait_send()
        for copy in last:
            copy.wait()

    block = (nb,) + x.shape[2:]
    return Task(
        [x],
        [like(x, block)],
        [
            pltpu.VMEM((chips,) + block, BF16),
            pltpu.VMEM((chips,) + block, BF16),
            pltpu.VMEM((chips - 1,) + block, BF16),
            pltpu.VMEM((chips - 1,) + block, BF16),
            pltpu.VMEM(block, BF16),
            DMA((n,)),
            DMA((n,)),
            DMA((chips,)),
            DMA((nb,)),
            DMA((nb,)),
            DMA,
        ],
        body,
        True,
    )


def times(left, right):
    return lax.dot_general(left, right, (((1,), (0,)), ((), ())), preferred_element_type=F32)


def times_t(left, right):
    return lax.dot_general(left, right, (((1,), (1,)), ((), ())), preferred_element_type=F32)


def rows_sum(left, right):
    return lax.dot_general(left, right, (((0,), (0,)), ((), ())), preferred_element_type=F32)


def mish_parts(v):
    e = jnp.exp(jnp.minimum(v, 20.0))
    n = e * (e + 2.0)
    inverse = 1.0 / (n + 2.0)
    return e, n, inverse


def mish(v):
    e, n, inverse = mish_parts(v)
    return v * (n * inverse)


def mish_slope(v):
    e, n, inverse = mish_parts(v)
    return n * inverse + v * (4.0 * e * (1.0 + e)) * inverse * inverse


CHUNK = 128


def interleave(even, odd):
    low = lax.broadcasted_iota(jnp.int32, even.shape, 1) < CHAN
    return (
        jnp.where(low, even, pltpu.roll(odd, CHAN, 1)),
        jnp.where(low, pltpu.roll(even, CHAN, 1), odd),
    )


def to_groups(even, odd):
    if even.shape[1] == CHAN:
        return (jnp.concatenate([even, odd], axis=1),)
    return interleave(even, odd)


def to_pair(blocks):
    if len(blocks) == 1:
        return blocks[0][:, :CHAN], blocks[0][:, CHAN:]
    return interleave(*blocks)


def place(buf, source, seg, length):
    rows = buf.shape[0]

    def clear(i, carry):
        buf[pl.ds(pl.multiple_of(i * 16, 16), 16), :] = jnp.zeros((16, buf.shape[1]), F32)
        return carry

    lax.fori_loop(0, rows // 16, clear, 0)

    def move(i, carry):
        at = pl.multiple_of(i * CHUNK, CHUNK)
        value = source(at)
        ids = seg[0, pl.ds(at, CHUNK), :] & 7
        for u in range(SEGS):
            to = pl.ds(at + GAP * (u + 1), CHUNK)
            buf[to, :] = buf[to, :] + jnp.where(ids == u, value, 0.0)
        return carry

    lax.fori_loop(0, length // CHUNK, move, 0)


def unplace(buf, sink, seg, length):
    def move(i, carry):
        at = pl.multiple_of(i * CHUNK, CHUNK)
        ids = seg[0, pl.ds(at, CHUNK), :] & 7
        value = buf[pl.ds(at + GAP, CHUNK), :]
        for u in range(1, SEGS):
            value = jnp.where(ids == u, buf[pl.ds(at + GAP * (u + 1), CHUNK), :], value)
        sink[0, pl.ds(at, CHUNK), :] = value.astype(sink.dtype)
        return carry

    lax.fori_loop(0, length // CHUNK, move, 0)


def folded(buf, count, first):
    return buf[pl.ds(first, count, stride=FOLD), :]


def spread_taps(x, buf, count):
    for t in range(TAPS // 2):
        blocks = to_groups(folded(buf, count, 2 * t + 1), folded(buf, count, 2 * t + 2))
        for g, block in enumerate(blocks):
            x[g, :, 2 * CHAN * t : 2 * CHAN * (t + 1)] = block.astype(BF16)


def write_folded(buf, count, groups, value, live=None):
    for w in range(FOLD // 2):
        lanes = slice(2 * CHAN * w, 2 * CHAN * (w + 1))
        for half, part in enumerate(to_pair([value(g, lanes) for g in range(groups)])):
            at = pl.ds(GAP + 2 * w + half, count, stride=FOLD)
            buf[at, :] = part if live is None else part * live[at, :]


def fill_bands(bands, taps, groups, back):
    low = lax.broadcasted_iota(jnp.int32, (CHAN, 2 * CHAN), 1) < CHAN
    zero = jnp.zeros((CHAN, 2 * CHAN), F32)
    width = groups * CHAN

    def forms(k):
        if not 0 <= k < KERNEL:
            return None
        full = taps[:, KERNEL - 1 - k if back else k].astype(F32).reshape(width, 2 * CHAN)
        if back:
            full = full.T
            if groups == 1:
                full = jnp.concatenate([full, full], axis=1)
        turned = pltpu.roll(full, CHAN, 1)
        result = {}
        for c in range(2):
            for g in range(groups):
                if back:
                    rows, own = slice(c * CHAN, (c + 1) * CHAN), g
                else:
                    rows, own = slice(g * CHAN, (g + 1) * CHAN), c
                pair = (full[rows], turned[rows])
                result[c, g] = pair if own == 0 else pair[::-1]
        return result

    known = {}
    for tap in range(TAPS):
        known[tap] = forms(tap)
        known.pop(tap - FOLD, None)
        for w in range(FOLD // 2):
            left, right = known.get(tap - 2 * w), known.get(tap - 2 * w - 1)
            for c in range(2):
                for g in range(groups):
                    a = zero if left is None else left[c, g][0]
                    b = zero if right is None else right[c, g][1]
                    bands[
                        c, g, tap * CHAN : (tap + 1) * CHAN, 2 * CHAN * w : 2 * CHAN * (w + 1)
                    ] = jnp.where(low, a, b).astype(BF16)


FOLDED = FOLD * CHAN
DEPTH = TAPS * CHAN


def conv_forward_kernel(count, length, groups, u, seg, taps, c1, c2, out, buf, live, x, bands):
    @pl.when(pl.program_id(0) == 0)
    def _():
        fill_bands(bands, taps, groups, False)

    width = groups * CHAN
    place(live, lambda at: jnp.ones((CHUNK, width), F32), seg, length)
    place(buf, lambda at: u[0, pl.ds(at, CHUNK), :].astype(F32), seg, length)
    spread_taps(x, buf, count)
    for g in range(groups):
        c1[0, g] = times(x[g], bands[0, g])
    write_folded(buf, count, groups, lambda g, lanes: mish(c1[0, g, :, lanes]), live)
    spread_taps(x, buf, count)
    for g in range(groups):
        c2[0, g] = times(x[g], bands[1, g])
    write_folded(buf, count, groups, lambda g, lanes: mish(c2[0, g, :, lanes]))
    unplace(buf, out, seg, length)


def conv_sizes(length):
    count = -(-(length + GAP * (SEGS - 1)) // FOLD)
    count = -(-count // 16) * 16
    return count, FOLD * count + 48


def whole(shape):
    zeros = (0,) * len(shape)
    return pl.BlockSpec(shape, lambda *i: zeros)


def by_row(shape):
    return pl.BlockSpec((1,) + tuple(shape[1:]), lambda r: (r,) + (0,) * (len(shape) - 1))


def conv_forward(u, seg, taps):
    rows, length, width = u.shape
    groups = width // CHAN
    count, buffer = conv_sizes(length)
    kept = (rows, groups, count, FOLDED)
    return pl.pallas_call(
        functools.partial(conv_forward_kernel, count, length, groups),
        grid=(rows,),
        in_specs=[by_row(u.shape), by_row(seg.shape), whole(taps.shape)],
        out_specs=[by_row(kept), by_row(kept), by_row(u.shape)],
        out_shape=[
            jax.ShapeDtypeStruct(kept, F32),
            jax.ShapeDtypeStruct(kept, F32),
            jax.ShapeDtypeStruct(u.shape, BF16),
        ],
        scratch_shapes=[
            pltpu.VMEM((buffer, width), F32),
            pltpu.VMEM((buffer, width), F32),
            pltpu.VMEM((groups, count, DEPTH), BF16),
            pltpu.VMEM((2, groups, DEPTH, FOLDED), BF16),
        ],
        compiler_params=params(),
    )(u, seg, taps)


def weight_sums(even, odd, c, turned, x, groups):
    rows = slice(c * CHAN, (c + 1) * CHAN)
    blocks = TAPS // 2
    pair = 2 * CHAN
    for g in range(groups):
        for start in range(0, blocks, 2):
            stop = min(start + 2, blocks)
            product = times(turned[g], x[g, :, start * pair : stop * pair])
            for t in range(start, stop):
                part = product[:, (t - start) * pair : (t - start + 1) * pair]
                for m in range(FOLD):
                    to = t - m // 2
                    if 0 <= to < 16:
                        sums = odd if m % 2 else even
                        sums[g, to, rows] = sums[g, to, rows] + part[m * CHAN : (m + 1) * CHAN]


def conv_chain(
    d, seg, c1, c2, dh, buf, grads, live, x, turned2, turned1, bands, count, length, groups
):
    width = groups * CHAN
    place(live, lambda at: jnp.ones((CHUNK, width), F32), seg, length)
    place(grads, lambda at: d[0, pl.ds(at, CHUNK), :].astype(F32), seg, length)

    def slope(kept, turned, scaled):
        values = {}
        for w in range(FOLD // 2):
            lanes = slice(2 * CHAN * w, 2 * CHAN * (w + 1))
            for g in range(groups):
                value = scaled(g, w, lanes) * mish_slope(kept[0, g, :, lanes])
                values[g, w] = value
                turned[g, lanes, :] = value.T.astype(BF16)
        write_folded(grads, count, groups, lambda g, lanes: values[g, lanes.start // (2 * CHAN)])

    def both(source, g, w):
        return to_groups(
            folded(source, count, GAP + 2 * w), folded(source, count, GAP + 2 * w + 1)
        )[g]

    slope(c2, turned2, lambda g, w, lanes: both(grads, g, w))
    yield
    spread_taps(x, grads, count)
    back = [times(x[g], bands[1, g]) for g in range(groups)]
    slope(c1, turned1, lambda g, w, lanes: back[g][:, lanes] * both(live, g, w))
    yield
    spread_taps(x, grads, count)
    last = [times(x[g], bands[0, g]) for g in range(groups)]
    write_folded(buf, count, groups, lambda g, lanes: last[g][:, lanes])
    unplace(buf, dh, seg, length)


def conv_weights(
    u, seg, c1, buf, live, x, turned2, turned1, even, odd, count, length, groups
):
    width = groups * CHAN
    place(live, lambda at: jnp.ones((CHUNK, width), F32), seg, length)
    for i in range(0, GAP, 8):
        buf[i : i + 8, :] = jnp.zeros((8, width), F32)
    for i in range(GAP + FOLD * count, buf.shape[0], 8):
        buf[i : i + 8, :] = jnp.zeros((8, width), F32)
    write_folded(buf, count, groups, lambda g, lanes: mish(c1[0, g, :, lanes]), live)
    spread_taps(x, buf, count)
    weight_sums(even, odd, 1, turned2, x, groups)
    yield
    place(buf, lambda at: u[0, pl.ds(at, CHUNK), :].astype(F32), seg, length)
    spread_taps(x, buf, count)
    weight_sums(even, odd, 0, turned1, x, groups)


def conv_pieces(pieces, even, odd, groups, nb):
    low = lax.broadcasted_iota(jnp.int32, (2 * CHAN, 2 * CHAN), 1) < CHAN
    part = groups * CHAN // nb
    each = CHAN // part
    for g in range(groups):
        for p in range(16):
            left = pltpu.roll(odd[g, p], CHAN, 1)
            right = pltpu.roll(odd[g, p + 1], CHAN, 1) if p < 15 else left
            total = (even[g, p] + jnp.where(low, left, right)).T.astype(BF16)
            for half in range(2):
                k = 2 * p + half
                if k < KERNEL:
                    for j in range(each):
                        first = half * CHAN + j * part
                        pieces[0, g * each + j, k] = total[first : first + part]


def conv_backward_kernel(
    count, length, groups, nb, d, u, seg, c1, c2, taps, dh, pieces, buf, grads, live, x, turned2, turned1, bands, even, odd
):
    row = pl.program_id(0)

    @pl.when(row == 0)
    def _():
        fill_bands(bands, taps, groups, True)
        even[...] = jnp.zeros_like(even)
        odd[...] = jnp.zeros_like(odd)

    for _ in conv_chain(
        d, seg, c1, c2, dh, buf, grads, live, x, turned2, turned1, bands, count, length, groups
    ):
        pass
    for _ in conv_weights(
        u, seg, c1, buf, live, x, turned2, turned1, even, odd, count, length, groups
    ):
        pass

    @pl.when(row == pl.num_programs(0) - 1)
    def _():
        conv_pieces(pieces, even, odd, groups, nb)


def conv_backward(d, u, seg, c1, c2, taps, nb):
    rows, length, width = u.shape
    groups = width // CHAN
    count, buffer = conv_sizes(length)
    pieces = (1, nb, KERNEL, width // nb, 2 * CHAN)
    sums = pltpu.VMEM((groups, 16, 2 * CHAN, 2 * CHAN), F32)
    frames = pltpu.VMEM((buffer, width), F32)
    return pl.pallas_call(
        functools.partial(conv_backward_kernel, count, length, groups, nb),
        grid=(rows,),
        in_specs=[
            by_row(d.shape),
            by_row(u.shape),
            by_row(seg.shape),
            by_row(c1.shape),
            by_row(c2.shape),
            whole(taps.shape),
        ],
        out_specs=[by_row(u.shape), whole(pieces)],
        out_shape=[
            jax.ShapeDtypeStruct(u.shape, BF16),
            jax.ShapeDtypeStruct(pieces, BF16),
        ],
        scratch_shapes=[
            frames,
            frames,
            frames,
            pltpu.VMEM((groups, count, DEPTH), BF16),
            pltpu.VMEM((groups, FOLDED, count), BF16),
            pltpu.VMEM((groups, FOLDED, count), BF16),
            pltpu.VMEM((2, groups, DEPTH, FOLDED), BF16),
            sums,
            sums,
        ],
        compiler_params=params(),
    )(d, u, seg, c1, c2, taps)


def pair_swap(x):
    width = x.shape[1]
    if width % 128:
        x = jnp.concatenate([x, x], axis=1)
    lane = lax.broadcasted_iota(jnp.int32, x.shape, 1)
    after = pltpu.roll(x, x.shape[1] - 1, 1)
    before = pltpu.roll(x, 1, 1)
    return jnp.where(lax.rem(lane, 2) == 0, -after, before)[:, :width]


def qkv_kernel(width, x, w, cos_t, sin_t, offset, seg, q, k, v, cos, sin):
    got = times(x[0], w[...])
    ids = seg[0] & 7
    size = cos_t.shape[0]
    cos_o, sin_o = pick(ids, offset[0, 0], size), pick(ids, offset[0, 1], size)
    cos[0] = cos_t[...] * cos_o + sin_t[...] * sin_o
    sin[0] = sin_t[...] * cos_o - cos_t[...] * sin_o
    for p, out in enumerate((q, k)):
        part = got[:, p * width : (p + 1) * width]
        out[0] = (part * cos[0] + pair_swap(part) * sin[0]).astype(BF16)
    v[0] = got[:, 2 * width :].astype(BF16)


def qkv_forward(x, w, starts, seg):
    rows, length, depth = x.shape
    width = w.shape[1] // 3
    pairs = (np.arange(width) % HEAD) // 2
    freq = 10000.0 ** (-2.0 * pairs / HEAD)
    angle = np.arange(length)[:, None] * freq[None, :]
    cos_t = jnp.asarray(np.cos(angle).astype(np.float32))
    sin_t = jnp.asarray(np.sin(angle).astype(np.float32))
    turned = starts.astype(F32)[:, :, None] * jnp.asarray(freq.astype(np.float32))
    offset = jnp.stack([jnp.cos(turned), jnp.sin(turned)], axis=1)
    block = 512
    spec = pl.BlockSpec((1, block, width), lambda r, i: (r, i, 0))
    table = pl.BlockSpec((block, width), lambda r, i: (i, 0))
    shape = jax.ShapeDtypeStruct((rows, length, width), BF16)
    angles = jax.ShapeDtypeStruct((rows, length, width), F32)
    return pl.pallas_call(
        functools.partial(qkv_kernel, width),
        grid=(rows, length // block),
        in_specs=[
            pl.BlockSpec((1, block, depth), lambda r, i: (r, i, 0)),
            whole(w.shape),
            table,
            table,
            pl.BlockSpec((1, 2, SEGS, width), lambda r, i: (r, 0, 0, 0)),
            pl.BlockSpec((1, block, 1), lambda r, i: (r, i, 0)),
        ],
        out_specs=[spec] * 5,
        out_shape=[shape] * 3 + [angles] * 2,
        compiler_params=params(),
    )(x, w, cos_t, sin_t, offset, seg)


def qkv_back_kernel(p, w, x, partial, grad, total):
    i = pl.program_id(0) * pl.num_programs(1) + pl.program_id(1)

    @pl.when(i == 0)
    def _():
        total[...] = jnp.zeros_like(total)

    partial[0] = times(p[0], w[...]).astype(BF16)
    total[...] = total[...] + rows_sum(p[0], x[0])

    @pl.when(i == pl.num_programs(0) * pl.num_programs(1) - 1)
    def _():
        grad[...] = total[...].astype(BF16)


def qkv_backward(p, w, x):
    rows, length, depth = x.shape
    block = 512

    def spec(size):
        return pl.BlockSpec((1, block, size), lambda r, i: (r, i, 0))

    return pl.pallas_call(
        qkv_back_kernel,
        grid=(rows, length // block),
        in_specs=[spec(p.shape[2]), whole(w.shape), spec(depth)],
        out_specs=[spec(depth), whole(w.shape)],
        out_shape=[
            jax.ShapeDtypeStruct((rows, length, depth), BF16),
            jax.ShapeDtypeStruct(w.shape, BF16),
        ],
        scratch_shapes=[pltpu.VMEM(w.shape, F32)],
        compiler_params=params(),
    )(p, w, x)


def attention_forward_kernel(width, q, k, v, q_code, k_code, out, low, log_sum):
    heads = width // HEAD
    lane = lax.broadcasted_iota(jnp.int32, q.shape[1:], 1) // HEAD
    allowed = (q_code[0] & 7) == k_code[0]
    queries = q[0] * 0.125
    result, logs = None, None
    for h in range(heads):
        chosen = jnp.where(lane == h, queries, jnp.zeros_like(queries))
        scores = lax.dot_general(
            chosen, k[0], (((1,), (1,)), ((), ())), preferred_element_type=F32
        )
        scores = jnp.where(allowed, scores, MASKED)
        peak = jnp.max(scores, axis=1, keepdims=True)
        weights = jnp.exp(scores - peak)
        total = jnp.sum(weights, axis=1, keepdims=True)
        value = jnp.dot(weights.astype(BF16), v[0], preferred_element_type=F32) / total
        log = jnp.broadcast_to(peak + jnp.log(total), value.shape)
        result = value if h == 0 else jnp.where(lane == h, value, result)
        logs = log if h == 0 else jnp.where(lane == h, log, logs)
    out[0] = result
    low[0] = result.astype(BF16)
    log_sum[0] = logs


def attention_forward(q, k, v, q_code, k_code):
    rows, length, width = q.shape
    block = 256
    spec = pl.BlockSpec((1, block, width), lambda r, i: (r, i, 0))
    row = pl.BlockSpec((1, length, width), lambda r, i: (r, 0, 0))
    return pl.pallas_call(
        functools.partial(attention_forward_kernel, width),
        grid=(rows, length // block),
        in_specs=[
            spec,
            row,
            row,
            pl.BlockSpec((1, block, 1), lambda r, i: (r, i, 0)),
            pl.BlockSpec((1, 1, length), lambda r, i: (r, 0, 0)),
        ],
        out_specs=[spec] * 3,
        out_shape=[
            jax.ShapeDtypeStruct(q.shape, F32),
            jax.ShapeDtypeStruct(q.shape, BF16),
            jax.ShapeDtypeStruct(q.shape, F32),
        ],
        compiler_params=params(),
    )(q, k, v, q_code, k_code)


BLOCK = 512


def attention_backward_kernel(
    length, width, ids, q, k, v, g, log_sum, delta, k_code, q_code, cos, sin, out, dq, dk, dv
):
    heads = width // HEAD
    row = pl.program_id(0)
    lane = lax.broadcasted_iota(jnp.int32, (BLOCK, width), 1) // HEAD
    dk[...] = jnp.zeros_like(dk)
    dv[...] = jnp.zeros_like(dv)

    def outer(i, carry):
        at = pl.ds(pl.multiple_of(i * BLOCK, BLOCK), BLOCK)
        queries = q[0, at, :] * 0.125
        grads = g[0, at, :]
        zero = jnp.zeros_like(queries)
        queries_of = [jnp.where(lane == h, queries, zero) for h in range(heads)]
        grads_of = [jnp.where(lane == h, grads, zero) for h in range(heads)]
        dq[...] = jnp.zeros_like(dq)
        first_id, last_id = ids[row, i * BLOCK], ids[row, i * BLOCK + BLOCK - 1]

        def inner(j, carry):
            @pl.when((ids[row, j * BLOCK + BLOCK - 1] >= first_id) & (ids[row, j * BLOCK] <= last_id))
            def _():
                pair(j)

            return carry

        def pair(j):
            to = pl.ds(pl.multiple_of(j * BLOCK, BLOCK), BLOCK)
            keys, values = k[0, to, :], v[0, to, :]
            allowed = k_code[0, to, :] == q_code[0, :, at]
            dk_part, dv_part, dq_part = None, None, None
            for h in range(heads):
                keys_of = jnp.where(lane == h, keys, zero)
                scores = lax.dot_general(
                    keys, queries_of[h], (((1,), (1,)), ((), ())), preferred_element_type=F32
                )
                probs = jnp.where(allowed, jnp.exp(scores - log_sum[0, h : h + 1, at]), 0.0)
                grad_probs = lax.dot_general(
                    values, grads_of[h], (((1,), (1,)), ((), ())), preferred_element_type=F32
                )
                grad_scores = (probs * (grad_probs - delta[0, h : h + 1, at])).astype(BF16)
                a = jnp.dot(probs.astype(BF16), grads_of[h], preferred_element_type=F32)
                c = jnp.dot(grad_scores, queries_of[h], preferred_element_type=F32)
                e = lax.dot_general(
                    grad_scores, keys_of, (((0,), (0,)), ((), ())), preferred_element_type=F32
                )
                dv_part = a if h == 0 else dv_part + a
                dk_part = c if h == 0 else dk_part + c
                dq_part = e if h == 0 else dq_part + e
            dv[to, :] = dv[to, :] + dv_part
            dk[to, :] = dk[to, :] + dk_part
            dq[...] = dq[...] + dq_part

        lax.fori_loop(0, length // BLOCK, inner, 0)
        grad = dq[...] * 0.125
        turned = grad * cos[0, at, :] - pair_swap(grad) * sin[0, at, :]
        out[0, at, 0:width] = turned.astype(BF16)
        return carry

    lax.fori_loop(0, length // BLOCK, outer, 0)

    def finish(i, carry):
        at = pl.ds(pl.multiple_of(i * BLOCK, BLOCK), BLOCK)
        grad = dk[at, :]
        turned = grad * cos[0, at, :] - pair_swap(grad) * sin[0, at, :]
        out[0, at, width : 2 * width] = turned.astype(BF16)
        out[0, at, 2 * width : 3 * width] = dv[at, :].astype(BF16)
        return carry

    lax.fori_loop(0, length // BLOCK, finish, 0)


def attention_backward(ids, q, k, v, g, log_sum, delta, k_code, q_code, cos, sin):
    rows, length, width = q.shape

    def spec(shape):
        return pl.BlockSpec((1,) + tuple(shape[1:]), lambda r, *_: (r,) + (0,) * (len(shape) - 1))

    arrays = (q, k, v, g, log_sum, delta, k_code, q_code, cos, sin)
    out = (rows, length, 3 * width)
    return pl.pallas_call(
        functools.partial(attention_backward_kernel, length, width),
        grid_spec=pltpu.PrefetchScalarGridSpec(
            num_scalar_prefetch=1,
            grid=(rows,),
            in_specs=[spec(a.shape) for a in arrays],
            out_specs=spec(out),
            scratch_shapes=[
                pltpu.VMEM((BLOCK, width), F32),
                pltpu.VMEM((length, width), F32),
                pltpu.VMEM((length, width), F32),
            ],
        ),
        out_shape=jax.ShapeDtypeStruct(out, BF16),
        compiler_params=params(),
    )(ids, *arrays)


def pick(ids, table, rows):
    value = table[SEGS - 1 : SEGS, :]
    for u in range(SEGS - 2, -1, -1):
        value = jnp.where(ids == u, table[u : u + 1, :], value)
    return jnp.broadcast_to(value, (rows, table.shape[1]))


def gelu_parts(v):
    c = 0.7978845608
    t = jnp.tanh(c * (v + 0.044715 * v * v * v))
    half = 0.5 * (1.0 + t)
    return v * half, half + 0.5 * v * (1.0 - t * t) * c * (1.0 + 0.134145 * v * v)


STEP = 32


def feed_kernel(
    rows,
    frames,
    part,
    att,
    embedded,
    late,
    ids,
    mod,
    cotangent,
    block_out,
    grad_att,
    grad_middle,
    sums,
    normed,
    low,
    grad_up,
    grad_feed,
    grad_branch,
    branch,
    middle,
    scale,
    bend,
    feed,
    grad_normed,
):
    tokens = rows * frames
    wide = 256
    per = wide // part

    def each_step(body):
        for r in range(rows):

            def step(i, carry, r=r):
                at = pl.ds(pl.multiple_of(r * frames + i * STEP, STEP), STEP)
                body(r, at)
                return carry

            lax.fori_loop(0, frames // STEP, step, 0)

    def gate(r, at, which):
        return pick(ids[at, :], mod[r, which], STEP)

    def columns(first, count, j):
        n = wide // count
        return late[j * n : (j + 1) * n, first : first + count, :].reshape(wide, D)

    for j in range(D // wide):
        branch[:, j * wide : (j + 1) * wide] = times_t(att[...], columns(0, part, j))

    def to_normed(r, at):
        value = embedded[at, :] + gate(r, at, 2) * branch[at, :]
        middle[at, :] = value
        centre = value - jnp.mean(value, axis=1, keepdims=True)
        factor = lax.rsqrt(jnp.mean(centre * centre, axis=1, keepdims=True) + EPSILON)
        hat = centre * factor
        scale[at, :] = jnp.broadcast_to(factor, (STEP, 128))
        normed[at, :] = (hat * (1.0 + gate(r, at, 4)) + gate(r, at, 3)).astype(BF16)

    each_step(to_normed)
    for j in range(2 * D // wide):
        lanes = slice(j * wide, (j + 1) * wide)
        value, slope = gelu_parts(times_t(normed[...], columns(part, 2 * part, j)))
        low[:, lanes] = value.astype(BF16)
        bend[:, lanes] = slope
    for j in range(D // wide):
        feed[:, j * wide : (j + 1) * wide] = times_t(
            low[:, :D], columns(3 * part, part, j)
        ) + times_t(low[:, D:], columns(4 * part, part, j))

    def to_out(r, at):
        gate_feed = gate(r, at, 5)
        block_out[at, :] = (middle[at, :] + gate_feed * feed[at, :]).astype(BF16)
        grad_feed[at, :] = (gate_feed * cotangent[at, :].astype(F32)).astype(BF16)

    each_step(to_out)

    def inner(first, count, lanes):
        return late[:, first : first + count, lanes].reshape(-1, wide)

    for half in range(2):
        for j in range(D // wide):
            lanes = slice(half * D + j * wide, half * D + (j + 1) * wide)
            weights = inner((3 + half) * part, part, slice(j * wide, (j + 1) * wide))
            grad_up[:, lanes] = (times(grad_feed[...], weights) * bend[:, lanes]).astype(BF16)
    for j in range(D // wide):
        lanes = slice(j * wide, (j + 1) * wide)
        grad_normed[:, lanes] = times(grad_up[...], inner(part, 2 * part, lanes))

    sums[...] = jnp.zeros_like(sums)

    def back(r, at):
        value = middle[at, :]
        factor = scale[at, 0:1]
        hat = (value - jnp.mean(value, axis=1, keepdims=True)) * factor
        grad = grad_normed[at, :]
        e = grad * (1.0 + gate(r, at, 4))
        out = cotangent[at, :].astype(F32)
        total = out + factor * (
            e
            - jnp.mean(e, axis=1, keepdims=True)
            - hat * jnp.mean(e * hat, axis=1, keepdims=True)
        )
        grad_middle[at, :] = total
        grad_branch[at, :] = (gate(r, at, 2) * total).astype(BF16)
        first = ids[at, :] == ids[r * frames : r * frames + 1, :]
        for k, part_sum in enumerate(
            (total * branch[at, :], grad, grad * hat, out * feed[at, :])
        ):
            kept = jnp.where(first, part_sum, 0.0)
            other = part_sum - kept
            for side, piece in enumerate((kept, other)):
                folded = piece[0:8]
                for q in range(1, STEP // 8):
                    folded = folded + piece[8 * q : 8 * q + 8]
                sums[r, side, k] = sums[r, side, k] + folded

    each_step(back)
    for j in range(D // wide):
        lanes = slice(j * wide, (j + 1) * wide)
        grad_att[:, lanes] = times(grad_branch[...], inner(0, part, lanes)).astype(BF16)


def feed_both(att, embedded, late, ids, mod, cotangent, rows, frames, part):
    tokens = rows * frames
    vmem = pl.BlockSpec(memory_space=pltpu.VMEM)

    def scratch(width):
        return pltpu.VMEM((tokens, width), F32)

    def out(width, dtype=BF16):
        return jax.ShapeDtypeStruct((tokens, width), dtype)

    return pl.pallas_call(
        functools.partial(feed_kernel, rows, frames, part),
        in_specs=[vmem] * 6,
        out_specs=[vmem] * 9,
        out_shape=[
            out(D),
            out(D),
            out(D, F32),
            jax.ShapeDtypeStruct((rows, 2, 4, 8, D), F32),
            out(D),
            out(2 * D),
            out(2 * D),
            out(D),
            out(D),
        ],
        scratch_shapes=[
            scratch(D),
            scratch(D),
            scratch(128),
            scratch(2 * D),
            scratch(D),
            scratch(D),
        ],
        compiler_params=params(),
    )(att, embedded, late, ids, mod, cotangent)


def lane_block(b, s, n, width):
    return pl.ds(pl.multiple_of(block_of(b, s, n) * width, 128), width)


def seat_rows(s, frames, first, count):
    return pl.ds(pl.multiple_of(s * frames + first, 16), count)


def norm_gather_task(bump_c, hidden, ids, mod, rows, frames):
    n = dims()[1]
    width = D // n
    half = frames // 2

    def body(ins, outs, scratch, b, s, nb, n):
        bump_in, hidden, ids, mod = ins
        embedded, o = outs
        bump, normed, send, recv, local, g_send, g_recv, g_local = scratch
        core, chip = lax.rem(s, 2), s // 2
        sibling = s + 1 - 2 * core
        flip_x = chip + 1 - 2 * lax.rem(chip, 2)
        flip_y = lax.rem(chip + 2, 4)
        seat_x, seat_y = 2 * flip_x + core, 2 * flip_y + core
        diagonal = 2 * lax.rem(flip_x + 2, 4) + core
        lanes = lane_block(b, s, n, width)
        swaps = {}
        for r in range(rows):
            for d in range(1, n):
                t = lax.rem(s + d, n)
                copy = remote(
                    bump_in.at[r, seat_rows(t, frames, 0, frames), :],
                    bump.at[r, :, lanes],
                    send.at[r, d],
                    recv.at[r, d],
                    seq=t,
                )
                copy.start()
                swaps[r, d] = copy
            copy = pltpu.make_async_copy(
                bump_in.at[r, seat_rows(s, frames, 0, frames), :], bump.at[r, :, lanes], local.at[r]
            )
            copy.start()
            swaps[r, 0] = copy
        yield
        parts = (pl.ds(0, half), pl.ds(half, half))
        pushes, near, far = {}, [], []

        def push(r, i, piece, source, target, fresh=False):
            where = o.at[r, source, parts[piece]]
            copy = remote(
                normed.at[r, parts[piece]] if fresh else where,
                where,
                g_send.at[r, i],
                g_recv.at[r, i],
                seq=target,
            )
            copy.start()
            return copy

        for r in range(rows):
            swaps[r, 0].wait()
            for d in range(1, n):
                swaps[r, d].wait_recv()

            def step(i, carry, r=r):
                inside = pl.ds(pl.multiple_of(i * STEP, STEP), STEP)
                at = pl.ds(pl.multiple_of(r * frames + i * STEP, STEP), STEP)
                value = hidden[at, :] + bump[r, inside, :].astype(F32)
                embedded[at, :] = value
                centre = value - jnp.mean(value, axis=1, keepdims=True)
                hat = centre * lax.rsqrt(
                    jnp.mean(centre * centre, axis=1, keepdims=True) + EPSILON
                )
                scale = pick(ids[at, :], mod[r, 1], STEP)
                shift = pick(ids[at, :], mod[r, 0], STEP)
                normed[r, inside, :] = (hat * (1.0 + scale) + shift).astype(BF16)
                return carry

            lax.fori_loop(0, frames // STEP, step, 0)
            pushes[r, "x0"] = push(r, 0, 0, s, seat_x, True)
            pushes[r, "y1"] = push(r, 1, 1, s, seat_y, True)
            pushes[r, "x1"] = push(r, 2, 1, s, seat_x, True)
            pushes[r, "y0"] = push(r, 3, 0, s, seat_y, True)
            near += [push(r, 4, 0, s, sibling, True), push(r, 5, 1, s, sibling, True)]
            copy = pltpu.make_async_copy(normed.at[r], o.at[r, s], g_local.at[r])
            copy.start()
            pushes[r, "own"] = copy
            yield
        for r in range(rows):
            pushes[r, "x0"].wait_recv()
            far.append(push(r, 6, 0, seat_x, seat_y))
            near.append(push(r, 7, 0, seat_x, sibling))
            pushes[r, "y1"].wait_recv()
            far.append(push(r, 8, 1, seat_y, seat_x))
            near.append(push(r, 9, 1, seat_y, sibling))
            pushes[r, "x1"].wait_recv()
            near.append(push(r, 10, 1, seat_x, sibling))
            pushes[r, "y0"].wait_recv()
            near.append(push(r, 11, 0, seat_y, sibling))
        for r in range(rows):
            far[2 * r].wait_recv()
            near.append(push(r, 12, 0, diagonal, sibling))
            far[2 * r + 1].wait_recv()
            near.append(push(r, 13, 1, diagonal, sibling))
        yield
        for r in range(rows):
            pushes[r, "own"].wait()
            for d in range(1, n):
                swaps[r, d].wait_send()
            for name in ("x0", "x1", "y0", "y1"):
                pushes[r, name].wait_send()
        for copy in far:
            copy.wait_send()
        for copy in near:
            copy.wait()

    vmem = pl.BlockSpec(memory_space=pltpu.VMEM)
    tokens = rows * frames
    return Task(
        [bump_c, hidden, ids, mod],
        [
            jax.ShapeDtypeStruct((tokens, D), F32),
            jax.ShapeDtypeStruct((rows, n, frames, D), BF16),
        ],
        [
            pltpu.VMEM((rows, frames, D), BF16),
            pltpu.VMEM((rows, frames, D), BF16),
            DMA((rows, n)),
            DMA((rows, n)),
            DMA((rows,)),
            DMA((rows, 14)),
            DMA((rows, 14)),
            DMA((rows,)),
        ],
        body,
        in_specs=[ANY, vmem, vmem, vmem],
        out_specs=[vmem, ANY],
    )


def fold_rows(piece):
    total = piece[0:8]
    for q in range(1, piece.shape[0] // 8):
        total = total + piece[8 * q : 8 * q + 8]
    return total


def sum_norm_task(partial, embedded, grad_middle, ids, mod, rows, frames):
    n = dims()[1]
    width = D // n
    half_len = frames // 2
    step = 16

    def body(ins, outs, scratch, b, s, nb, n):
        x, embedded, middle, ids, mod = ins
        grad, o, sums = outs
        mine, first, one, got_one, two, got_two, send, recv, local, low, c_send, c_recv, c_local = scratch
        copies = []
        sums[...] = jnp.zeros_like(sums)

        def value(half, whole_refs, half_refs, r, at):
            parts = [ref[r, pl.ds(half * half_len + at, step), :] for ref in whole_refs]
            parts += [ref[r, pl.ds(at, step), :] for ref in half_refs]
            result = parts[0].astype(F32)
            for p in parts[1:]:
                result = result + p.astype(F32)
            return result

        def each(work):
            def move(i, carry):
                at = pl.multiple_of(i * step, step)
                for r in range(rows):
                    work(r, at)
                return carry

            lax.fori_loop(0, half_len // step, move, 0)

        def add(target, half, whole_refs, half_refs):
            def work(r, at):
                target[r, pl.ds(at, step), :] = value(half, whole_refs, half_refs, r, at).astype(BF16)

            each(work)

        def finish(half, whole_refs, half_refs):
            def work(r, at):
                down = value(half, whole_refs, half_refs, r, at)
                where = pl.ds(pl.multiple_of(r * frames + half * half_len + at, step), step)
                field = embedded[where, :]
                centre = field - jnp.mean(field, axis=1, keepdims=True)
                factor = lax.rsqrt(jnp.mean(centre * centre, axis=1, keepdims=True) + EPSILON)
                hat = centre * factor
                e = down * (1.0 + pick(ids[where, :], mod[r, 1], step))
                result = middle[where, :] + factor * (
                    e
                    - jnp.mean(e, axis=1, keepdims=True)
                    - hat * jnp.mean(e * hat, axis=1, keepdims=True)
                )
                grad[where, :] = result
                low[r, pl.ds(half * half_len + at, step), :] = result.astype(BF16)
                begin = ids[where, :] == ids[r * frames : r * frames + 1, :]
                for k, part_sum in enumerate((down, down * hat)):
                    kept = jnp.where(begin, part_sum, 0.0)
                    sums[r, 0, k] = sums[r, 0, k] + fold_rows(kept)
                    sums[r, 1, k] = sums[r, 1, k] + fold_rows(part_sum - kept)

            each(work)
            rows_at = pl.ds(half * half_len, half_len)
            target = o.at[:, seat_rows(s, frames, half * half_len, half_len), :]
            for d in range(1, n):
                t = lax.rem(s + d, n)
                copy = remote(
                    low.at[:, rows_at, lane_block(b, t, n, width)],
                    target,
                    c_send.at[half, d],
                    c_recv.at[half, d],
                    seq=t,
                )
                copy.start()
                copies.append(copy)
            copy = pltpu.make_async_copy(
                low.at[:, rows_at, lane_block(b, s, n, width)], target, c_local.at[half]
            )
            copy.start()
            copies.append(copy)

        yield from quad_stages(
            s,
            x,
            mine,
            first,
            lambda ref, i: ref.at[:, i],
            one,
            got_one,
            two,
            got_two,
            (send, recv, local),
            add,
            finish,
        )
        for copy in copies:
            copy.wait()

    vmem = pl.BlockSpec(memory_space=pltpu.VMEM)
    tokens = rows * frames
    return Task(
        [partial, embedded, grad_middle, ids, mod],
        [
            jax.ShapeDtypeStruct((tokens, D), F32),
            jax.ShapeDtypeStruct((rows, n * frames, width), BF16),
            jax.ShapeDtypeStruct((rows, 2, 2, 8, D), F32),
        ],
        quad_scratch((rows, frames, D), (rows, half_len, D))
        + [pltpu.VMEM((rows, frames, D), BF16), DMA((2, n)), DMA((2, n)), DMA((2,))],
        body,
        in_specs=[ANY] + [vmem] * 4,
        out_specs=[vmem, ANY, vmem],
    )


def late_grads_task(att, grad_branch, grad_feed, low, grad_up, normed, ndev, part):
    def body(ins, outs, scratch, b, s, nb, n):
        yield
        late_work(*ins, *outs, part)

    vmem = pl.BlockSpec(memory_space=pltpu.VMEM)
    return Task(
        [att, grad_branch, grad_feed, low, grad_up, normed],
        [
            jax.ShapeDtypeStruct((ndev, 3 * part, D), BF16),
            jax.ShapeDtypeStruct((ndev, 2 * part, D), BF16),
        ],
        [],
        body,
        in_specs=[vmem] * 6,
        out_specs=[vmem] * 2,
    )


def late_work(att, grad_branch, grad_feed, low, grad_up, normed, out, down, part):
    wide = 256
    per = wide // part
    for j in range(D // wide):
        lanes = slice(j * wide, (j + 1) * wide)
        out[j * per : (j + 1) * per, 0:part, :] = (
            rows_sum(grad_branch[:, lanes], att[...]).astype(BF16).reshape(per, part, D)
        )
        for half in range(2):
            down[j * per : (j + 1) * per, half * part : (half + 1) * part, :] = (
                rows_sum(grad_feed[:, lanes], low[:, half * D : (half + 1) * D])
                .astype(BF16)
                .reshape(per, part, D)
            )
    for j in range(2 * D // wide):
        lanes = slice(j * wide, (j + 1) * wide)
        out[j * per // 2 : (j + 1) * per // 2, part : 3 * part, :] = (
            rows_sum(grad_up[:, lanes], normed[...]).astype(BF16).reshape(per // 2, 2 * part, D)
        )


def conv_back_task(d, u, seg, c1, c2, taps, frames):
    nb, n = dims()
    rows, length, width = u.shape
    groups = width // CHAN
    count, buffer = conv_sizes(length)
    pieces_shape = (1, nb, KERNEL, width // nb, 2 * CHAN)

    def body(ins, outs, scratch, b, s, nb, n):
        d, u, seg, c1, c2, taps = ins
        o, pieces = outs
        buf, grads, live, x, turned2, turned1, bands, even, odd, dh, send, recv, local = scratch
        yield
        fill_bands(bands, taps, groups, True)
        even[...] = jnp.zeros_like(even)
        odd[...] = jnp.zeros_like(odd)
        copies = []
        for r in range(rows):
            row = pl.ds(r, 1)
            yield from conv_chain(
                d.at[row], seg.at[row], c1.at[row], c2.at[row], dh.at[row], buf, grads, live, x,
                turned2.at[r], turned1.at[r], bands, count, length, groups,
            )
            target = o.at[r, :, lane_block(b, s, n, width)]
            for k in range(1, n):
                t = lax.rem(s + k, n)
                copy = remote(
                    dh.at[r, seat_rows(t, frames, 0, frames), :],
                    target,
                    send.at[r, k],
                    recv.at[r, k],
                    seq=t,
                )
                copy.start()
                copies.append(copy)
            copy = pltpu.make_async_copy(
                dh.at[r, seat_rows(s, frames, 0, frames), :], target, local.at[r]
            )
            copy.start()
            copies.append(copy)
            yield
        for r in range(rows):
            row = pl.ds(r, 1)
            yield from conv_weights(
                u.at[row], seg.at[row], c1.at[row], buf, live, x, turned2.at[r], turned1.at[r],
                even, odd, count, length, groups,
            )
            yield
        conv_pieces(pieces, even, odd, groups, nb)
        yield
        for copy in copies:
            copy.wait()

    vmem = pl.BlockSpec(memory_space=pltpu.VMEM)
    frames_buf = pltpu.VMEM((buffer, width), F32)
    turned = pltpu.VMEM((rows, groups, FOLDED, count), BF16)
    sums = pltpu.VMEM((groups, 16, 2 * CHAN, 2 * CHAN), F32)
    return Task(
        [d, u, seg, c1, c2, taps],
        [
            jax.ShapeDtypeStruct((rows, frames, n * width), BF16),
            jax.ShapeDtypeStruct(pieces_shape, BF16),
        ],
        [
            frames_buf,
            frames_buf,
            frames_buf,
            pltpu.VMEM((groups, count, DEPTH), BF16),
            turned,
            turned,
            pltpu.VMEM((2, groups, DEPTH, FOLDED), BF16),
            sums,
            sums,
            pltpu.VMEM(u.shape, BF16),
            DMA((rows, n)),
            DMA((rows, n)),
            DMA((rows,)),
        ],
        body,
        in_specs=[vmem] * 6,
        out_specs=[ANY, vmem],
    )


def tail_kernel(grad_embedded, grad_conv, joined, in_t, ids, grad_in, mels, grad_text, hidden):
    tokens = joined.shape[0]
    for i in range(tokens // 64):
        at = slice(64 * i, 64 * (i + 1))
        hidden[at, :] = (grad_embedded[at, :] + grad_conv[at, :].astype(F32)).astype(BF16)
    back = times(hidden[...], in_t[...])
    mels[...] = back[:, : 2 * MEL]
    embed = back[:, 2 * MEL :].astype(BF16)
    for start in range(0, D, 256):
        at = slice(start, start + 256)
        grad_in[at, :] = rows_sum(hidden[:, at], joined[...]).astype(BF16)
    turned = embed.astype(F32).T.astype(BF16)
    for start in range(0, VOCAB, 512):
        stop = min(start + 512, VOCAB)
        word = lax.broadcasted_iota(jnp.int32, (tokens, stop - start), 1) + start
        hot = (word == ids[...]).astype(F32).astype(BF16)
        grad_text[:, start:stop] = times(turned, hot).astype(BF16)


def tail_back(grad_embedded, grad_conv, joined, in_t, ids):
    tokens, inner = joined.shape
    vmem = pl.BlockSpec(memory_space=pltpu.VMEM)
    return pl.pallas_call(
        tail_kernel,
        in_specs=[vmem] * 5,
        out_specs=[vmem] * 3,
        out_shape=[
            jax.ShapeDtypeStruct((D, inner), BF16),
            jax.ShapeDtypeStruct((tokens, 2 * MEL), F32),
            jax.ShapeDtypeStruct((inner - 2 * MEL, VOCAB), BF16),
        ],
        scratch_shapes=[pltpu.VMEM((tokens, D), BF16)],
        compiler_params=params(),
    )(grad_embedded, grad_conv, joined, in_t, ids)


def layer_norm(field):
    centre = field - jnp.mean(field, axis=-1, keepdims=True)
    return centre * lax.rsqrt(jnp.mean(centre * centre, axis=-1, keepdims=True) + EPSILON)


def modulate(field, scaling, shifting):
    return layer_norm(field) * (1.0 + scaling) + shifting


def gelu_curve(inputs):
    return jax.nn.gelu(inputs, approximate=True)


def by_segment(ids, table):
    value = table[:, SEGS - 1][:, None, :]
    for u in range(SEGS - 2, -1, -1):
        value = jnp.where(ids[:, :, None] == u, table[:, u][:, None, :], value)
    return value


def on_device(
    mel_inputs,
    text_ids,
    segment_ids,
    key_mask,
    time_index,
    input_proj,
    conv_first,
    conv_second,
    time_table,
    adaln_proj,
    qkv_proj,
    out_proj,
    up_proj,
    down_proj,
    text_table,
    grad_out,
):
    nb, n = dims()
    ndev = nb * n
    rows, frames = mel_inputs.shape[:2]
    tokens = rows * frames
    length = frames * n
    width = D // n
    part = D // ndev
    mine = lax.axis_index("seq")
    first_frame = mine * frames

    out_t, up_t, down_t = out_proj.T, up_proj.T, down_proj.T
    wide_t = jnp.concatenate([out_t, up_t, down_t[:, :D], down_t[:, D:]], axis=0)
    per = wide_t.shape[0]
    (
        (full_in,),
        (full_text,),
        (full_time,),
        (all_index,),
        (got_convs,),
    ) = transfer(
        [
            spread_task(input_proj.T),
            spread_task(text_table.T),
            spread_task(time_table.T),
            spread_task(time_index),
            columns_out_task(jnp.concatenate([conv_first, conv_second], axis=2)[None], True),
        ],
        0,
    )
    got_convs = got_convs[0]
    wide_t, _ = lax.optimization_barrier((wide_t, all_index))
    late = lax.all_gather(wide_t, ("batch", "seq"), axis=0, tiled=True).reshape(ndev, per, D)
    in_t = full_in.reshape(D, input_proj.shape[0])
    text_t = full_text.reshape(-1, VOCAB)
    time_t = full_time.reshape(D, STEPS)
    slot_steps = all_index[:, 0].reshape(nb * rows * SEGS)

    own_ids = lax.dynamic_slice_in_dim(segment_ids, first_frame, frames, 1)
    key_code = segment_ids + jnp.where(key_mask > 0, 0, 8)
    seg_column = key_code[:, :, None]
    seg_index = jnp.arange(SEGS, dtype=jnp.int32)
    starts = jnp.sum((segment_ids[:, None, :] < seg_index[None, :, None]).astype(jnp.int32), axis=2)

    text_hot = (
        text_ids.reshape(-1)[:, None] == jnp.arange(VOCAB, dtype=jnp.int32)[None, :]
    ).astype(BF16)
    text_embed = times_t(text_hot, text_t).astype(BF16)
    joined = jnp.concatenate([mel_inputs.reshape(tokens, 2 * MEL), text_embed], axis=1)
    hidden = times_t(joined, in_t).reshape(rows, frames, D)

    step_hot = (
        slot_steps[:, None] == jnp.arange(STEPS, dtype=jnp.int32)[None, :]
    ).astype(BF16)
    cond_value = times_t(step_hot, time_t)
    soft_cond = jax.nn.silu(cond_value).astype(BF16)
    own_mod = times(soft_cond, adaln_proj)
    task, arrange = to_channels(hidden.astype(BF16))
    got, (mod_got,) = transfer(
        [task, spray_task(own_mod.reshape(nb, rows * SEGS, 6 * part), True)], 2
    )
    hidden_c = arrange(got)
    modulation = mod_got.transpose(1, 0, 2).reshape(rows, SEGS, 6, D)
    mod_table = modulation.transpose(0, 2, 1, 3)
    ids_column = own_ids.reshape(tokens, 1)
    fused = n == 8 and width % 128 == 0
    shift_attn, scale_attn = (by_segment(own_ids, modulation[:, :, i]) for i in range(2))

    conv_one, conv_two, bump_c = conv_forward(hidden_c, seg_column, got_convs)
    qkv_task = columns_out_task(qkv_proj.T.reshape(3, part, D))
    if fused:
        (embedded, normed_all), (got_qkv,) = transfer(
            [
                norm_gather_task(
                    bump_c, hidden.reshape(tokens, D), ids_column, mod_table, rows, frames
                ),
                qkv_task,
            ],
            3,
        )
        embedded = embedded.reshape(rows, frames, D)
    else:
        task, arrange = to_frames(bump_c)
        bump = arrange(transfer([task], 3)[0])
        embedded = hidden + bump.astype(F32)
        normed = modulate(embedded, scale_attn, shift_attn).astype(BF16)
        (normed_all,), (got_qkv,) = transfer([gather_task(normed), qkv_task], 4)
    normed_all = normed_all.reshape(rows, length, D)
    qkv_t = got_qkv.reshape(3 * width, D)
    query, key, value, cos, sin = qkv_forward(normed_all, qkv_t.T, starts, seg_column)
    attended, attended_low, log_lanes = attention_forward(
        query, key, value, seg_column, key_code[:, None, :]
    )
    task, arrange = to_frames(attended_low)
    attended_own = arrange(transfer([task], 5)[0])
    attended_own = attended_own.reshape(tokens, D)

    (
        block_out,
        grad_att,
        grad_middle,
        feed_sums,
        normed_feed,
        gelu_low,
        grad_up,
        grad_feed,
        grad_branch,
    ) = feed_both(
        attended_own,
        embedded.reshape(tokens, D),
        late,
        ids_column,
        mod_table,
        grad_out.reshape(tokens, D),
        rows,
        frames,
        part,
    )
    late_task = late_grads_task(
        attended_own, grad_branch, grad_feed, gelu_low, grad_up, normed_feed, ndev, part
    )
    block_out = block_out.reshape(rows, frames, D)
    grad_att = grad_att.reshape(rows, frames, D)
    grad_middle = grad_middle.reshape(rows, frames, D)
    task, arrange = to_channels(grad_att)
    grad_att_c = arrange(transfer([task], 6)[0])
    heads = width // HEAD
    delta = jnp.sum(
        (grad_att_c.astype(F32) * attended).reshape(rows, length, heads, HEAD), axis=3
    ).transpose(0, 2, 1)
    log_rows = log_lanes.reshape(rows, length, heads, HEAD)[:, :, :, 0].transpose(0, 2, 1)
    grad_projected = attention_backward(
        segment_ids,
        query,
        key,
        value,
        grad_att_c,
        log_rows,
        delta,
        seg_column,
        segment_ids[:, None, :],
        cos,
        sin,
    )
    partial, grad_qkv = qkv_backward(grad_projected, qkv_t, normed_all)
    partial = partial.reshape(rows, n, frames, D)
    qkv_back = columns_back_task(grad_qkv.reshape(3, nb, part, D))
    if fused:
        (grad_embedded, grad_emb_c, attn_sums), (got_qkv_grads,), late_grads = transfer(
            [
                sum_norm_task(
                    partial,
                    embedded.reshape(tokens, D),
                    grad_middle.reshape(tokens, D),
                    ids_column,
                    mod_table,
                    rows,
                    frames,
                ),
                qkv_back,
                late_task,
            ],
            7,
        )
        grad_embedded = grad_embedded.reshape(rows, frames, D)
        attn_sums = jnp.sum(attn_sums, axis=3)
        attn_sums = [attn_sums[:, :, 0], attn_sums[:, :, 1]]
    else:
        (grad_normed,), (got_qkv_grads,), late_grads = transfer(
            [sum_task(partial), qkv_back, late_task], 7
        )
        grad_emb_part, grad_scale_attn, grad_shift_attn = jax.vjp(
            modulate, embedded, scale_attn, shift_attn
        )[1](grad_normed)
        grad_embedded = grad_middle + grad_emb_part
        task, arrange = to_channels(grad_embedded.astype(BF16))
        grad_emb_c = arrange(transfer([task], 10)[0])
    first_ids, last_ids = own_ids[:, 0], own_ids[:, -1]
    if not fused:
        first = (own_ids == first_ids[:, None])[:, :, None]
        attn_sums = [
            jnp.stack(
                [jnp.sum(jnp.where(first, g, 0.0), axis=1), jnp.sum(jnp.where(first, 0.0, g), axis=1)],
                axis=1,
            )
            for g in (grad_shift_attn, grad_scale_attn)
        ]
    feed_sums = jnp.sum(feed_sums, axis=3)
    sides = jnp.concatenate(
        [attn_sums[0], attn_sums[1]] + [feed_sums[:, :, i] for i in range(4)], axis=2
    )
    is_first = (first_ids[:, None] == seg_index).astype(F32)
    is_last = (last_ids[:, None] == seg_index).astype(F32)
    local_sums = is_first[:, :, None] * sides[:, :1] + is_last[:, :, None] * sides[:, 1:]
    slots = rows * SEGS
    sums_out = local_sums.reshape(slots, ndev, 6 * part).transpose(1, 0, 2)
    if fused:
        late_tasks = []
        for x, sides in zip(late_grads, (3, 2)):
            x = x.reshape(nb, n, -1, D)
            size = x.shape[2] // sides
            for side in range(sides):
                rests = (len(late_tasks), 2, 2)
                late_tasks.append(quad_scatter_task(x, rests, side * size, size))
        *late_got, (sums_got,), (grad_hidden_conv, conv_sums) = transfer(
            late_tasks
            + [
                spray_task(sums_out, False),
                conv_back_task(
                    grad_emb_c, hidden_c, seg_column, conv_one, conv_two, got_convs, frames
                ),
            ],
            11,
        )
        late_sum = jnp.concatenate([jnp.sum(x[0].astype(F32), axis=0) for x in late_got], axis=0)
    else:
        late_sum = lax.psum_scatter(
            jnp.concatenate(late_grads, axis=1), ("batch", "seq"), scatter_dimension=0, tiled=False
        ).astype(F32)
        grad_hidden_c, conv_sums = conv_backward(
            grad_emb_c, hidden_c, seg_column, conv_one, conv_two, got_convs, nb
        )
        task, arrange = to_frames(grad_hidden_c)
        got, (sums_got,) = transfer([task, spray_task(sums_out, False)], 11)
        grad_hidden_conv = arrange(got)
    sums_got = sums_got.reshape(nb, n, slots, 6 * part)
    grad_mod = jnp.sum(sums_got, axis=1).astype(BF16).reshape(nb * slots, 6 * part)
    grad_adaln = rows_sum(soft_cond, grad_mod)
    soft_part = times_t(grad_mod, adaln_proj)
    soft_out = soft_part.reshape(nb * slots, ndev, part).transpose(1, 0, 2)
    grad_qkv_own = jnp.sum(got_qkv_grads.astype(F32), axis=0).reshape(3 * part, D).T

    grad_input, grad_mels, grad_text = tail_back(
        grad_embedded.reshape(tokens, D),
        grad_hidden_conv.reshape(tokens, D),
        joined,
        in_t,
        text_ids.reshape(tokens, 1),
    )
    grad_mels = grad_mels.reshape(rows, frames, 2 * MEL)
    scatter = quad_scatter_task if n == 8 and nb % 2 == 0 else scatter_task
    (in_sum,), (text_sum,), (soft_got,), (got_conv_grads,) = transfer(
        [
            scatter(grad_input.reshape(nb, n, part, -1)),
            scatter(grad_text.reshape(nb, n, -1, VOCAB)),
            spray_task(soft_out, False),
            columns_back_task(conv_sums),
        ],
        13,
    )
    grad_convs = jnp.sum(got_conv_grads.astype(F32), axis=0)[0]
    grad_first, grad_second = grad_convs[..., :CHAN], grad_convs[..., CHAN:]
    grad_soft = jnp.sum(soft_got, axis=0)
    own_cond = times(step_hot, time_table)
    grad_cond = jax.vjp(jax.nn.silu, own_cond)[1](grad_soft)[0]
    grad_time = jnp.dot(step_hot.astype(F32).T, grad_cond, precision=EXACT)
    grad_input_own = jnp.sum(in_sum.astype(F32), axis=0).T
    grad_text_own = jnp.sum(text_sum.astype(F32), axis=0).T
    grad_down_own = jnp.concatenate([late_sum[3 * part : 4 * part], late_sum[4 * part :]], axis=1)

    return (
        block_out,
        grad_mels,
        grad_input_own,
        grad_first,
        grad_second,
        grad_time,
        grad_adaln,
        grad_qkv_own,
        late_sum[:part].T,
        late_sum[part : 3 * part].T,
        grad_down_own.T,
        grad_text_own,
    )


def solution(mesh):
    frames = P("batch", "seq", None)
    columns = P(None, ("batch", "seq"))
    taps = P(None, ("batch", "seq"), None)
    in_specs = (
        frames,
        P("batch", "seq"),
        P("batch", None),
        P("batch", None),
        P("batch", None),
        columns,
        taps,
        taps,
        columns,
        columns,
        columns,
        columns,
        columns,
        columns,
        columns,
        frames,
    )
    out_specs = (
        frames,
        frames,
        columns,
        taps,
        taps,
        columns,
        columns,
        columns,
        columns,
        columns,
        columns,
        columns,
    )
    return jax.shard_map(
        on_device, mesh=mesh, in_specs=in_specs, out_specs=out_specs, check_vma=False
    )
```
